32 devices in a mesh: dp: 2 (over core), ctx: 4 (over y, x), exp: 4 (over z).
Axes of the slice: x: 2, y: 2, z: 4, core: 2. Of those that a mesh axis runs over, the one named last changes fastest.
Arguments:
- prompt_x: bfloat16 [8, 512, 2048], P(('dp', 'exp'), 'ctx'), may hold values from -6 to 6
- cont_x: bfloat16 [8, 32, 2048], P(('dp', 'exp'), 'ctx'), may hold values from -6 to 6
- cont_ids: int32 [8, 4, 8], P(('dp', 'exp'), 'ctx'), may hold values from 0 to 2, never falling along the last dimension, each value on 1 to 4 neighbouring positions
- routes: int32 [8, 4, 136, 8], P(('dp', 'exp'), 'ctx'), may hold values from 0 to 15, all different within a row; in each aligned block of 136 rows (0 to 135, 136 to 271, ..., all dimensions but the last counted through in order) at most 72 rows name the same one
- qkv_weight: bfloat16 [2048, 6144], P(('dp', 'ctx', 'exp')), may hold values from -0.125 to 0.125
- out_weight: bfloat16 [2048, 2048], P(('dp', 'ctx', 'exp')), may hold values from -1 to 1
- router_weight: bfloat16 [2048, 16], P(('dp', 'ctx', 'exp')), may hold values from -0.0625 to 0.0625
- norm_gains: bfloat16 [2048, 4], P(('dp', 'ctx', 'exp')), may hold values from 0.25 to 1.75
- gate_up_weight: bfloat16 [16, 2048, 2048], P(('ctx', 'exp')), may hold values from -0.125 to 0.125
- down_weight: bfloat16 [16, 1024, 2048], P(('ctx', 'exp')), may hold values from -1.5 to 1.5
- prompt_cot: bfloat16 [8, 512, 2048], P(('dp', 'exp'), 'ctx'), may hold values from -6 to 6
- cont_cot: bfloat16 [8, 32, 2048], P(('dp', 'exp'), 'ctx'), may hold values from -6 to 6
Outputs:
- out_prompt: bfloat16 [8, 512, 2048], P(('dp', 'exp'), 'ctx')
- out_cont: bfloat16 [8, 32, 2048], P(('dp', 'exp'), 'ctx')
- grad_prompt: float32 [8, 512, 2048], P(('dp', 'exp'), 'ctx')
- grad_cont: float32 [8, 32, 2048], P(('dp', 'exp'), 'ctx')
- grad_qkv: float32 [2048, 6144], P(('dp', 'ctx', 'exp'))
- grad_out: float32 [2048, 2048], P(('dp', 'ctx', 'exp'))
- grad_router: float32 [2048, 16], P(('dp', 'ctx', 'exp'))
- grad_gains: float32 [2048, 4], P(('dp', 'ctx', 'exp'))
- grad_gate_up: float32 [16, 2048, 2048], P(('ctx', 'exp'), 'dp')
- grad_down: float32 [16, 1024, 2048], P(('ctx', 'exp'), 'dp')
The draws below stay inside these ranges and needn't reach their ends.
Inputs may be any that keep to these rules, and one draw needn't show every extreme that they name: `routes`: each row names 8 different experts; the rows of one device name one expert at most 72 times, a bound that some block reaches. `cont_ids`: along each device's 8 positions the numbers never fall; each of the 3 continuations has 1 to 4 positions and one has exactly 4.
All inputs are finite; a program needn't handle non-finite values.
Results may differ from the reference program's by a relative error of at most 0.018.
Values may be sent and summed in bfloat16 or wider, within the bound.
No kernel may reach another device: no remote copies, remote signals or barrier semaphores. Data moves between devices by JAX's collectives and lax.ppermute only.
A program may use at most 256 MiB of HBM per device.

```python
import math
import jax
import jax.numpy as jnp
import numpy as np
from jax import lax

D = 2048
HEADS = 16
HEAD_DIM = 128
FF = 1024
TOP = 8
PR_DEV = 128
CL = 8
SEGS = 3
ROWS = 136
PROMPT = 512
CONT = 32
GROUPS = 8
EXPERTS = 16
CAP = 72
N_CTX = 4


def levels(own_key, extent, cuts, smallest, top_value):
    factor_of = 1.0
    for axis_at, blocks in cuts:
        draws = jax.random.uniform(jax.random.fold_in(jax.random.fold_in(own_key, 6), axis_at), (blocks,), jnp.float32, smallest / len(cuts), top_value / len(cuts))
        factor_of = factor_of * jnp.repeat(jnp.exp(draws), extent[axis_at] // blocks).reshape((-1,) + (1,) * (len(extent) - 1 - axis_at))
    return factor_of


def profile(count, total, most, lean):
    loads = [(1 << 20) // math.isqrt(standing ** lean) + 1 for standing in range(2, count + 1)]
    spare, holding = total - most - (count - 1), [1] * (count - 1)
    while spare > 0:
        candidates = [i for i in range(count - 1) if holding[i] < most]
        pool, left = sum([loads[i] for i in candidates]), spare
        for i in candidates:
            more = min(most - holding[i], max(1, left * loads[i] // pool), spare)
            holding[i] = holding[i] + more
            spare = spare - more
    return np.array([most] + holding)


def uneven_parts(stream_key, number_of, total, most, skew):
    if number_of == 2:
        one = jax.random.randint(stream_key, (), max(1, total - most), min(most, total - 1) + 1)
        return jnp.stack([one, total - one])
    lengths = jnp.asarray(profile(number_of, total, most, skew), jnp.int32)
    couples = (number_of - 1) // 2
    source_of, receiver = lengths[1:1 + 2 * couples:2], lengths[2:2 + 2 * couples:2]
    room = jnp.minimum(source_of - 1, most - receiver)
    shifted = jax.random.randint(jax.random.fold_in(stream_key, 1), (couples,), 0, 1 << 20) % (room + 1)
    lengths = lengths.at[1:1 + 2 * couples:2].set(source_of - shifted).at[2:2 + 2 * couples:2].set(receiver + shifted)
    return lengths[jax.random.permutation(jax.random.fold_in(stream_key, 2), number_of)]


def shared_out(stream_key, own, number, rows, amount, top, bound, slope):
    order = jax.random.permutation(stream_key, amount)
    heavy_load, usual = load_shares(amount, rows * top, bound, slope, True), load_shares(amount, rows * top, bound, slope, False)
    places = jnp.arange(amount)

    def named(sizes, rotation):
        used = int((sizes > 0).sum())
        fixed = max(1, used // 4)
        shifted = fixed + (places - fixed + rotation * (used - fixed)) % max(1, amount - fixed)
        return jnp.zeros((amount,), jnp.int32).at[order[jnp.where(places < fixed, places, shifted)]].set(jnp.asarray(sizes, jnp.int32))

    sizes = jnp.where(number % 4 == 0, named(heavy_load, number // 4), named(usual, number - number // 4 - 1))
    mixed = jax.random.permutation(jax.random.fold_in(own, 3), amount)
    giver, sink = mixed[0:amount // 2 * 2:2], mixed[1:amount // 2 * 2:2]
    slack = jnp.minimum(sizes[giver] - 1, bound - sizes[sink]) // 2
    slack = jnp.where((giver == order[0]) | (sink == order[0]) | (sizes[sink] == 0), 0, jnp.maximum(slack, 0))
    shifted = jax.random.randint(jax.random.fold_in(own, 4), (amount // 2,), 0, 1 << 20) % (slack + 1)
    sizes = sizes.at[giver].add(-shifted).at[sink].add(shifted)
    labels = jnp.searchsorted(jnp.cumsum(sizes), jnp.arange(rows * top), side="right").astype(jnp.int32)
    grid = labels.reshape(top, rows).T
    grid = grid[jax.random.permutation(jax.random.fold_in(own, 1), rows)]
    rotation = jax.random.randint(jax.random.fold_in(own, 2), (rows, 1), 0, top)
    return jnp.take_along_axis(grid, (jnp.arange(top)[None, :] + rotation) % top, axis=1)


def load_shares(count, total, bound, lean, full):
    portions = [(1 << 20) // math.isqrt(rank ** lean) + 1 for rank in range(1, count + 1)]
    largest = bound if full else min(bound, max(-(-total // count), total * portions[0] // sum(portions)))
    least = 1 if total - largest >= count - 1 else 0
    holding, rest = [largest] + [least] * (count - 1), total - largest - least * (count - 1)
    while rest > 0:
        free = [i for i in range(1, count) if holding[i] < largest] or [i for i in range(1, count) if holding[i] < bound]
        mass, left = sum([portions[i] for i in free]), rest
        for i in free:
            extra = min(bound - holding[i], max(1, left * portions[i] // mass), rest)
            holding[i] = holding[i] + extra
            rest = rest - extra
    return np.array(holding)


def gaussian(own_key, extent, width, reach, split=(), kind=jnp.bfloat16):
    entries = width * jax.random.normal(own_key, extent, jnp.float32)
    if split:
        entries = entries * levels(own_key, extent, split, -0.22, 0.18)
    return jnp.clip(entries, -reach, reach).astype(kind)


def setup_inputs(seed: int = 0) -> dict:
    splits = jax.random.split(jax.random.key(seed), 13)
    prompt_x = gaussian(splits[0], (GROUPS, PROMPT, D), 1.0, 6.0, ((0, 8), (1, 4)))
    cont_x = gaussian(splits[1], (GROUPS, CONT, D), 1.0, 6.0, ((0, 8), (1, 4)))
    cont_ids = jax.vmap(lambda own: jnp.searchsorted(jnp.cumsum(uneven_parts(own, SEGS, CL, CL // 2, 1)), jnp.arange(CL), side="right"))(jax.random.split(splits[2], GROUPS * N_CTX)).reshape((GROUPS, N_CTX, CL)).astype(jnp.int32)
    routes_keys = jax.random.split(jax.random.fold_in(splits[3], 1), GROUPS * N_CTX * ROWS // ROWS)
    routes_turns = jax.random.permutation(jax.random.fold_in(splits[3], 3), GROUPS * N_CTX * ROWS // ROWS)
    routes = jax.vmap(lambda own, number: shared_out(jax.random.fold_in(splits[3], 2), own, number, ROWS, EXPERTS, TOP, CAP, 1))(routes_keys, routes_turns).reshape((GROUPS, N_CTX, ROWS, TOP))
    qkv_weight = gaussian(splits[4], (D, 3 * D), D ** -0.5, 0.125, ((0, 32),))
    out_weight = gaussian(splits[5], (D, D), (D // 64) ** -0.5, 1.0, ((0, 32),))
    router_weight = gaussian(splits[6], (D, EXPERTS), (4 * D) ** -0.5, 0.0625, ((0, 32),))
    norm_gains = jnp.clip(1.0 + 0.15 * jax.random.normal(splits[7], (D, 4), jnp.float32), 0.25, 1.75).astype(jnp.bfloat16)
    gate_up_weight = gaussian(splits[8], (EXPERTS, D, 2 * FF), D ** -0.5, 0.125, ((0, 16),))
    down_weight = gaussian(splits[9], (EXPERTS, FF, D), (FF // 64) ** -0.5, 1.5, ((0, 16),))
    prompt_cot = gaussian(splits[10], (GROUPS, PROMPT, D), 1.0, 6.0, ((0, 8), (1, 4)))
    cont_cot = gaussian(splits[11], (GROUPS, CONT, D), 1.0, 6.0, ((0, 8), (1, 4)))
    return {"prompt_x": prompt_x, "cont_x": cont_x, "cont_ids": cont_ids, "routes": routes, "qkv_weight": qkv_weight, "out_weight": out_weight, "router_weight": router_weight, "norm_gains": norm_gains, "gate_up_weight": gate_up_weight, "down_weight": down_weight, "prompt_cot": prompt_cot, "cont_cot": cont_cot}


NORM_EPS = 1e-05
ROPE_BASE = 10000.0
NEGATIVE = -1e+30
HIGHEST_PREC = lax.Precision.HIGHEST

@jax.custom_vjp
def low(v):
    return lax.optimization_barrier(v.astype(jnp.bfloat16)).astype(jnp.float32)

@jax.custom_vjp
def low_back(v):
    return v

def low_keep(v):
    return (low(v), None)

def low_pass(kept, grad):
    return (grad,)

def back_keep(v):
    return (v, None)

def back_low(kept, grad):
    return (low(grad),)
low.defvjp(low_keep, low_pass)
low_back.defvjp(back_keep, back_low)

def norm_rows(values, gain_col):
    return values * lax.rsqrt(lax.optimization_barrier(jnp.mean(values * values, axis=-1, keepdims=True)) + NORM_EPS) * gain_col

def rope_tables(position, half_dim):
    inverse = ROPE_BASE ** (-jnp.arange(half_dim, dtype=jnp.float32) / half_dim)
    angles = position[:, None] * inverse[None, :]
    return (jnp.cos(angles), jnp.sin(angles))

def rotate(values, cosine, sine_rows):
    row_count = values.shape[0]
    shaped = values.reshape(row_count, HEADS, HEAD_DIM)
    half_dim = HEAD_DIM // 2
    first_half = shaped[..., :half_dim]
    second_half = shaped[..., half_dim:]
    cos_heads = cosine[:, None, :]
    sin_heads = sine_rows[:, None, :]
    turned = jnp.concatenate([first_half * cos_heads - second_half * sin_heads, second_half * cos_heads + first_half * sin_heads], axis=-1)
    return turned.reshape(row_count, -1)

def attend(group_rows, w_qkv, w_out, gain_cols):
    prompt_rows, cont_rows, seg_ids = group_rows
    prompt_len = prompt_rows.shape[0]
    model_width = w_out.shape[0]
    block_len = seg_ids.shape[1]
    all_rows = jnp.concatenate([prompt_rows, cont_rows], axis=0)
    row_count = all_rows.shape[0]
    hidden_in = low(norm_rows(all_rows, gain_cols[:, 0]))
    projected = low_back(jnp.dot(hidden_in, w_qkv, precision=HIGHEST_PREC))
    query_n = norm_rows(projected[:, :model_width], gain_cols[:, 1])
    key_n = norm_rows(projected[:, model_width:2 * model_width], gain_cols[:, 2])
    value_rows = low(projected[:, 2 * model_width:])
    starts = lax.optimization_barrier(jnp.sum((seg_ids[:, None, :] < seg_ids[:, :, None]).astype(jnp.int32), axis=-1))
    within = (jnp.arange(block_len, dtype=jnp.int32)[None, :] - starts).reshape(-1)
    position = jnp.concatenate([jnp.arange(prompt_len, dtype=jnp.int32), prompt_len + within]).astype(jnp.float32)
    cosine, sine_rows = rope_tables(position, HEAD_DIM // 2)
    queries = low(rotate(query_n, cosine, sine_rows))
    key_rows = low(rotate(key_n, cosine, sine_rows))
    row_index = jnp.arange(row_count, dtype=jnp.int32)
    is_prompt = row_index < prompt_len
    dev_block = (row_index - prompt_len) // block_len
    segment = jnp.concatenate([jnp.full((prompt_len,), -1, jnp.int32), seg_ids.reshape(-1)])
    causal = row_index[None, :] <= row_index[:, None]
    same_doc = (dev_block[:, None] == dev_block[None, :]) & (segment[:, None] == segment[None, :]) & causal
    allowed = jnp.where(is_prompt[:, None], is_prompt[None, :] & causal, is_prompt[None, :] | same_doc)
    heads_q = queries.reshape(row_count, HEADS, HEAD_DIM)
    heads_k = key_rows.reshape(row_count, HEADS, HEAD_DIM)
    heads_v = value_rows.reshape(row_count, HEADS, HEAD_DIM)
    scores = low_back(jnp.einsum('qhd,khd->hqk', heads_q, heads_k, precision=HIGHEST_PREC) * HEAD_DIM ** (-0.5))
    scores = jnp.where(allowed[None], scores, NEGATIVE)
    log_total = jax.nn.logsumexp(scores, axis=-1, keepdims=True)
    attention = low(jnp.exp(scores - log_total))
    mixed_rows = jnp.einsum('hqk,khd->qhd', attention, heads_v, precision=HIGHEST_PREC).reshape(row_count, model_width)
    mixed_rows = low(low_back(mixed_rows))
    return all_rows + low_back(jnp.dot(mixed_rows, w_out, precision=HIGHEST_PREC))

def reference(prompt_x, cont_x, cont_ids, routes, qkv_weight, out_weight, router_weight, norm_gains, gate_up_weight, down_weight, prompt_cot, cont_cot):
    groups = prompt_x.shape[0]
    prompt_total = prompt_x.shape[1]
    cont_total = cont_x.shape[1]
    experts = router_weight.shape[1]
    route_prompt = routes[:, :, :PR_DEV, :].reshape(groups, prompt_total, TOP)
    route_cont = routes[:, :, PR_DEV:, :].reshape(groups, cont_total, TOP)
    route_all = jnp.concatenate([route_prompt, route_cont], axis=1).reshape(-1, TOP)
    routed = lax.optimization_barrier(jnp.sum((route_all[:, :, None] == jnp.arange(experts, dtype=jnp.int32)[None, None, :]).astype(jnp.float32), axis=1))

    def block_forward(w_qkv, w_out, w_router, gain_cols, w_gate_up, w_down, prompt_f, cont_f):

        def attend_group(group_rows):
            return attend(group_rows, w_qkv, w_out, gain_cols)
        mid_rows = lax.map(jax.checkpoint(attend_group), (prompt_f, cont_f, cont_ids))
        mid_flat = mid_rows.reshape(-1, mid_rows.shape[-1])
        hidden_ffn = low(norm_rows(mid_flat, gain_cols[:, 3]))
        logits = jnp.dot(hidden_ffn, w_router, precision=HIGHEST_PREC)
        router = jax.nn.softmax(logits, axis=-1)
        coefficients = router * routed

        def expert_step(running, pieces):
            weight_gu, weight_dn, coefficient = pieces
            routed_in = low_back(hidden_ffn)
            gate_up = low_back(jnp.dot(routed_in, weight_gu, precision=HIGHEST_PREC))
            activated = low(jax.nn.silu(gate_up[:, :FF]) * gate_up[:, FF:])
            produced = low(low_back(jnp.dot(activated, weight_dn, precision=HIGHEST_PREC)))
            return (running + coefficient[:, None] * produced, None)
        mixture, unused = lax.scan(jax.checkpoint(expert_step), jnp.zeros_like(mid_flat), (w_gate_up, w_down, coefficients.T))
        final_rows = (mid_flat + mixture).reshape(mid_rows.shape)
        return (final_rows[:, :prompt_total], final_rows[:, prompt_total:])
    outputs, pullback = jax.vjp(block_forward, qkv_weight.astype(jnp.float32), out_weight.astype(jnp.float32), router_weight.astype(jnp.float32), norm_gains.astype(jnp.float32), gate_up_weight.astype(jnp.float32), down_weight.astype(jnp.float32), prompt_x.astype(jnp.float32), cont_x.astype(jnp.float32))
    grads = pullback((prompt_cot.astype(jnp.float32), cont_cot.astype(jnp.float32)))
    return (outputs[0].astype(jnp.bfloat16), outputs[1].astype(jnp.bfloat16), grads[6], grads[7], grads[0], grads[1], grads[2], grads[3], grads[4], grads[5])
```

```python
import jax
import jax.numpy as jnp
from jax import lax
from jax.sharding import PartitionSpec as P

D = 2048
HEADS = 16
HEAD_DIM = 128
FF = 1024
TOP = 8

NORM_EPS = 1e-05
ROPE_BASE = 10000.0
NEGATIVE = -1e30
HIGHEST_PREC = lax.Precision.HIGHEST
F32 = jnp.float32
BF16 = jnp.bfloat16


def row_scale(values):
    return lax.rsqrt(jnp.mean(values * values, axis=-1, keepdims=True) + NORM_EPS)


def rope_tables(position, half_dim):
    inverse = ROPE_BASE ** (-jnp.arange(half_dim, dtype=F32) / half_dim)
    angles = position[:, None] * inverse[None, :]
    cosine, sine_rows = jnp.cos(angles), jnp.sin(angles)
    return (
        jnp.concatenate([cosine, cosine], axis=1),
        jnp.concatenate([-sine_rows, sine_rows], axis=1),
    )


def rotate(values, cosine, sine_rows):
    half_dim = HEAD_DIM // 2
    turned = jnp.concatenate([values[..., half_dim:], values[..., :half_dim]], axis=-1)
    return values * cosine[None] + turned * sine_rows[None]


def norm_back(grad_rows, normed, scale_rows, gain_col):
    grad_normed = grad_rows * gain_col
    grad_input = scale_rows * (
        grad_normed - normed * jnp.mean(grad_normed * normed, axis=-1, keepdims=True)
    )
    return (grad_input, jnp.sum(grad_rows * normed, axis=0))


def dot(a, b):
    return jnp.dot(a, b, preferred_element_type=F32)


def dot_bt(a, b):
    return lax.dot_general(a, b, (((1,), (1,)), ((), ())), preferred_element_type=F32)


def dot_at(a, b):
    return lax.dot_general(a, b, (((0,), (0,)), ((), ())), preferred_element_type=F32)


def body(
    prompt_x,
    cont_x,
    cont_ids,
    routes,
    qkv_weight,
    out_weight,
    router_weight,
    norm_gains,
    gate_up_weight,
    down_weight,
    prompt_cot,
    cont_cot,
):
    n_dp, n_ctx, n_exp = lax.axis_size("dp"), lax.axis_size("ctx"), lax.axis_size("exp")
    d, c, z = lax.axis_index("dp"), lax.axis_index("ctx"), lax.axis_index("exp")
    prompt_len = prompt_x.shape[1]
    cont_len = cont_x.shape[1]
    rows = prompt_len + cont_len
    prompt_total = prompt_len * n_ctx
    experts = router_weight.shape[1]
    capacity = rows * TOP * 17 // (16 * experts)
    score_scale = HEAD_DIM ** (-0.5)
    shard = qkv_weight.shape[0]
    heads_own = HEADS // n_ctx
    width = heads_own * HEAD_DIM
    head_groups = n_dp if (D // (n_dp * n_ctx)) % HEAD_DIM == 0 else 1
    head_run = D // (head_groups * n_ctx)
    own_expert = c * n_exp + z

    def ctx_swap(x, k):
        return lax.ppermute(x, "ctx", [(i, i ^ k) for i in range(n_ctx)])

    def exp_shift(x, s):
        return lax.ppermute(x, "exp", [(i, (i + s) % n_exp) for i in range(n_exp)])

    def dp_shift(x, m):
        return lax.ppermute(x, "dp", [(i, (i + m) % n_dp) for i in range(n_dp)])

    def pick(x, axis, k):
        return lax.dynamic_index_in_dim(x, c ^ k, axis, keepdims=False)

    def place(buffer, x, *index):
        start, shape = [], []
        for at, size in zip(index, buffer.shape):
            start.append(0 if at is None else at)
            shape.append(size if at is None else 1)
        shape += buffer.shape[len(index) :]
        start += [0] * (buffer.ndim - len(index))
        return lax.dynamic_update_slice(buffer, x.reshape(shape), start)

    x_own = jnp.concatenate([prompt_x[0], cont_x[0]], axis=0)
    cot_own = jnp.concatenate([prompt_cot[0], cont_cot[0]], axis=0)

    small = jnp.concatenate([router_weight, norm_gains], axis=1)
    small_width = small.shape[1]
    small_ctx = jnp.zeros((n_ctx,) + small.shape, BF16)
    for k in range(n_ctx):
        small_ctx = place(small_ctx, ctx_swap(small, k) if k else small, c ^ k)
    small_all = jnp.zeros((n_dp, n_ctx, n_exp) + small.shape, BF16)
    small_exp = jnp.zeros((n_ctx, n_exp) + small.shape, BF16)
    for s in range(n_exp):
        small_exp = place(
            small_exp, exp_shift(small_ctx, s) if s else small_ctx, None, (z - s) % n_exp
        )
    for m in range(n_dp):
        small_all = place(small_all, dp_shift(small_exp, m) if m else small_exp, (d - m) % n_dp)
    small_all = small_all.reshape(D, small_width)
    w_router = small_all[:, :experts]
    gains_t = small_all[:, experts:].astype(F32).T
    gain_in, gain_ffn = gains_t[0], gains_t[3]

    def own_features(v):
        shaped = v.reshape(v.shape[:-1] + (head_groups, n_ctx, head_run))
        return pick(shaped, v.ndim, 0).reshape(v.shape[:-1] + (width,))

    gain_query, gain_key = own_features(gains_t[1]), own_features(gains_t[2])

    x_blocks = [x_own] + [ctx_swap(x_own, k) for k in range(1, n_ctx)]
    id_row = cont_ids[0]
    ids = [id_row] + [ctx_swap(id_row, k) for k in range(1, n_ctx)]
    route_rows = routes[0, 0]
    route_blocks = [route_rows] + [exp_shift(route_rows, s) for s in range(1, n_exp)]

    def by_owner(v):
        runs = v.shape[1] // (n_ctx * head_run)
        return jnp.stack(
            [
                jnp.concatenate(
                    [
                        v[:, (i * n_ctx + j) * head_run : (i * n_ctx + j + 1) * head_run]
                        for i in range(runs)
                    ],
                    axis=1,
                )
                for j in range(n_ctx)
            ]
        )

    def all_owners(v):
        runs = v.shape[2] // head_run
        return jnp.concatenate(
            [
                v[j][:, i * head_run : (i + 1) * head_run]
                for i in range(runs)
                for j in range(n_ctx)
            ],
            axis=1,
        )

    parts_w = by_owner(qkv_weight)
    slab = jnp.zeros((n_ctx, shard, 3 * width), BF16)
    for k in range(n_ctx):
        piece = pick(parts_w, 0, k)
        slab = place(slab, ctx_swap(piece, k) if k else piece, c ^ k)
    w_qkv = jnp.zeros((n_dp, n_ctx, n_exp, shard, 3 * width), BF16)
    moving = slab
    for s in range(n_exp):
        if s:
            moving = exp_shift(moving, 1)
        for m in range(n_dp):
            w_qkv = place(
                w_qkv,
                dp_shift(moving, m) if m else moving,
                (d - m) % n_dp,
                None,
                (z - s) % n_exp,
            )
    w_qkv = w_qkv.reshape(D, 3 * width)

    moving = out_weight
    out_exp = jnp.zeros((n_exp, shard, D), BF16)
    for s in range(n_exp):
        if s:
            moving = exp_shift(moving, 1)
        out_exp = place(out_exp, moving, (z - s) % n_exp)
    w_out = jnp.zeros((n_dp, n_ctx, n_exp, shard, D), BF16)
    for k in range(n_ctx):
        from_ctx = ctx_swap(out_exp, k) if k else out_exp
        for m in range(n_dp):
            w_out = place(
                w_out, dp_shift(from_ctx, m) if m else from_ctx, (d - m) % n_dp, c ^ k
            )
    w_out = w_out.reshape(D, D)

    upper = (
        jnp.arange(rows, dtype=jnp.int32)[:, None] < jnp.arange(rows, dtype=jnp.int32)[None, :]
    ).astype(BF16)
    send_experts = jnp.stack([(c ^ k) * n_exp + z for k in range(n_ctx)])
    spread = []
    for s in range(n_exp):
        named = jnp.any(
            route_blocks[s][None, :, :] == send_experts[:, None, None], axis=-1
        )
        rank = dot(named.astype(BF16), upper)
        slots = jnp.where(named, rank, -1.0)
        spread.append(
            (slots[:, None, :] == jnp.arange(capacity, dtype=F32)[None, :, None])
            .astype(BF16)
            .reshape(n_ctx * capacity, rows)
        )

    def dispatch(own_rows):
        arrived = [None] * (n_exp * n_ctx)
        block = own_rows
        for s in range(n_exp):
            if s:
                block = exp_shift(block, 1)
            packed = dot(spread[s], block).astype(BF16)
            for k in range(n_ctx):
                piece = packed[k * capacity : (k + 1) * capacity]
                arrived[s * n_ctx + k] = ctx_swap(piece, k) if k else piece
        return jnp.concatenate(arrived, axis=0)

    def give_back(expert_rows):
        total = None
        for s in range(n_exp):
            pieces = []
            for k in range(n_ctx):
                at = (s * n_ctx + k) * capacity
                piece = expert_rows[at : at + capacity]
                pieces.append(ctx_swap(piece, k) if k else piece)
            summed = dot_at(spread[s], jnp.concatenate(pieces, axis=0))
            if s:
                summed = exp_shift(summed.astype(BF16), n_exp - s).astype(F32)
            total = summed if total is None else total + summed
        return total

    cot_rows = dispatch(cot_own)
    w_gate_up = gate_up_weight[0]
    w_down = down_weight[0]
    act_cot = dot_bt(cot_rows, w_down)

    total_rows = rows * n_ctx
    index = jnp.arange(rows, dtype=jnp.int32)
    in_prompt = index < prompt_len
    position, seg_rows, block_rows, order_rows, prompt_rows = [], [], [], [], []
    for k in range(n_ctx):
        seg = ids[k][0]
        starts = jnp.sum((seg[None, :] < seg[:, None]).astype(jnp.int32), axis=1)
        within = jnp.arange(cont_len, dtype=jnp.int32) - starts
        at = (c ^ k) * prompt_len
        position.append(
            jnp.concatenate([at + index[:prompt_len], prompt_total + within])
        )
        order_rows.append(jnp.where(in_prompt, at + index, index))
        seg_rows.append(
            jnp.concatenate([jnp.full((prompt_len,), -1, jnp.int32), k * 64 + seg])
        )
        prompt_rows.append(in_prompt)
    position = jnp.concatenate(position).astype(F32)
    order = jnp.concatenate(order_rows)
    seg_of = jnp.concatenate(seg_rows)
    is_prompt = jnp.concatenate(prompt_rows)
    before = order[None, :] <= order[:, None]
    allowed = jnp.where(
        is_prompt[:, None],
        is_prompt[None, :] & before,
        is_prompt[None, :] | ((seg_of[None, :] == seg_of[:, None]) & before),
    )
    cosine, sine_rows = rope_tables(position, HEAD_DIM // 2)

    x_all = jnp.concatenate(x_blocks, axis=0).astype(F32)
    scale_in = row_scale(x_all)
    hidden_in = (x_all * scale_in * gain_in).astype(BF16)
    projected = dot(hidden_in, w_qkv)

    def ctx_sum(pair):
        total = pair
        for k in range(1, n_ctx):
            turned = [pair[:, (j ^ k) * rows : ((j ^ k) + 1) * rows] for j in range(n_ctx)]
            total = total + ctx_swap(jnp.concatenate(turned, axis=1), k)
        return total

    raw_query, raw_key = projected[:, :width], projected[:, width : 2 * width]
    squares = jnp.stack([jnp.sum(raw_query * raw_query, axis=-1), jnp.sum(raw_key * raw_key, axis=-1)])
    scales = lax.rsqrt(ctx_sum(squares) / D + NORM_EPS)
    scale_query, scale_key = scales[0][:, None], scales[1][:, None]
    normed_query = raw_query * scale_query
    normed_key = raw_key * scale_key

    def by_head(v):
        return jnp.stack([v[:, i * HEAD_DIM : (i + 1) * HEAD_DIM] for i in range(heads_own)])

    def side_by_side(v):
        return jnp.concatenate([v[i] for i in range(heads_own)], axis=1)

    heads_q = rotate(by_head(normed_query * gain_query), cosine, sine_rows).astype(BF16)
    heads_k = rotate(by_head(normed_key * gain_key), cosine, sine_rows).astype(BF16)
    heads_v = by_head(projected[:, 2 * width :].astype(BF16))

    def score_block():
        raw_scores = (
            jnp.einsum("hrd,hkd->hrk", heads_q, heads_k, preferred_element_type=F32) * score_scale
        )
        return jnp.where(allowed[None], raw_scores, NEGATIVE)

    scores = score_block()
    row_max = jnp.max(scores, axis=-1, keepdims=True)
    log_total = row_max + jnp.log(jnp.sum(jnp.exp(scores - row_max), axis=-1, keepdims=True))
    attention = jnp.exp(scores - log_total)
    attention_b = attention.astype(BF16)
    mixed_heads = side_by_side(
        jnp.einsum("hrk,hkd->hrd", attention_b, heads_v, preferred_element_type=F32).astype(BF16)
    )

    mixed = jnp.zeros((n_ctx, rows, width), BF16)
    for k in range(n_ctx):
        piece = mixed_heads[k * rows : (k + 1) * rows]
        mixed = place(mixed, ctx_swap(piece, k) if k else piece, c ^ k)
    mixed = all_owners(mixed)
    inputs = x_own.astype(F32)
    mid_rows = inputs + dot(mixed, w_out)
    scale_ffn = row_scale(mid_rows)
    normed_ffn = mid_rows * scale_ffn
    hidden_ffn = (normed_ffn * gain_ffn).astype(BF16)

    def softmax(logits):
        shifted = jnp.exp(logits - jnp.max(logits, axis=-1, keepdims=True))
        return shifted / jnp.sum(shifted, axis=-1, keepdims=True)

    expert_in = dispatch(hidden_ffn)
    router_in = softmax(dot(expert_in, w_router))
    gate_in = jnp.sum(
        jnp.where(jnp.arange(experts)[None, :] == own_expert, router_in, 0.0), axis=-1, keepdims=True
    )
    gate_up = dot(expert_in, w_gate_up)
    gate_part, up_part = gate_up[:, :FF], gate_up[:, FF:]
    sigmoid_gate = jax.nn.sigmoid(gate_part)
    swish = gate_part * sigmoid_gate
    activated = (swish * up_part).astype(BF16)
    act_grad = gate_in * act_cot
    gate_part_grad = act_grad * up_part * sigmoid_gate * (1.0 + gate_part * (1.0 - sigmoid_gate))
    gu_grad = jnp.concatenate([gate_part_grad, act_grad * swish], axis=1).astype(BF16)
    gate_grad = jnp.sum(act_cot * activated.astype(F32), axis=-1, keepdims=True)
    row_grad = dot_bt(gu_grad, w_gate_up).astype(BF16)
    grad_high = gate_grad.astype(BF16)
    grad_low = (gate_grad - grad_high.astype(F32)).astype(BF16)
    column = jnp.arange(-(-2 * experts // 128) * 128)[None, :]
    zero = jnp.zeros((), BF16)
    gate_cols = jnp.where(
        column == own_expert, grad_high, jnp.where(column == experts + own_expert, grad_low, zero)
    )
    returned = give_back(jnp.concatenate([row_grad, gate_cols], axis=1))

    expert_out = dot(activated, w_down).astype(BF16)
    mixture = give_back((gate_in * expert_out.astype(F32)).astype(BF16))
    final_rows = (mid_rows + mixture).astype(BF16)

    def dp_halves(grad):
        total = lax.dynamic_index_in_dim(grad, d, 0, keepdims=False)
        for m in range(1, n_dp):
            part = lax.dynamic_index_in_dim(grad, (d + m) % n_dp, 0, keepdims=False)
            total = total + dp_shift(part.astype(BF16), m).astype(F32)
        return total

    route_grad = (gate_in * cot_rows.astype(F32)).astype(BF16)
    grad_gate_up = dp_halves(
        dot_at(expert_in, gu_grad).reshape(n_dp, D // n_dp, 2 * FF)
    )
    grad_down = dp_halves(dot_at(activated, route_grad).reshape(n_dp, FF // n_dp, D))

    router = softmax(dot(hidden_ffn, w_router))
    prob_grad = returned[:, D : D + experts] + returned[:, D + experts : D + 2 * experts]
    logit_grad = router * (prob_grad - jnp.sum(router * prob_grad, axis=-1, keepdims=True))
    ffn_grad = returned[:, :D] + jnp.dot(logit_grad, w_router.astype(F32).T, precision=HIGHEST_PREC)
    router_grad_t = jnp.einsum(
        "re,rd->ed", logit_grad, hidden_ffn.astype(F32), precision=HIGHEST_PREC
    )
    mid_norm_grad, ffn_gain_grad = norm_back(ffn_grad, normed_ffn, scale_ffn, gain_ffn)
    mid_grad = cot_own.astype(F32) + mid_norm_grad

    attn_grad = mid_grad.astype(BF16)
    mixed_grad_own = dot_bt(attn_grad, w_out).astype(BF16)
    shaped_grad = by_owner(mixed_grad_own)
    mixed_grad = []
    for k in range(n_ctx):
        piece = pick(shaped_grad, 0, k)
        mixed_grad.append(ctx_swap(piece, k) if k else piece)
    heads_g = by_head(jnp.concatenate(mixed_grad, axis=0))
    prob_att = jnp.einsum("hrd,hkd->hrk", heads_g, heads_v, preferred_element_type=F32)
    attention = jnp.exp(score_block() - log_total)
    attention_b = attention.astype(BF16)
    delta = jnp.sum(attention * prob_att, axis=-1, keepdims=True)
    score_grad = (attention * (prob_att - delta)).astype(BF16)
    query_grad = (
        jnp.einsum("hrk,hkd->hrd", score_grad, heads_k, preferred_element_type=F32) * score_scale
    )
    key_grad = (
        jnp.einsum("hrk,hrd->hkd", score_grad, heads_q, preferred_element_type=F32) * score_scale
    )
    value_grad = jnp.einsum("hrk,hrd->hkd", attention_b, heads_g, preferred_element_type=F32)
    query_turn = side_by_side(rotate(query_grad, cosine, -sine_rows))
    key_turn = side_by_side(rotate(key_grad, cosine, -sine_rows))
    query_up, key_up = query_turn * gain_query, key_turn * gain_key
    sums = jnp.stack(
        [jnp.sum(query_up * normed_query, axis=-1), jnp.sum(key_up * normed_key, axis=-1)]
    )
    means = ctx_sum(sums) / D
    raw_query_grad = scale_query * (query_up - normed_query * means[0][:, None])
    raw_key_grad = scale_key * (key_up - normed_key * means[1][:, None])
    query_gain_grad = jnp.sum(query_turn * normed_query, axis=0)
    key_gain_grad = jnp.sum(key_turn * normed_key, axis=0)
    proj_grad = jnp.concatenate(
        [raw_query_grad, raw_key_grad, side_by_side(value_grad)], axis=1
    ).astype(BF16)

    def exp_reduce(grad):
        moving = None
        for s in range(1, n_exp + 1):
            part = lax.dynamic_index_in_dim(grad, (z - s) % n_exp, 0, keepdims=False)
            moving = part if moving is None else moving.astype(F32) + part
            if s < n_exp:
                moving = exp_shift(moving.astype(BF16), 1)
        return moving

    qkv_local = dot_at(hidden_in, proj_grad).reshape(n_dp, n_ctx, n_exp, shard, 3 * width)
    qkv_dp = dp_halves(qkv_local)
    qkv_exp = exp_reduce(jnp.moveaxis(qkv_dp, 1, 0))
    grad_qkv = jnp.zeros((n_ctx, shard, 3 * width), F32)
    for k in range(n_ctx):
        piece = pick(qkv_exp, 0, k)
        piece = ctx_swap(piece.astype(BF16), k).astype(F32) if k else piece
        grad_qkv = place(grad_qkv, piece, c ^ k)
    grad_qkv = all_owners(grad_qkv)

    if head_groups == n_dp:
        attn_grad_all = jnp.concatenate(
            [attn_grad] + [ctx_swap(attn_grad, k) for k in range(1, n_ctx)], axis=0
        )
        out_local = dot_at(mixed_heads, attn_grad_all).reshape(n_dp, n_exp, shard, D)
        grad_out = exp_reduce(dp_halves(out_local))
    else:
        grad_out = lax.psum_scatter(
            dot_at(mixed, attn_grad), ("dp", "ctx", "exp"), scatter_dimension=0, tiled=True
        )

    hidden_part = dot_bt(proj_grad, w_qkv)
    hidden_grad = hidden_part[:rows]
    for k in range(1, n_ctx):
        piece = hidden_part[k * rows : (k + 1) * rows].astype(BF16)
        hidden_grad = hidden_grad + ctx_swap(piece, k).astype(F32)
    scale_own = scale_in[:rows]
    in_norm_grad, in_gain_grad = norm_back(hidden_grad, inputs * scale_own, scale_own, gain_in)
    input_grad = mid_grad + in_norm_grad

    def spread_features(v):
        shaped = jnp.zeros((head_groups, n_ctx, head_run), F32)
        return place(shaped, v.reshape(head_groups, 1, head_run), None, c).reshape(1, D)

    small_grad = jnp.concatenate(
        [
            router_grad_t,
            in_gain_grad[None],
            spread_features(query_gain_grad),
            spread_features(key_gain_grad),
            ffn_gain_grad[None],
        ],
        axis=0,
    )
    count = small_grad.shape[0]
    part = small_grad.reshape(count, n_dp, n_ctx, n_exp, shard).transpose(1, 2, 3, 0, 4)
    total = lax.dynamic_index_in_dim(part, d, 0, keepdims=False)
    for m in range(1, n_dp):
        total = total + dp_shift(
            lax.dynamic_index_in_dim(part, (d + m) % n_dp, 0, keepdims=False), m
        )
    part = total
    total = pick(part, 0, 0)
    for k in range(1, n_ctx):
        total = total + ctx_swap(pick(part, 0, k), k)
    part = total
    total = lax.dynamic_index_in_dim(part, z, 0, keepdims=False)
    for s in range(1, n_exp):
        total = total + exp_shift(
            lax.dynamic_index_in_dim(part, (z + s) % n_exp, 0, keepdims=False), s
        )
    small_sum = total.T

    return (
        final_rows[:prompt_len][None],
        final_rows[prompt_len:][None],
        input_grad[:prompt_len][None],
        input_grad[prompt_len:][None],
        grad_qkv,
        grad_out,
        small_sum[:, :experts],
        small_sum[:, experts:],
        grad_gate_up[None],
        grad_down[None],
    )


def solution(mesh):
    return jax.shard_map(
        body,
        mesh=mesh,
        in_specs=(
            P(("dp", "exp"), "ctx", None),
            P(("dp", "exp"), "ctx", None),
            P(("dp", "exp"), "ctx", None),
            P(("dp", "exp"), "ctx", None, None),
            P(("dp", "ctx", "exp"), None),
            P(("dp", "ctx", "exp"), None),
            P(("dp", "ctx", "exp"), None),
            P(("dp", "ctx", "exp"), None),
            P(("ctx", "exp"), None, None),
            P(("ctx", "exp"), None, None),
            P(("dp", "exp"), "ctx", None),
            P(("dp", "exp"), "ctx", None),
        ),
        out_specs=(
            P(("dp", "exp"), "ctx", None),
            P(("dp", "exp"), "ctx", None),
            P(("dp", "exp"), "ctx", None),
            P(("dp", "exp"), "ctx", None),
            P(("dp", "ctx", "exp"), None),
            P(("dp", "ctx", "exp"), None),
            P(("dp", "ctx", "exp"), None),
            P(("dp", "ctx", "exp"), None),
            P(("ctx", "exp"), "dp", None),
            P(("ctx", "exp"), "dp", None),
        ),
        check_vma=False,
    )
```

```python
import jax
import jax.numpy as jnp
from jax import lax
from jax.experimental import pallas as pl
from jax.experimental.pallas import tpu as pltpu
from jax.sharding import PartitionSpec as P

D = 2048
HEADS = 16
HEAD_DIM = 128
FF = 1024
TOP = 8

NORM_EPS = 1e-05
ROPE_BASE = 10000.0
NEGATIVE = -1e30
HIGHEST_PREC = lax.Precision.HIGHEST
F32 = jnp.float32
BF16 = jnp.bfloat16


def row_scale(values):
    return lax.rsqrt(jnp.mean(values * values, axis=-1, keepdims=True) + NORM_EPS)


def rope_tables(position, half_dim):
    inverse = ROPE_BASE ** (-jnp.arange(half_dim, dtype=F32) / half_dim)
    angles = position[:, None] * inverse[None, :]
    cosine, sine_rows = jnp.cos(angles), jnp.sin(angles)
    return (
        jnp.concatenate([cosine, cosine], axis=1),
        jnp.concatenate([-sine_rows, sine_rows], axis=1),
    )


def norm_back(grad_rows, normed, scale_rows, gain_col):
    grad_normed = grad_rows * gain_col
    grad_input = scale_rows * (
        grad_normed - normed * jnp.mean(grad_normed * normed, axis=-1, keepdims=True)
    )
    return (grad_input, jnp.sum(grad_rows * normed, axis=0))


def dot(a, b):
    return jnp.dot(a, b, preferred_element_type=F32)


def dot_bt(a, b):
    return lax.dot_general(a, b, (((1,), (1,)), ((), ())), preferred_element_type=F32)


def dot_at(a, b):
    return lax.dot_general(a, b, (((0,), (0,)), ((), ())), preferred_element_type=F32)


def attend(projected, scales, gains, cosine, sine_rows, hidden_pairs):
    rows = projected.shape[0]
    width = projected.shape[1] // 3
    heads = width // HEAD_DIM

    def kernel(pq, pk, pv, scale_ref, gain_ref, cos_ref, sin_ref, pair_ref, mixed, q, k, v, total):
        def turned(values):
            return values * cos_ref[...] + pltpu.roll(values, HEAD_DIM // 2, 1) * sin_ref[...]

        query = turned(pq[...] * scale_ref[:, :1] * gain_ref[:1, :]).astype(BF16)
        key = turned(pk[...] * scale_ref[:, 1:2] * gain_ref[1:2, :]).astype(BF16)
        value = pv[...].astype(BF16)
        scores = dot_bt(query, key) * HEAD_DIM ** (-0.5)
        scores = jnp.where(pair_ref[...] < 0.0, NEGATIVE, scores)
        row_max = jnp.max(scores, axis=-1, keepdims=True)
        log_total = row_max + jnp.log(
            jnp.sum(jnp.exp(scores - row_max), axis=-1, keepdims=True)
        )
        mixed[...] = dot(jnp.exp(scores - log_total).astype(BF16), value).astype(BF16)
        q[...], k[...], v[...] = query, key, value
        total[...] = jnp.broadcast_to(log_total, total.shape)

    def head(part):
        return pl.BlockSpec((rows, HEAD_DIM), lambda h: (0, part * heads + h))

    def whole(shape):
        return pl.BlockSpec(shape, lambda h: (0, 0))

    return pl.pallas_call(
        kernel,
        grid=(heads,),
        in_specs=[
            head(0),
            head(1),
            head(2),
            whole((rows, 2)),
            pl.BlockSpec((2, HEAD_DIM), lambda h: (0, h)),
            whole((rows, HEAD_DIM)),
            whole((rows, HEAD_DIM)),
            whole((rows, rows)),
        ],
        out_specs=[head(0)] * 5,
        out_shape=[jax.ShapeDtypeStruct((rows, width), BF16)] * 4
        + [jax.ShapeDtypeStruct((rows, width), F32)],
        compiler_params=pltpu.CompilerParams(vmem_limit_bytes=48 << 20),
        cost_estimate=pl.CostEstimate(flops=0, bytes_accessed=0, transcendentals=0),
        name="attend",
    )(projected, projected, projected, scales, gains, cosine, sine_rows, hidden_pairs)


def attend_back(grads, kept, projected, scales, gains, cosine, sine_rows, hidden_pairs):
    query_b, key_b, value_b, log_total = kept
    rows = projected.shape[0]
    width = projected.shape[1] // 3
    heads = width // HEAD_DIM
    scale = HEAD_DIM ** (-0.5)

    def kernel(
        g, q, k, v, total, pq, pk, scale_ref, gain_ref, cos_ref, sin_ref, pair_ref,
        query_out, key_out, value_out, gain_out, sum_out,
    ):
        def turned_back(values):
            return values * cos_ref[...] - pltpu.roll(values, HEAD_DIM // 2, 1) * sin_ref[...]

        scores = dot_bt(q[...], k[...]) * scale
        scores = jnp.where(pair_ref[...] < 0.0, NEGATIVE, scores)
        attention = jnp.exp(scores - total[:, :1])
        prob_att = dot_bt(g[...], v[...])
        delta = jnp.sum(attention * prob_att, axis=-1, keepdims=True)
        score_grad = (attention * (prob_att - delta)).astype(BF16)
        query = turned_back(dot(score_grad, k[...]) * scale)
        key = turned_back(dot_at(score_grad, q[...]) * scale)
        value_out[...] = dot_at(attention.astype(BF16), g[...]).astype(BF16)
        query_out[...], key_out[...] = query, key
        query_n = query * (pq[...] * scale_ref[:, :1])
        key_n = key * (pk[...] * scale_ref[:, 1:2])
        gain_out[:1, :] = jnp.sum(query_n, axis=0, keepdims=True)
        gain_out[1:2, :] = jnp.sum(key_n, axis=0, keepdims=True)
        query_sum = jnp.sum(query_n * gain_ref[:1, :], axis=-1, keepdims=True)
        key_sum = jnp.sum(key_n * gain_ref[1:2, :], axis=-1, keepdims=True)
        sums = jnp.concatenate(
            [
                jnp.broadcast_to(query_sum, (rows, HEAD_DIM)),
                jnp.broadcast_to(key_sum, (rows, HEAD_DIM)),
            ],
            axis=1,
        )

        @pl.when(pl.program_id(0) == 0)
        def _():
            sum_out[...] = sums

        @pl.when(pl.program_id(0) > 0)
        def _():
            sum_out[...] += sums

    def head(part):
        return pl.BlockSpec((rows, HEAD_DIM), lambda h: (0, part * heads + h))

    def whole(shape):
        return pl.BlockSpec(shape, lambda h: (0, 0))

    pair = pl.BlockSpec((2, HEAD_DIM), lambda h: (0, h))
    return pl.pallas_call(
        kernel,
        grid=(heads,),
        in_specs=[head(0)] * 5
        + [
            head(0),
            head(1),
            whole((rows, 2)),
            pair,
            whole((rows, HEAD_DIM)),
            whole((rows, HEAD_DIM)),
            whole((rows, rows)),
        ],
        out_specs=[head(0)] * 3 + [pair, whole((rows, 2 * HEAD_DIM))],
        out_shape=[
            jax.ShapeDtypeStruct((rows, width), F32),
            jax.ShapeDtypeStruct((rows, width), F32),
            jax.ShapeDtypeStruct((rows, width), BF16),
            jax.ShapeDtypeStruct((2, width), F32),
            jax.ShapeDtypeStruct((rows, 2 * HEAD_DIM), F32),
        ],
        compiler_params=pltpu.CompilerParams(vmem_limit_bytes=48 << 20),
        cost_estimate=pl.CostEstimate(flops=0, bytes_accessed=0, transcendentals=0),
        name="attend_back",
    )(
        grads, query_b, key_b, value_b, log_total, projected, projected, scales, gains,
        cosine, sine_rows, hidden_pairs,
    )


def norms_back(query_turn, key_turn, value_grad, projected, scales, means, gains):
    rows, width = query_turn.shape

    def kernel(query, key, value, projected_ref, scale_ref, mean_ref, gain_ref, out):
        for i, turn in enumerate((query, key)):
            at = slice(i * width, (i + 1) * width)
            scale = scale_ref[:, i : i + 1]
            normed = projected_ref[:, at] * scale
            out[:, at] = (
                scale * (turn[...] * gain_ref[i : i + 1, :] - normed * mean_ref[:, i : i + 1])
            ).astype(BF16)
        out[:, 2 * width :] = value[...]

    return pl.pallas_call(
        kernel,
        out_shape=jax.ShapeDtypeStruct((rows, 3 * width), BF16),
        compiler_params=pltpu.CompilerParams(vmem_limit_bytes=48 << 20),
        cost_estimate=pl.CostEstimate(flops=0, bytes_accessed=0, transcendentals=0),
        name="norms_back",
    )(query_turn, key_turn, value_grad, projected, scales, means, gains)


def expert_rows(rows, cot, w_gate_up, w_down, w_router, expert, senders, blocks):
    count, experts = rows.shape[0], w_router.shape[1]
    tile = FF // 2
    steps = FF // tile
    extra = -(-2 * experts // 128) * 128
    piece = count // (senders * blocks)

    def kernel(expert_ref, rows_ref, cot_ref, wg_ref, wu_ref, wd_ref, wr_ref, *refs):
        row_refs = refs[:blocks]
        act_ref, gg_ref, ug_ref, gate_ref, row_sum, gate_grad = refs[blocks:]
        step = pl.program_id(0)
        row_block = rows_ref[...]

        @pl.when(step == 0)
        def _():
            logits = dot(row_block, wr_ref[...])
            shifted = jnp.exp(logits - jnp.max(logits, axis=-1, keepdims=True))
            router = shifted / jnp.sum(shifted, axis=-1, keepdims=True)
            lane = lax.broadcasted_iota(jnp.int32, router.shape, 1)
            own = jnp.sum(jnp.where(lane == expert_ref[0], router, 0.0), axis=-1, keepdims=True)
            gate_ref[...] = jnp.broadcast_to(own, gate_ref.shape)

        gate = gate_ref[:, :1]
        gate_part = dot(row_block, wg_ref[...])
        up_part = dot(row_block, wu_ref[...])
        cot_act = dot_bt(cot_ref[...], wd_ref[...])
        sigmoid_gate = jax.nn.sigmoid(gate_part)
        swish = gate_part * sigmoid_gate
        activated = (swish * up_part).astype(BF16)
        act_grad = gate * cot_act
        gate_part_grad = (
            act_grad * up_part * sigmoid_gate * (1.0 + gate_part * (1.0 - sigmoid_gate))
        ).astype(BF16)
        up_part_grad = (act_grad * swish).astype(BF16)
        act_ref[...] = activated
        gg_ref[...] = gate_part_grad
        ug_ref[...] = up_part_grad
        row_part = dot_bt(gate_part_grad, wg_ref[...]) + dot_bt(up_part_grad, wu_ref[...])
        part = jnp.sum(cot_act * activated.astype(F32), axis=-1, keepdims=True)
        part = jnp.broadcast_to(part, gate_grad.shape)

        @pl.when(step == 0)
        def _():
            row_sum[...] = row_part
            gate_grad[...] = part

        @pl.when(step > 0)
        def _():
            row_sum[...] += row_part
            gate_grad[...] += part

        @pl.when(step == steps - 1)
        def _():
            lane = lax.broadcasted_iota(jnp.int32, (piece, extra), 1)
            for j in range(senders):
                for i in range(blocks):
                    at = pl.ds((j * blocks + i) * piece, piece)
                    row_refs[i][j, :, :D] = row_sum[at, :].astype(BF16)
                    both = jnp.broadcast_to(gate_grad[at, :1], (piece, extra))
                    high = both.astype(BF16).astype(F32)
                    row_refs[i][j, :, D:] = jnp.where(
                        lane == expert_ref[0],
                        high,
                        jnp.where(lane == experts + expert_ref[0], both - high, 0.0),
                    ).astype(BF16)

    def whole(shape):
        return pl.BlockSpec(shape, lambda j, at: (0, 0))

    columns = pl.BlockSpec((count, tile), lambda j, at: (0, j))
    return pl.pallas_call(
        kernel,
        grid_spec=pltpu.PrefetchScalarGridSpec(
            num_scalar_prefetch=1,
            grid=(steps,),
            in_specs=[
                whole((count, D)),
                whole((count, D)),
                pl.BlockSpec((D, tile), lambda j, at: (0, j)),
                pl.BlockSpec((D, tile), lambda j, at: (0, steps + j)),
                pl.BlockSpec((tile, D), lambda j, at: (j, 0)),
                whole((D, experts)),
            ],
            out_specs=[pl.BlockSpec((senders, piece, D + extra), lambda j, at: (0, 0, 0))] * blocks
            + [columns, columns, columns, whole((count, 128))],
            scratch_shapes=[pltpu.VMEM((count, D), F32), pltpu.VMEM((count, 128), F32)],
        ),
        out_shape=[jax.ShapeDtypeStruct((senders, piece, D + extra), BF16)] * blocks
        + [
            jax.ShapeDtypeStruct((count, FF), BF16),
            jax.ShapeDtypeStruct((count, FF), BF16),
            jax.ShapeDtypeStruct((count, FF), BF16),
            jax.ShapeDtypeStruct((count, 128), F32),
        ],
        compiler_params=pltpu.CompilerParams(vmem_limit_bytes=56 << 20),
        cost_estimate=pl.CostEstimate(flops=0, bytes_accessed=0, transcendentals=0),
        name="expert",
    )(expert, rows, cot, w_gate_up, w_gate_up, w_down, w_router)


def expert_outs(acts, gates, cot, w_down):
    count = acts.shape[0]
    tile = count // 2

    def kernel(act_ref, gate_ref, cot_ref, wd_ref, mix_ref, route_ref):
        gate = gate_ref[:, :1]
        out = dot(act_ref[...], wd_ref[...]).astype(BF16)
        mix_ref[...] = (gate * out.astype(F32)).astype(BF16)
        route_ref[...] = (gate * cot_ref[...].astype(F32)).astype(BF16)

    def rows_of(columns):
        return pl.BlockSpec((tile, columns), lambda i: (i, 0))

    return pl.pallas_call(
        kernel,
        grid=(count // tile,),
        in_specs=[rows_of(FF), rows_of(128), rows_of(D), pl.BlockSpec((FF, D), lambda i: (0, 0))],
        out_specs=[rows_of(D), rows_of(D)],
        out_shape=[jax.ShapeDtypeStruct((count, D), BF16)] * 2,
        compiler_params=pltpu.CompilerParams(vmem_limit_bytes=56 << 20),
        cost_estimate=pl.CostEstimate(
            flops=2 * count * FF * D, bytes_accessed=6 * count * D + 2 * FF * D, transcendentals=0
        ),
        name="expert_outs",
    )(acts, gates, cot, w_down)


def weight_grad(lefts, rights, part, rows_out, arrived=()):
    blocks, parts = len(lefts), len(rights[0])
    depth = lefts[0].shape[0]
    tile = min(256, rows_out)
    tiles = rows_out // tile
    widths = [v.shape[1] for v in rights[0]]

    def kernel(part_ref, *refs):
        left, right, out = refs[:blocks], refs[blocks : blocks * (1 + parts)], refs[-1]
        at = 0
        for p in range(parts):
            total = dot_at(left[0][...], right[p][...])
            for b in range(1, blocks):
                total = total + dot_at(left[b][...], right[b * parts + p][...])
            for more in refs[blocks * (1 + parts) : -1]:
                total = total + more[:, at : at + widths[p]].astype(F32)
            out[:, at : at + widths[p]] = total.astype(out.dtype)
            at += widths[p]

    row_block = pl.BlockSpec((tile, sum(widths)), lambda i, at: (i, 0))
    return pl.pallas_call(
        kernel,
        grid_spec=pltpu.PrefetchScalarGridSpec(
            num_scalar_prefetch=1,
            grid=(tiles,),
            in_specs=[pl.BlockSpec((depth, tile), lambda i, at: (0, at[0] * tiles + i))] * blocks
            + [
                pl.BlockSpec((depth, w), lambda i, at: (0, 0))
                for _ in range(blocks)
                for w in widths
            ]
            + [row_block] * len(arrived),
            out_specs=row_block,
        ),
        out_shape=jax.ShapeDtypeStruct((rows_out, sum(widths)), F32 if arrived else BF16),
        compiler_params=pltpu.CompilerParams(vmem_limit_bytes=56 << 20),
        cost_estimate=pl.CostEstimate(
            flops=4 * blocks * depth * rows_out * sum(widths),
            bytes_accessed=2 * blocks * depth * (rows_out + sum(widths)) + 4 * rows_out * sum(widths),
            transcendentals=0,
        ),
        name="weight_grad",
    )(part.reshape(1).astype(jnp.int32), *lefts, *[v for r in rights for v in r], *arrived)


def body(
    prompt_x,
    cont_x,
    cont_ids,
    routes,
    qkv_weight,
    out_weight,
    router_weight,
    norm_gains,
    gate_up_weight,
    down_weight,
    prompt_cot,
    cont_cot,
):
    n_dp, n_ctx, n_exp = lax.axis_size("dp"), lax.axis_size("ctx"), lax.axis_size("exp")
    d, c, z = lax.axis_index("dp"), lax.axis_index("ctx"), lax.axis_index("exp")
    prompt_len = prompt_x.shape[1]
    cont_len = cont_x.shape[1]
    rows = prompt_len + cont_len
    prompt_total = prompt_len * n_ctx
    experts = router_weight.shape[1]
    capacity = rows * TOP * 17 // (16 * experts)
    score_scale = HEAD_DIM ** (-0.5)
    shard = qkv_weight.shape[0]
    heads_own = HEADS // n_ctx
    width = heads_own * HEAD_DIM
    head_groups = n_dp if (D // (n_dp * n_ctx)) % HEAD_DIM == 0 else 1
    head_run = D // (head_groups * n_ctx)
    own_expert = c * n_exp + z

    def ctx_swap(x, k):
        return lax.ppermute(x, "ctx", [(i, i ^ k) for i in range(n_ctx)])

    def ctx_trade(x):
        return lax.all_to_all(x, "ctx", 0, 0, tiled=True)

    def ctx_gather(x):
        return ctx_trade(jnp.broadcast_to(x[None], (n_ctx,) + x.shape))

    def exp_shift(x, s):
        return lax.ppermute(x, "exp", [(i, (i + s) % n_exp) for i in range(n_exp)])

    def dp_shift(x, m):
        return lax.ppermute(x, "dp", [(i, (i + m) % n_dp) for i in range(n_dp)])

    def part_of(x, axis, at):
        return lax.dynamic_index_in_dim(x, at, axis, keepdims=False)

    def place(buffer, x, *index):
        start, shape = [], []
        for at, size in zip(index, buffer.shape):
            start.append(0 if at is None else at)
            shape.append(size if at is None else 1)
        shape += buffer.shape[len(index) :]
        start += [0] * (buffer.ndim - len(index))
        return lax.dynamic_update_slice(buffer, x.reshape(shape), start)

    def gate(x, *others):
        out = lax.optimization_barrier((x,) + others)[0]
        return list(out) if isinstance(out, tuple) else out

    mark = jnp.full((8, 128), d, jnp.int32).astype(F32)

    def hand_on(in_ref, out_ref):
        out_ref[...] = in_ref[...]

    def fence(*values):
        nonlocal mark
        mark = pl.pallas_call(
            hand_on,
            out_shape=jax.ShapeDtypeStruct(mark.shape, mark.dtype),
            cost_estimate=pl.CostEstimate(
                flops=2 * 10**11, bytes_accessed=0, transcendentals=0
            ),
            name="fence",
        )(gate(mark, *values))

    def after(*values):
        out = lax.optimization_barrier(values + (mark,))
        return out[0] if len(values) == 1 else out[:-1]

    def by_owner(v):
        runs = v.shape[1] // (n_ctx * head_run)
        return jnp.stack(
            [
                jnp.concatenate(
                    [
                        v[:, (i * n_ctx + j) * head_run : (i * n_ctx + j + 1) * head_run]
                        for i in range(runs)
                    ],
                    axis=1,
                )
                for j in range(n_ctx)
            ]
        )

    def all_owners(v):
        runs = v.shape[2] // head_run
        return jnp.concatenate(
            [
                v[j][:, i * head_run : (i + 1) * head_run]
                for i in range(runs)
                for j in range(n_ctx)
            ],
            axis=1,
        )

    x_own = jnp.concatenate([prompt_x[0], cont_x[0]], axis=0)
    cot_own = jnp.concatenate([prompt_cot[0], cont_cot[0]], axis=0)

    small_width = experts + norm_gains.shape[1]
    route_width = -(-rows * TOP // shard)
    route_cols = routes[0, 0].T.astype(BF16).reshape(-1)
    route_cols = jnp.pad(route_cols, (0, route_width * shard - rows * TOP)).reshape(shard, -1)
    extra = jnp.concatenate(
        [
            router_weight,
            norm_gains,
            jnp.broadcast_to(cont_ids[0].astype(BF16), (shard, cont_len)),
            route_cols,
        ],
        axis=1,
    )
    extra_width = -(-extra.shape[1] // 128) * 128
    extra = jnp.pad(extra, ((0, 0), (0, extra_width - extra.shape[1])))
    all_width = 3 * width + extra_width
    runs = 3 * width // head_run


    def pack(w_ref, extra_ref, out_ref):
        for j in range(n_ctx):
            for i in range(runs):
                out_ref[j, :, i * head_run : (i + 1) * head_run] = w_ref[
                    :, (i * n_ctx + j) * head_run : (i * n_ctx + j + 1) * head_run
                ]
            out_ref[j, :, 3 * width :] = extra_ref[...]

    packed_w = pl.pallas_call(
        pack, out_shape=jax.ShapeDtypeStruct((n_ctx, shard, all_width), BF16), name="pack"
    )(qkv_weight, extra)
    slab = ctx_trade(packed_w)
    out_blocks = [out_weight] + [exp_shift(out_weight, s) for s in range(1, n_exp)]
    fence(packed_w)

    def by_exp(v):
        shaped = v.reshape(v.shape[:-1] + (n_dp, n_ctx, n_exp, shard))
        return jnp.swapaxes(shaped, -3, -2).reshape(v.shape)

    def from_exp(v):
        shaped = v.reshape(v.shape[:-1] + (n_dp, n_exp, n_ctx, shard))
        return jnp.swapaxes(shaped, -3, -2).reshape(v.shape)

    x_turned = by_exp(x_own)
    out_blocks = after(*out_blocks)
    out_exp = jnp.zeros((n_exp, shard, D), BF16)
    for j in range(n_exp):
        out_exp = place(out_exp, out_blocks[j], (z - j) % n_exp)

    slab = after(slab)
    ids_at = 3 * width + small_width
    ids = slab[:, 0, ids_at : ids_at + cont_len].astype(F32).astype(jnp.int32)
    w_blocks = [slab] + [exp_shift(slab, s) for s in range(1, n_exp)]
    w_sets = [[dp_shift(slab, m)] for m in range(1, n_dp)]
    out_ctx = ctx_gather(gate(out_exp, slab))
    fence(slab, out_exp)
    out_ctx = after(out_ctx)
    x_sent = gate(x_turned, out_ctx)
    x_all = ctx_gather(x_sent)
    fence(x_sent)

    x_all = after(x_all).reshape(n_ctx * rows, D).astype(F32)
    scale_in = row_scale(x_all)
    w_blocks = gate(tuple(w_blocks), scale_in)
    for m in range(1, n_dp):
        w_sets[m - 1] += [dp_shift(v, m) for v in w_blocks[1:]]
    cot_blocks = [cot_own]
    routes_at = ids_at + cont_len
    route_rows = [
        part_of(v[..., routes_at : routes_at + route_width], 0, c)
        .reshape(-1)[: rows * TOP]
        .reshape(TOP, rows)
        for v in w_blocks
    ]
    places = jnp.stack(
        [(d - m) % n_dp for m in range(n_dp)] + [(z - s) % n_exp for s in range(n_exp)]
    ).astype(jnp.int32)

    def assemble(at_ref, *refs):
        blocks, (w_ref, small_ref) = refs[: n_dp * n_exp], refs[n_dp * n_exp :]
        for m in range(n_dp):
            for s in range(n_exp):
                block = blocks[m * n_exp + s]
                w_ref[at_ref[m], at_ref[n_dp + s]] = block[:, :, : 3 * width]
                small_ref[at_ref[m], at_ref[n_dp + s]] = block[:, :, 3 * width :]

    in_vmem = pl.BlockSpec(memory_space=pltpu.VMEM)
    w_qkv, w_small = pl.pallas_call(
        assemble,
        in_specs=[pl.BlockSpec(memory_space=pltpu.SMEM)] + [in_vmem] * (n_dp * n_exp),
        out_specs=[in_vmem] * 2,
        out_shape=[
            jax.ShapeDtypeStruct((n_dp, n_exp, n_ctx, shard, 3 * width), BF16),
            jax.ShapeDtypeStruct((n_dp, n_exp, n_ctx, shard, extra_width), BF16),
        ],
        compiler_params=pltpu.CompilerParams(vmem_limit_bytes=56 << 20),
        cost_estimate=pl.CostEstimate(flops=0, bytes_accessed=0, transcendentals=0),
        name="assemble",
    )(places, *w_blocks, *[v for w_set in w_sets for v in w_set])
    w_qkv = w_qkv.reshape(D, 3 * width)
    w_small = jnp.swapaxes(w_small, 1, 2).reshape(D, extra_width)
    w_router = w_small[:, :experts]
    gains_t = w_small[:, experts:small_width].astype(F32).T
    gain_in, gain_ffn = gains_t[0], gains_t[3]

    def own_features(v):
        shaped = v.reshape(v.shape[:-1] + (head_groups, n_ctx, head_run))
        return part_of(shaped, v.ndim, c).reshape(v.shape[:-1] + (width,))

    gain_query, gain_key = own_features(gains_t[1]), own_features(gains_t[2])

    upper = (
        jnp.arange(rows, dtype=jnp.int32)[:, None] < jnp.arange(rows, dtype=jnp.int32)[None, :]
    ).astype(BF16)
    send_experts = (jnp.arange(n_ctx) * n_exp + z).astype(F32)

    def spread_of(route_cols):
        named = jnp.any(
            route_cols.astype(F32)[None] == send_experts[:, None, None], axis=1
        )
        rank = dot(named.astype(BF16), upper)
        slots = jnp.where(named, rank, -1.0)
        return (
            (slots[:, None, :] == jnp.arange(capacity, dtype=F32)[None, :, None])
            .astype(BF16)
            .reshape(n_ctx * capacity, rows)
        )

    spread = [spread_of(v) for v in route_rows]

    def spread_pair(blocks):
        n = len(blocks)
        parts = []
        for i, s in enumerate(blocks):
            part = spread[s].reshape(n_ctx, 1, capacity, rows)
            parts.append(jnp.pad(part, ((0, 0), (0, 0), (0, 0), (i * rows, (n - 1 - i) * rows))))
        return jnp.concatenate(parts, axis=1).reshape(n_ctx * n * capacity, n * rows)

    def pack_of(spread_rows, blocks):
        n = len(blocks)
        sent = dot(spread_rows, blocks[0] if n == 1 else jnp.concatenate(blocks, axis=0))
        return sent.astype(BF16).reshape(n_ctx, n, capacity, -1)

    def pack_cot(blocks):
        return pack_of(
            spread_pair(blocks) if len(blocks) > 1 else spread[blocks[0]],
            [cot_blocks[s] for s in blocks],
        )

    def trade_pieces(pieces):
        return [ctx_swap(pieces[k], k) if k else pieces[k] for k in range(n_ctx)]

    def in_order(pieces):
        whole = jnp.zeros((n_ctx,) + pieces[0].shape, pieces[0].dtype)
        for k in range(n_ctx):
            whole = place(whole, pieces[k], c ^ k)
        return whole

    w_gate_up = gate_up_weight[0]
    w_down = down_weight[0]
    pairs = [list(range(i, i + 2)) for i in range(0, n_exp, 2)]

    total_rows = rows * n_ctx
    index = jnp.arange(rows, dtype=jnp.int32)
    in_prompt = index < prompt_len
    position, seg_rows, order = [], [], []
    for j in range(n_ctx):
        seg = ids[j]
        starts = jnp.sum((seg[None, :] < seg[:, None]).astype(jnp.int32), axis=1)
        within = jnp.arange(cont_len, dtype=jnp.int32) - starts
        at = j * prompt_len
        position.append(jnp.concatenate([at + index[:prompt_len], prompt_total + within]))
        order.append(jnp.where(in_prompt, at + index, index))
        seg_rows.append(
            jnp.concatenate([jnp.full((prompt_len,), -1, jnp.int32), j * 64 + seg])
        )
    position = jnp.concatenate(position).astype(F32)
    order = jnp.concatenate(order)
    seg_of = jnp.concatenate(seg_rows)
    is_prompt = jnp.concatenate([in_prompt] * n_ctx)
    before = order[None, :] <= order[:, None]
    allowed = jnp.where(
        is_prompt[:, None],
        is_prompt[None, :] & before,
        is_prompt[None, :] | ((seg_of[None, :] == seg_of[:, None]) & before),
    )
    hidden_pairs = jnp.where(allowed, 0.0, -1.0)
    cosine, sine_rows = rope_tables(position, HEAD_DIM // 2)

    cot_sent = gate(pack_cot([0]), scale_in)
    cot_trade = ctx_trade(cot_sent)
    fence(cot_sent, w_qkv)
    hidden_in = (x_all * after(scale_in) * by_exp(gain_in)).astype(BF16)
    projected = dot(hidden_in, w_qkv)

    def ctx_sum(total):
        k = 1
        while k < n_ctx:
            total = total + ctx_swap(total, k)
            k *= 2
        return total

    raw_query, raw_key = projected[:, :width], projected[:, width : 2 * width]
    squares = jnp.stack([jnp.sum(raw_query * raw_query, axis=-1), jnp.sum(raw_key * raw_key, axis=-1)])
    cot_flight = [exp_shift(gate(cot_blocks[0], squares), s) for s in range(1, n_exp)]
    scales = lax.rsqrt(ctx_sum(squares) / D + NORM_EPS)
    out_ctx = gate(out_ctx, scales)
    out_halves = [out_ctx] + [dp_shift(out_ctx, m) for m in range(1, n_dp)]
    fence(scales, out_ctx)
    scales = after(scales)
    scales = scales.T
    head_gains = jnp.stack([gain_query, gain_key])
    mixed_heads, *kept = attend(projected, scales, head_gains, cosine, sine_rows, hidden_pairs)

    mixed_heads = gate(mixed_heads, cot_trade)
    mixed = ctx_trade(mixed_heads.reshape(n_ctx, rows, width))
    cot_own_rows = cot_trade
    spreads = [spread_pair(pair) for pair in pairs]
    fence(mixed_heads, *spreads)
    mixed = after(mixed)
    cot_blocks += gate(tuple(cot_flight), mixed)
    mixed = all_owners(mixed)
    cot_sent = gate(pack_cot(list(range(1, n_exp))), mixed)
    cot_trade = ctx_trade(cot_sent)
    fence(mixed, cot_sent)
    mixed = after(mixed)
    half = D // n_dp
    mixed_halves = jnp.stack([mixed[:, i * half : (i + 1) * half] for i in range(n_dp)])
    inputs = x_own.astype(F32)
    mid_rows = inputs
    for m in range(n_dp):
        mid_rows = mid_rows + dot(
            part_of(mixed_halves, 0, (d - m) % n_dp), out_halves[m].reshape(half, D)
        )
    scale_ffn = row_scale(mid_rows)
    normed_ffn = mid_rows * scale_ffn
    hidden_ffn = (normed_ffn * gain_ffn).astype(BF16)

    def softmax(logits):
        shifted = jnp.exp(logits - jnp.max(logits, axis=-1, keepdims=True))
        return shifted / jnp.sum(shifted, axis=-1, keepdims=True)

    cot_rows, made = [], []

    def towards(blocks, back, spread_rows):
        return dot_at(spread_rows, back.reshape(spread_rows.shape[0], -1))

    def home(s, summed):
        return exp_shift(summed, n_exp - s)

    near = exp_shift(hidden_ffn, 1)
    fence(hidden_ffn)

    near = after(near)
    far = [exp_shift(gate(hidden_ffn, near), s) for s in range(2, n_exp)]
    cot_trade = after(cot_trade)
    sent = gate(pack_of(spreads[0], [hidden_ffn, near]), cot_trade)
    plane = ctx_trade(sent)
    fence(near, sent)

    cot_back = [cot_own_rows[:, 0]] + [after(cot_trade)[:, s] for s in range(n_exp - 1)]
    for pair in pairs:
        cot_rows.append(jnp.stack([cot_back[s] for s in pair], axis=1).reshape(-1, D))
    plane = after(plane)
    far = gate(tuple(after(*far)), plane)
    sent = pack_of(spreads[1], far)
    plane_next = ctx_trade(sent)
    fence(sent, plane)

    expert_at = own_expert.reshape(1).astype(jnp.int32)

    def compute(i, in_rows):
        in_rows = in_rows.reshape(-1, D)
        out = expert_rows(
            in_rows, cot_rows[i], w_gate_up, w_down, w_router, expert_at, n_ctx, 2
        )
        made.append([in_rows] + list(out))

    compute(0, plane)
    sent = gate(made[0][2], plane_next)
    back = ctx_trade(sent)
    fence(sent)

    compute(1, after(plane_next))
    back = gate(after(back), made[1][1])
    leaving = towards([1], back, spread[1]).astype(BF16)
    homes = [home(1, leaving)]
    sent = gate(made[1][1], back)
    back = ctx_trade(sent)
    fence(sent, leaving)

    mix_sent, route_grads = [], []

    def weigh(i):
        acts, gates = after(made[i][3], made[i][6])
        mix, route = expert_outs(acts, gates, cot_rows[i], w_down)
        mix_sent.append(mix.reshape(n_ctx, 2, capacity, D))
        route_grads.append(route)

    def grads_sent(lefts, rights, rows_out):
        sent = [weight_grad(lefts, rights, half_rows[m], rows_out) for m in range(1, n_dp)]
        return sent, [dp_shift(v, m + 1) for m, v in enumerate(sent)]

    half_rows = [(d + m) % n_dp for m in range(n_dp)]
    weigh(0)
    back = gate(after(back), mix_sent[0])
    leaving = towards([2], back, spread[2]).astype(BF16)
    homes.append(home(2, leaving))
    sent = gate(made[1][2], back)
    back = ctx_trade(sent)
    fence(sent, leaving)

    weigh(1)
    back = gate(after(back), mix_sent[1])
    leaving = towards([3], back, spread[3]).astype(BF16)
    homes.append(home(3, leaving))
    sent = gate(made[0][1], back)
    back = ctx_trade(sent)
    fence(sent, leaving)

    back = after(back)
    returned = towards([0], back, spread[0])
    sent = gate(mix_sent[1], back)
    mix_trade = ctx_trade(sent)
    fence(sent)
    homes = after(*homes)
    for v in after(*homes):
        returned = returned + v.astype(F32)

    router = softmax(dot(hidden_ffn, w_router))
    prob_grad = returned[:, D : D + experts] + returned[:, D + experts : D + 2 * experts]
    logit_grad = router * (prob_grad - jnp.sum(router * prob_grad, axis=-1, keepdims=True))
    ffn_grad = returned[:, :D] + jnp.dot(logit_grad, w_router.astype(F32).T, precision=HIGHEST_PREC)
    router_grad_t = jnp.einsum(
        "re,rd->ed", logit_grad, hidden_ffn.astype(F32), precision=HIGHEST_PREC
    )
    mid_norm_grad, ffn_gain_grad = norm_back(ffn_grad, normed_ffn, scale_ffn, gain_ffn)
    mid_grad = cot_own.astype(F32) + mid_norm_grad

    attn_grad = mid_grad.astype(BF16)
    grad_halves = jnp.zeros((n_dp, rows, half), BF16)
    for m in range(n_dp):
        grad_halves = place(
            grad_halves,
            dot_bt(attn_grad, out_halves[m].reshape(half, D)).astype(BF16),
            (d - m) % n_dp,
        )
    pieces = by_owner(jnp.concatenate([grad_halves[i] for i in range(n_dp)], axis=1))
    mixed_grad = in_order(trade_pieces([part_of(pieces, 0, c ^ k) for k in range(n_ctx)]))
    back = gate(mix_trade, mixed_grad)
    leaving = towards(pairs[1], back, spreads[1]).astype(BF16)
    mix_homes = [home(2, leaving[:rows]), home(3, leaving[rows:])]
    fence(mixed_grad, leaving)
    mixed_grad = after(mixed_grad)
    query_turn, key_turn, value_grad, head_gain_grads, sums = attend_back(
        mixed_grad.reshape(total_rows, width),
        kept,
        projected,
        scales,
        head_gains,
        cosine,
        sine_rows,
        hidden_pairs,
    )
    sums = jnp.stack([sums[:, 0], sums[:, HEAD_DIM]])
    means = ctx_sum(sums) / D
    attn_sent = gate(attn_grad, means)
    attn_grad_all = ctx_gather(attn_sent)
    fence(means, attn_sent)
    means = after(means)
    proj_grad = norms_back(
        query_turn, key_turn, value_grad, projected, scales, means.T, head_gains
    )

    sent = [
        weight_grad([hidden_in], [[proj_grad]], half_rows[m], half) for m in range(1, n_dp)
    ]
    arrived = [dp_shift(v, m + 1) for m, v in enumerate(sent)]
    fence(*sent)
    hidden_part = dot_bt(gate(proj_grad, *sent), w_qkv).astype(BF16)
    arrived = gate(tuple([after(v) for v in arrived]), hidden_part)
    qkv_dp = weight_grad([hidden_in], [[proj_grad]], half_rows[0], half, arrived)
    qkv_dp = qkv_dp.reshape(n_exp, n_ctx * shard, 3 * width)
    mix_homes = after(*mix_homes)
    qkv_dp = gate(qkv_dp, *mix_homes)
    sent = [part_of(qkv_dp, 0, (z + s) % n_exp).astype(BF16) for s in range(1, n_exp)]
    qkv_arrived = [exp_shift(v, s + 1) for s, v in enumerate(sent)]
    attn_grad_all = gate(attn_grad_all, *sent)
    hidden_part = gate(hidden_part, attn_grad_all)
    hidden_trade = ctx_trade(hidden_part.reshape(n_ctx, rows, D))
    attn_grad_all = attn_grad_all.reshape(total_rows, D)
    fence(hidden_part, *sent)

    in_rows, acts, gate_grads, up_grads = [after(*[v[i] for v in made]) for i in (0, 3, 4, 5)]
    gate_up_grads = [[gate_grads[i], up_grads[i]] for i in range(len(pairs))]
    out_rows = width // n_dp
    if head_groups == n_dp:
        out_left = [after(mixed_heads)]
        out_sent, out_arrived = grads_sent(out_left, [[attn_grad_all]], out_rows)
        acts = gate(tuple(acts), *out_sent)
    down_sent, down_arrived = grads_sent(acts, [[v] for v in route_grads], FF // n_dp)
    in_rows = gate(tuple(in_rows), *down_sent)
    if head_groups == n_dp:
        out_left = gate(tuple(out_left), *down_sent)
        out_dp = weight_grad(out_left, [[attn_grad_all]], half_rows[0], out_rows, out_arrived)
        out_dp = out_dp.reshape(n_exp, shard, D)
        in_rows = gate(tuple(in_rows), out_dp)
    gate_up_sent, gate_up_arrived = grads_sent(in_rows, gate_up_grads, D // n_dp)
    hidden_trade = gate(hidden_trade, *gate_up_sent)
    mix_back = ctx_trade(gate(mix_sent[0], hidden_trade))
    acts = gate(tuple(acts), *gate_up_sent)
    grad_down = weight_grad(acts, [[v] for v in route_grads], d, FF // n_dp, down_arrived)
    mix_back = gate(mix_back, grad_down)
    leaving = towards(pairs[0], mix_back, spreads[0])
    mix_homes = list(mix_homes) + [leaving[:rows], home(1, leaving[rows:].astype(BF16))]
    in_rows = gate(tuple(in_rows), leaving)
    grad_gate_up = weight_grad(in_rows, gate_up_grads, d, D // n_dp, gate_up_arrived)

    hidden_grad = from_exp(jnp.sum(hidden_trade.astype(F32), axis=0))
    scale_own = lax.dynamic_slice_in_dim(scale_in, c * rows, rows, axis=0)
    in_norm_grad, in_gain_grad = norm_back(hidden_grad, inputs * scale_own, scale_own, gain_in)
    input_grad = mid_grad + in_norm_grad

    def spread_features(v):
        shaped = jnp.zeros((head_groups, n_ctx, head_run), F32)
        return place(shaped, v.reshape(head_groups, 1, head_run), None, c).reshape(1, D)

    small_grad = jnp.concatenate(
        [
            router_grad_t,
            in_gain_grad[None],
            spread_features(head_gain_grads[0]),
            spread_features(head_gain_grads[1]),
            ffn_gain_grad[None],
        ],
        axis=0,
    )
    count = small_grad.shape[0]
    part = small_grad.reshape(count, n_dp, n_ctx, n_exp, shard).transpose(1, 2, 3, 0, 4)
    late_d = mark[0, 0].astype(jnp.int32)
    total = lax.dynamic_index_in_dim(part, late_d, 0, keepdims=False)
    for m in range(1, n_dp):
        total = total + dp_shift(
            lax.dynamic_index_in_dim(part, (late_d + m) % n_dp, 0, keepdims=False), m
        )
    part = total
    part = jnp.sum(ctx_trade(gate(part, mix_back)), axis=0)
    if head_groups == n_dp:
        flat = part.reshape(n_exp, count * shard)
        high = flat.astype(BF16)
        flat = jnp.concatenate([high, (flat - high.astype(F32)).astype(BF16)], axis=1)
        lines = -(-2 * count * shard // (8 * D)) * 8
        flat = jnp.pad(flat, ((0, 0), (0, lines * D - 2 * count * shard)))
        out_sent = jnp.concatenate([out_dp.astype(BF16), flat.reshape(n_exp, lines, D)], axis=1)
        out_trade = lax.all_to_all(out_sent, "exp", 0, 0, tiled=True)
        out_trade = gate(out_trade, grad_gate_up)
        grad_out = jnp.sum(out_trade[:, :shard].astype(F32), axis=0)
        flat = jnp.sum(out_trade[:, shard:].astype(F32), axis=0).reshape(-1)
        total = (flat[: count * shard] + flat[count * shard : 2 * count * shard]).reshape(
            count, shard
        )
    else:
        grad_out = lax.psum_scatter(
            dot_at(mixed, attn_grad), ("dp", "ctx", "exp"), scatter_dimension=0, tiled=True
        )
        total = jnp.sum(lax.all_to_all(part, "exp", 0, 0, tiled=True), axis=0)
    small_sum = total.T
    mix_homes = gate(tuple(mix_homes), grad_out)
    mixture = mix_homes[2] + sum(v.astype(F32) for v in mix_homes[:2] + mix_homes[3:])
    final_rows = (mid_rows + mixture).astype(BF16)

    qkv_arrived = gate(tuple(qkv_arrived), final_rows, small_sum)
    qkv_exp = part_of(qkv_dp, 0, z)
    for v in qkv_arrived:
        qkv_exp = qkv_exp + v.astype(F32)
    qkv_exp = qkv_exp.reshape(n_ctx, shard, 3 * width)
    grad_qkv = all_owners(ctx_trade(qkv_exp.astype(BF16)).astype(F32))

    return (
        final_rows[:prompt_len][None],
        final_rows[prompt_len:][None],
        input_grad[:prompt_len][None],
        input_grad[prompt_len:][None],
        grad_qkv,
        grad_out,
        small_sum[:, :experts],
        small_sum[:, experts:],
        grad_gate_up[None],
        grad_down[None],
    )


def solution(mesh):
    return jax.shard_map(
        body,
        mesh=mesh,
        in_specs=(
            P(("dp", "exp"), "ctx", None),
            P(("dp", "exp"), "ctx", None),
            P(("dp", "exp"), "ctx", None),
            P(("dp", "exp"), "ctx", None, None),
            P(("dp", "ctx", "exp"), None),
            P(("dp", "ctx", "exp"), None),
            P(("dp", "ctx", "exp"), None),
            P(("dp", "ctx", "exp"), None),
            P(("ctx", "exp"), None, None),
            P(("ctx", "exp"), None, None),
            P(("dp", "exp"), "ctx", None),
            P(("dp", "exp"), "ctx", None),
        ),
        out_specs=(
            P(("dp", "exp"), "ctx", None),
            P(("dp", "exp"), "ctx", None),
            P(("dp", "exp"), "ctx", None),
            P(("dp", "exp"), "ctx", None),
            P(("dp", "ctx", "exp"), None),
            P(("dp", "ctx", "exp"), None),
            P(("dp", "ctx", "exp"), None),
            P(("dp", "ctx", "exp"), None),
            P(("ctx", "exp"), "dp", None),
            P(("ctx", "exp"), "dp", None),
        ),
        check_vma=False,
    )
```

```python
import jax
import jax.numpy as jnp
from jax import lax
from jax.experimental import pallas as pl
from jax.experimental.pallas import tpu as pltpu
from jax.sharding import PartitionSpec as P

D = 2048
HEADS = 16
HEAD_DIM = 128
FF = 1024
TOP = 8

NORM_EPS = 1e-05
ROPE_BASE = 10000.0
NEGATIVE = -1e30
HIGHEST_PREC = lax.Precision.HIGHEST
F32 = jnp.float32
BF16 = jnp.bfloat16


def row_scale(values):
    return lax.rsqrt(jnp.mean(values * values, axis=-1, keepdims=True) + NORM_EPS)


def rope_tables(position, half_dim):
    inverse = ROPE_BASE ** (-jnp.arange(half_dim, dtype=F32) / half_dim)
    angles = position[:, None] * inverse[None, :]
    cosine, sine_rows = jnp.cos(angles), jnp.sin(angles)
    return (
        jnp.concatenate([cosine, cosine], axis=1),
        jnp.concatenate([-sine_rows, sine_rows], axis=1),
    )


def norm_back(grad_rows, normed, scale_rows, gain_col):
    grad_normed = grad_rows * gain_col
    grad_input = scale_rows * (
        grad_normed - normed * jnp.mean(grad_normed * normed, axis=-1, keepdims=True)
    )
    return (grad_input, jnp.sum(grad_rows * normed, axis=0))


def dot(a, b):
    return jnp.dot(a, b, preferred_element_type=F32)


def dot_bt(a, b):
    return lax.dot_general(a, b, (((1,), (1,)), ((), ())), preferred_element_type=F32)


def dot_at(a, b):
    return lax.dot_general(a, b, (((0,), (0,)), ((), ())), preferred_element_type=F32)


def attend(projected, scales, gains, cosine, sine_rows, hidden_pairs):
    rows = projected.shape[0]
    width = projected.shape[1] // 3
    heads = width // HEAD_DIM

    def kernel(pq, pk, pv, scale_ref, gain_ref, cos_ref, sin_ref, pair_ref, mixed, q, k, v, total):
        def turned(values):
            return values * cos_ref[...] + pltpu.roll(values, HEAD_DIM // 2, 1) * sin_ref[...]

        query = turned(pq[...] * scale_ref[:, :1] * gain_ref[:1, :]).astype(BF16)
        key = turned(pk[...] * scale_ref[:, 1:2] * gain_ref[1:2, :]).astype(BF16)
        value = pv[...].astype(BF16)
        scores = dot_bt(query, key) * HEAD_DIM ** (-0.5)
        scores = jnp.where(pair_ref[...] < 0.0, NEGATIVE, scores)
        row_max = jnp.max(scores, axis=-1, keepdims=True)
        log_total = row_max + jnp.log(
            jnp.sum(jnp.exp(scores - row_max), axis=-1, keepdims=True)
        )
        mixed[...] = dot(jnp.exp(scores - log_total).astype(BF16), value).astype(BF16)
        q[...], k[...], v[...] = query, key, value
        total[...] = jnp.broadcast_to(log_total, total.shape)

    def head(part):
        return pl.BlockSpec((rows, HEAD_DIM), lambda h: (0, part * heads + h))

    def whole(shape):
        return pl.BlockSpec(shape, lambda h: (0, 0))

    return pl.pallas_call(
        kernel,
        grid=(heads,),
        in_specs=[
            head(0),
            head(1),
            head(2),
            whole((rows, 2)),
            pl.BlockSpec((2, HEAD_DIM), lambda h: (0, h)),
            whole((rows, HEAD_DIM)),
            whole((rows, HEAD_DIM)),
            whole((rows, rows)),
        ],
        out_specs=[head(0)] * 5,
        out_shape=[jax.ShapeDtypeStruct((rows, width), BF16)] * 4
        + [jax.ShapeDtypeStruct((rows, width), F32)],
        compiler_params=pltpu.CompilerParams(vmem_limit_bytes=48 << 20),
        cost_estimate=pl.CostEstimate(flops=0, bytes_accessed=0, transcendentals=0),
        name="attend",
    )(projected, projected, projected, scales, gains, cosine, sine_rows, hidden_pairs)


def attend_back(grads, kept, projected, scales, gains, cosine, sine_rows, hidden_pairs):
    query_b, key_b, value_b, log_total = kept
    rows = projected.shape[0]
    width = projected.shape[1] // 3
    heads = width // HEAD_DIM
    scale = HEAD_DIM ** (-0.5)

    def kernel(
        g, q, k, v, total, pq, pk, scale_ref, gain_ref, cos_ref, sin_ref, pair_ref,
        query_out, key_out, value_out, gain_out, sum_out,
    ):
        def turned_back(values):
            return values * cos_ref[...] - pltpu.roll(values, HEAD_DIM // 2, 1) * sin_ref[...]

        scores = dot_bt(q[...], k[...]) * scale
        scores = jnp.where(pair_ref[...] < 0.0, NEGATIVE, scores)
        attention = jnp.exp(scores - total[:, :1])
        prob_att = dot_bt(g[...], v[...])
        delta = jnp.sum(attention * prob_att, axis=-1, keepdims=True)
        score_grad = (attention * (prob_att - delta)).astype(BF16)
        query = turned_back(dot(score_grad, k[...]) * scale)
        key = turned_back(dot_at(score_grad, q[...]) * scale)
        value_out[...] = dot_at(attention.astype(BF16), g[...]).astype(BF16)
        query_out[...], key_out[...] = query, key
        query_n = query * (pq[...] * scale_ref[:, :1])
        key_n = key * (pk[...] * scale_ref[:, 1:2])
        gain_out[:1, :] = jnp.sum(query_n, axis=0, keepdims=True)
        gain_out[1:2, :] = jnp.sum(key_n, axis=0, keepdims=True)
        query_sum = jnp.sum(query_n * gain_ref[:1, :], axis=-1, keepdims=True)
        key_sum = jnp.sum(key_n * gain_ref[1:2, :], axis=-1, keepdims=True)
        sums = jnp.concatenate(
            [
                jnp.broadcast_to(query_sum, (rows, HEAD_DIM)),
                jnp.broadcast_to(key_sum, (rows, HEAD_DIM)),
            ],
            axis=1,
        )

        @pl.when(pl.program_id(0) == 0)
        def _():
            sum_out[...] = sums

        @pl.when(pl.program_id(0) > 0)
        def _():
            sum_out[...] += sums

    def head(part):
        return pl.BlockSpec((rows, HEAD_DIM), lambda h: (0, part * heads + h))

    def whole(shape):
        return pl.BlockSpec(shape, lambda h: (0, 0))

    pair = pl.BlockSpec((2, HEAD_DIM), lambda h: (0, h))
    return pl.pallas_call(
        kernel,
        grid=(heads,),
        in_specs=[head(0)] * 5
        + [
            head(0),
            head(1),
            whole((rows, 2)),
            pair,
            whole((rows, HEAD_DIM)),
            whole((rows, HEAD_DIM)),
            whole((rows, rows)),
        ],
        out_specs=[head(0)] * 3 + [pair, whole((rows, 2 * HEAD_DIM))],
        out_shape=[
            jax.ShapeDtypeStruct((rows, width), F32),
            jax.ShapeDtypeStruct((rows, width), F32),
            jax.ShapeDtypeStruct((rows, width), BF16),
            jax.ShapeDtypeStruct((2, width), F32),
            jax.ShapeDtypeStruct((rows, 2 * HEAD_DIM), F32),
        ],
        compiler_params=pltpu.CompilerParams(vmem_limit_bytes=48 << 20),
        cost_estimate=pl.CostEstimate(flops=0, bytes_accessed=0, transcendentals=0),
        name="attend_back",
    )(
        grads, query_b, key_b, value_b, log_total, projected, projected, scales, gains,
        cosine, sine_rows, hidden_pairs,
    )


def norms_back(query_turn, key_turn, value_grad, projected, scales, means, gains):
    rows, width = query_turn.shape

    def kernel(query, key, value, projected_ref, scale_ref, mean_ref, gain_ref, out):
        for i, turn in enumerate((query, key)):
            at = slice(i * width, (i + 1) * width)
            scale = scale_ref[:, i : i + 1]
            normed = projected_ref[:, at] * scale
            out[:, at] = (
                scale * (turn[...] * gain_ref[i : i + 1, :] - normed * mean_ref[:, i : i + 1])
            ).astype(BF16)
        out[:, 2 * width :] = value[...]

    return pl.pallas_call(
        kernel,
        out_shape=jax.ShapeDtypeStruct((rows, 3 * width), BF16),
        compiler_params=pltpu.CompilerParams(vmem_limit_bytes=48 << 20),
        cost_estimate=pl.CostEstimate(flops=0, bytes_accessed=0, transcendentals=0),
        name="norms_back",
    )(query_turn, key_turn, value_grad, projected, scales, means, gains)


def expert_rows(rows, cot, w_gate_up, w_down, w_router, expert, senders, blocks):
    count, experts = rows.shape[0], w_router.shape[1]
    tile = FF // 2
    steps = FF // tile
    extra = -(-2 * experts // 128) * 128
    piece = count // (senders * blocks)

    def kernel(expert_ref, rows_ref, cot_ref, wg_ref, wu_ref, wd_ref, wr_ref, *refs):
        row_refs = refs[:blocks]
        act_ref, gg_ref, ug_ref, gate_ref, row_sum, gate_grad = refs[blocks:]
        step = pl.program_id(0)
        row_block = rows_ref[...]

        @pl.when(step == 0)
        def _():
            logits = dot(row_block, wr_ref[...])
            shifted = jnp.exp(logits - jnp.max(logits, axis=-1, keepdims=True))
            router = shifted / jnp.sum(shifted, axis=-1, keepdims=True)
            lane = lax.broadcasted_iota(jnp.int32, router.shape, 1)
            own = jnp.sum(jnp.where(lane == expert_ref[0], router, 0.0), axis=-1, keepdims=True)
            gate_ref[...] = jnp.broadcast_to(own, gate_ref.shape)

        gate = gate_ref[:, :1]
        gate_part = dot(row_block, wg_ref[...])
        up_part = dot(row_block, wu_ref[...])
        cot_act = dot_bt(cot_ref[...], wd_ref[...])
        sigmoid_gate = jax.nn.sigmoid(gate_part)
        swish = gate_part * sigmoid_gate
        activated = (swish * up_part).astype(BF16)
        act_grad = gate * cot_act
        gate_part_grad = (
            act_grad * up_part * sigmoid_gate * (1.0 + gate_part * (1.0 - sigmoid_gate))
        ).astype(BF16)
        up_part_grad = (act_grad * swish).astype(BF16)
        act_ref[...] = activated
        gg_ref[...] = gate_part_grad
        ug_ref[...] = up_part_grad
        row_part = dot_bt(gate_part_grad, wg_ref[...]) + dot_bt(up_part_grad, wu_ref[...])
        part = jnp.sum(cot_act * activated.astype(F32), axis=-1, keepdims=True)
        part = jnp.broadcast_to(part, gate_grad.shape)

        @pl.when(step == 0)
        def _():
            row_sum[...] = row_part
            gate_grad[...] = part

        @pl.when(step > 0)
        def _():
            row_sum[...] += row_part
            gate_grad[...] += part

        @pl.when(step == steps - 1)
        def _():
            lane = lax.broadcasted_iota(jnp.int32, (piece, extra), 1)
            for j in range(senders):
                for i in range(blocks):
                    at = pl.ds((j * blocks + i) * piece, piece)
                    row_refs[i][j, :, :D] = row_sum[at, :].astype(BF16)
                    both = jnp.broadcast_to(gate_grad[at, :1], (piece, extra))
                    high = both.astype(BF16).astype(F32)
                    row_refs[i][j, :, D:] = jnp.where(
                        lane == expert_ref[0],
                        high,
                        jnp.where(lane == experts + expert_ref[0], both - high, 0.0),
                    ).astype(BF16)

    def whole(shape):
        return pl.BlockSpec(shape, lambda j, at: (0, 0))

    columns = pl.BlockSpec((count, tile), lambda j, at: (0, j))
    return pl.pallas_call(
        kernel,
        grid_spec=pltpu.PrefetchScalarGridSpec(
            num_scalar_prefetch=1,
            grid=(steps,),
            in_specs=[
                whole((count, D)),
                whole((count, D)),
                pl.BlockSpec((D, tile), lambda j, at: (0, j)),
                pl.BlockSpec((D, tile), lambda j, at: (0, steps + j)),
                pl.BlockSpec((tile, D), lambda j, at: (j, 0)),
                whole((D, experts)),
            ],
            out_specs=[pl.BlockSpec((senders, piece, D + extra), lambda j, at: (0, 0, 0))] * blocks
            + [columns, columns, columns, whole((count, 128))],
            scratch_shapes=[pltpu.VMEM((count, D), F32), pltpu.VMEM((count, 128), F32)],
        ),
        out_shape=[jax.ShapeDtypeStruct((senders, piece, D + extra), BF16)] * blocks
        + [
            jax.ShapeDtypeStruct((count, FF), BF16),
            jax.ShapeDtypeStruct((count, FF), BF16),
            jax.ShapeDtypeStruct((count, FF), BF16),
            jax.ShapeDtypeStruct((count, 128), F32),
        ],
        compiler_params=pltpu.CompilerParams(vmem_limit_bytes=56 << 20),
        cost_estimate=pl.CostEstimate(flops=0, bytes_accessed=0, transcendentals=0),
        name="expert",
    )(expert, rows, cot, w_gate_up, w_gate_up, w_down, w_router)


def expert_outs(acts, gates, cot, w_down):
    count = acts.shape[0]
    tile = count // 2

    def kernel(act_ref, gate_ref, cot_ref, wd_ref, mix_ref, route_ref):
        gate = gate_ref[:, :1]
        out = dot(act_ref[...], wd_ref[...]).astype(BF16)
        mix_ref[...] = (gate * out.astype(F32)).astype(BF16)
        route_ref[...] = (gate * cot_ref[...].astype(F32)).astype(BF16)

    def rows_of(columns):
        return pl.BlockSpec((tile, columns), lambda i: (i, 0))

    return pl.pallas_call(
        kernel,
        grid=(count // tile,),
        in_specs=[rows_of(FF), rows_of(128), rows_of(D), pl.BlockSpec((FF, D), lambda i: (0, 0))],
        out_specs=[rows_of(D), rows_of(D)],
        out_shape=[jax.ShapeDtypeStruct((count, D), BF16)] * 2,
        compiler_params=pltpu.CompilerParams(vmem_limit_bytes=56 << 20),
        cost_estimate=pl.CostEstimate(
            flops=2 * count * FF * D, bytes_accessed=6 * count * D + 2 * FF * D, transcendentals=0
        ),
        name="expert_outs",
    )(acts, gates, cot, w_down)


def weight_grad(lefts, rights, part, rows_out, arrived=()):
    blocks, parts = len(lefts), len(rights[0])
    depth = lefts[0].shape[0]
    tile = min(256, rows_out)
    tiles = rows_out // tile
    widths = [v.shape[1] for v in rights[0]]

    def kernel(part_ref, *refs):
        left, right, out = refs[:blocks], refs[blocks : blocks * (1 + parts)], refs[-1]
        at = 0
        for p in range(parts):
            total = dot_at(left[0][...], right[p][...])
            for b in range(1, blocks):
                total = total + dot_at(left[b][...], right[b * parts + p][...])
            for more in refs[blocks * (1 + parts) : -1]:
                total = total + more[:, at : at + widths[p]].astype(F32)
            out[:, at : at + widths[p]] = total.astype(out.dtype)
            at += widths[p]

    row_block = pl.BlockSpec((tile, sum(widths)), lambda i, at: (i, 0))
    return pl.pallas_call(
        kernel,
        grid_spec=pltpu.PrefetchScalarGridSpec(
            num_scalar_prefetch=1,
            grid=(tiles,),
            in_specs=[pl.BlockSpec((depth, tile), lambda i, at: (0, at[0] * tiles + i))] * blocks
            + [
                pl.BlockSpec((depth, w), lambda i, at: (0, 0))
                for _ in range(blocks)
                for w in widths
            ]
            + [row_block] * len(arrived),
            out_specs=row_block,
        ),
        out_shape=jax.ShapeDtypeStruct((rows_out, sum(widths)), F32 if arrived else BF16),
        compiler_params=pltpu.CompilerParams(vmem_limit_bytes=56 << 20),
        cost_estimate=pl.CostEstimate(
            flops=4 * blocks * depth * rows_out * sum(widths),
            bytes_accessed=2 * blocks * depth * (rows_out + sum(widths)) + 4 * rows_out * sum(widths),
            transcendentals=0,
        ),
        name="weight_grad",
    )(part.reshape(1).astype(jnp.int32), *lefts, *[v for r in rights for v in r], *arrived)


def body(
    prompt_x,
    cont_x,
    cont_ids,
    routes,
    qkv_weight,
    out_weight,
    router_weight,
    norm_gains,
    gate_up_weight,
    down_weight,
    prompt_cot,
    cont_cot,
):
    n_dp, n_ctx, n_exp = lax.axis_size("dp"), lax.axis_size("ctx"), lax.axis_size("exp")
    d, c, z = lax.axis_index("dp"), lax.axis_index("ctx"), lax.axis_index("exp")
    prompt_len = prompt_x.shape[1]
    cont_len = cont_x.shape[1]
    rows = prompt_len + cont_len
    prompt_total = prompt_len * n_ctx
    experts = router_weight.shape[1]
    capacity = rows * TOP * 17 // (16 * experts)
    score_scale = HEAD_DIM ** (-0.5)
    shard = qkv_weight.shape[0]
    heads_own = HEADS // n_ctx
    width = heads_own * HEAD_DIM
    head_groups = n_dp if (D // (n_dp * n_ctx)) % HEAD_DIM == 0 else 1
    head_run = D // (head_groups * n_ctx)
    own_expert = c * n_exp + z

    def ctx_swap(x, k):
        return lax.ppermute(x, "ctx", [(i, i ^ k) for i in range(n_ctx)])

    def ctx_trade(x):
        return lax.all_to_all(x, "ctx", 0, 0, tiled=True)

    def ctx_gather(x):
        return ctx_trade(jnp.broadcast_to(x[None], (n_ctx,) + x.shape))

    def exp_shift(x, s):
        return lax.ppermute(x, "exp", [(i, (i + s) % n_exp) for i in range(n_exp)])

    def dp_shift(x, m):
        return lax.ppermute(x, "dp", [(i, (i + m) % n_dp) for i in range(n_dp)])

    def part_of(x, axis, at):
        return lax.dynamic_index_in_dim(x, at, axis, keepdims=False)

    def place(buffer, x, *index):
        start, shape = [], []
        for at, size in zip(index, buffer.shape):
            start.append(0 if at is None else at)
            shape.append(size if at is None else 1)
        shape += buffer.shape[len(index) :]
        start += [0] * (buffer.ndim - len(index))
        return lax.dynamic_update_slice(buffer, x.reshape(shape), start)

    def gate(x, *others):
        out = lax.optimization_barrier((x,) + others)[0]
        return list(out) if isinstance(out, tuple) else out

    mark = jnp.full((8, 128), d, jnp.int32).astype(F32)

    def hand_on(in_ref, out_ref):
        out_ref[...] = in_ref[...]

    def fence(*values):
        nonlocal mark
        mark = pl.pallas_call(
            hand_on,
            out_shape=jax.ShapeDtypeStruct(mark.shape, mark.dtype),
            cost_estimate=pl.CostEstimate(
                flops=2 * 10**11, bytes_accessed=0, transcendentals=0
            ),
            name="fence",
        )(gate(mark, *values))

    def after(*values):
        out = lax.optimization_barrier(values + (mark,))
        return out[0] if len(values) == 1 else out[:-1]

    def by_owner(v):
        runs = v.shape[1] // (n_ctx * head_run)
        return jnp.stack(
            [
                jnp.concatenate(
                    [
                        v[:, (i * n_ctx + j) * head_run : (i * n_ctx + j + 1) * head_run]
                        for i in range(runs)
                    ],
                    axis=1,
                )
                for j in range(n_ctx)
            ]
        )

    def all_owners(v):
        runs = v.shape[2] // head_run
        return jnp.concatenate(
            [
                v[j][:, i * head_run : (i + 1) * head_run]
                for i in range(runs)
                for j in range(n_ctx)
            ],
            axis=1,
        )

    x_own = jnp.concatenate([prompt_x[0], cont_x[0]], axis=0)
    cot_own = jnp.concatenate([prompt_cot[0], cont_cot[0]], axis=0)

    small_width = experts + norm_gains.shape[1]
    route_width = -(-rows * TOP // shard)
    route_cols = routes[0, 0].T.astype(BF16).reshape(-1)
    route_cols = jnp.pad(route_cols, (0, route_width * shard - rows * TOP)).reshape(shard, -1)
    extra = jnp.concatenate(
        [
            router_weight,
            norm_gains,
            jnp.broadcast_to(cont_ids[0].astype(BF16), (shard, cont_len)),
            route_cols,
        ],
        axis=1,
    )
    extra_width = -(-extra.shape[1] // 128) * 128
    extra = jnp.pad(extra, ((0, 0), (0, extra_width - extra.shape[1])))
    all_width = 3 * width + extra_width
    runs = 3 * width // head_run


    def pack(w_ref, extra_ref, out_ref):
        for j in range(n_ctx):
            for i in range(runs):
                out_ref[j, :, i * head_run : (i + 1) * head_run] = w_ref[
                    :, (i * n_ctx + j) * head_run : (i * n_ctx + j + 1) * head_run
                ]
            out_ref[j, :, 3 * width :] = extra_ref[...]

    packed_w = pl.pallas_call(
        pack, out_shape=jax.ShapeDtypeStruct((n_ctx, shard, all_width), BF16), name="pack"
    )(qkv_weight, extra)
    slab = ctx_trade(packed_w)
    out_blocks = [out_weight] + [exp_shift(out_weight, s) for s in range(1, n_exp)]
    fence(packed_w)

    def by_exp(v):
        shaped = v.reshape(v.shape[:-1] + (n_dp, n_ctx, n_exp, shard))
        return jnp.swapaxes(shaped, -3, -2).reshape(v.shape)

    def from_exp(v):
        shaped = v.reshape(v.shape[:-1] + (n_dp, n_exp, n_ctx, shard))
        return jnp.swapaxes(shaped, -3, -2).reshape(v.shape)

    x_turned = by_exp(x_own)
    out_blocks = after(*out_blocks)
    out_exp = jnp.zeros((n_exp, shard, D), BF16)
    for j in range(n_exp):
        out_exp = place(out_exp, out_blocks[j], (z - j) % n_exp)

    slab = after(slab)
    ids_at = 3 * width + small_width
    ids = slab[:, 0, ids_at : ids_at + cont_len].astype(F32).astype(jnp.int32)
    w_blocks = [slab] + [exp_shift(slab, s) for s in range(1, n_exp)]
    w_sets = [[dp_shift(slab, m)] for m in range(1, n_dp)]
    out_ctx = ctx_gather(gate(out_exp, slab))
    fence(slab, out_exp)
    out_ctx = after(out_ctx)
    x_sent = gate(x_turned, out_ctx)
    x_all = ctx_gather(x_sent)
    fence(x_sent)

    x_all = after(x_all).reshape(n_ctx * rows, D).astype(F32)
    scale_in = row_scale(x_all)
    w_blocks = gate(tuple(w_blocks), scale_in)
    for m in range(1, n_dp):
        w_sets[m - 1] += [dp_shift(v, m) for v in w_blocks[1:]]
    cot_blocks = [cot_own]
    routes_at = ids_at + cont_len
    places = jnp.stack(
        [(d - m) % n_dp for m in range(n_dp)] + [(z - s) % n_exp for s in range(n_exp)]
    ).astype(jnp.int32)

    def assemble(at_ref, *refs):
        blocks, (w_ref, small_ref) = refs[: n_dp * n_exp], refs[n_dp * n_exp :]
        for m in range(n_dp):
            for s in range(n_exp):
                block = blocks[m * n_exp + s]
                w_ref[at_ref[m], at_ref[n_dp + s]] = block[:, :, : 3 * width]
                small_ref[at_ref[m], at_ref[n_dp + s]] = block[:, :, 3 * width :]

    in_vmem = pl.BlockSpec(memory_space=pltpu.VMEM)
    w_qkv, w_small = pl.pallas_call(
        assemble,
        in_specs=[pl.BlockSpec(memory_space=pltpu.SMEM)] + [in_vmem] * (n_dp * n_exp),
        out_specs=[in_vmem] * 2,
        out_shape=[
            jax.ShapeDtypeStruct((n_dp, n_exp, n_ctx, shard, 3 * width), BF16),
            jax.ShapeDtypeStruct((n_dp, n_exp, n_ctx, shard, extra_width), BF16),
        ],
        compiler_params=pltpu.CompilerParams(vmem_limit_bytes=56 << 20),
        cost_estimate=pl.CostEstimate(flops=0, bytes_accessed=0, transcendentals=0),
        name="assemble",
    )(places, *w_blocks, *[v for w_set in w_sets for v in w_set])
    w_qkv = w_qkv.reshape(D, 3 * width)
    w_small = jnp.swapaxes(w_small, 1, 2).reshape(D, extra_width)
    w_router = w_small[:, :experts]
    gains_t = w_small[:, experts:small_width].astype(F32).T
    gain_in, gain_ffn = gains_t[0], gains_t[3]

    def own_features(v):
        shaped = v.reshape(v.shape[:-1] + (head_groups, n_ctx, head_run))
        return part_of(shaped, v.ndim, c).reshape(v.shape[:-1] + (width,))

    gain_query, gain_key = own_features(gains_t[1]), own_features(gains_t[2])

    upper = (
        jnp.arange(rows, dtype=jnp.int32)[:, None] < jnp.arange(rows, dtype=jnp.int32)[None, :]
    ).astype(BF16)
    send_experts = (jnp.arange(n_ctx) * n_exp + z).astype(F32)

    def spread_of(route_cols):
        named = jnp.any(
            route_cols.astype(F32)[None] == send_experts[:, None, None], axis=1
        )
        rank = dot(named.astype(BF16), upper)
        slots = jnp.where(named, rank, -1.0)
        return (
            (slots[:, None, :] == jnp.arange(capacity, dtype=F32)[None, :, None])
            .astype(BF16)
            .reshape(n_ctx * capacity, rows)
        )

    spread = [spread_of(routes[0, 0].T)]

    def spread_pair(blocks):
        n = len(blocks)
        parts = []
        for i, s in enumerate(blocks):
            part = spread[s].reshape(n_ctx, 1, capacity, rows)
            parts.append(jnp.pad(part, ((0, 0), (0, 0), (0, 0), (i * rows, (n - 1 - i) * rows))))
        return jnp.concatenate(parts, axis=1).reshape(n_ctx * n * capacity, n * rows)

    def pack_of(spread_rows, blocks):
        n = len(blocks)
        sent = dot(spread_rows, blocks[0] if n == 1 else jnp.concatenate(blocks, axis=0))
        return sent.astype(BF16).reshape(n_ctx, n, capacity, -1)

    def pack_cot(blocks):
        return pack_of(
            spread_pair(blocks) if len(blocks) > 1 else spread[blocks[0]],
            [cot_blocks[s] for s in blocks],
        )

    def trade_pieces(pieces):
        return [ctx_swap(pieces[k], k) if k else pieces[k] for k in range(n_ctx)]

    def in_order(pieces):
        whole = jnp.zeros((n_ctx,) + pieces[0].shape, pieces[0].dtype)
        for k in range(n_ctx):
            whole = place(whole, pieces[k], c ^ k)
        return whole

    w_gate_up = gate_up_weight[0]
    w_down = down_weight[0]
    pairs = [list(range(i, i + 2)) for i in range(0, n_exp, 2)]

    total_rows = rows * n_ctx
    index = jnp.arange(rows, dtype=jnp.int32)
    in_prompt = index < prompt_len
    position, seg_rows, order = [], [], []
    for j in range(n_ctx):
        seg = ids[j]
        starts = jnp.sum((seg[None, :] < seg[:, None]).astype(jnp.int32), axis=1)
        within = jnp.arange(cont_len, dtype=jnp.int32) - starts
        at = j * prompt_len
        position.append(jnp.concatenate([at + index[:prompt_len], prompt_total + within]))
        order.append(jnp.where(in_prompt, at + index, index))
        seg_rows.append(
            jnp.concatenate([jnp.full((prompt_len,), -1, jnp.int32), j * 64 + seg])
        )
    position = jnp.concatenate(position).astype(F32)
    order = jnp.concatenate(order)
    seg_of = jnp.concatenate(seg_rows)
    is_prompt = jnp.concatenate([in_prompt] * n_ctx)
    before = order[None, :] <= order[:, None]
    allowed = jnp.where(
        is_prompt[:, None],
        is_prompt[None, :] & before,
        is_prompt[None, :] | ((seg_of[None, :] == seg_of[:, None]) & before),
    )
    hidden_pairs = jnp.where(allowed, 0.0, -1.0)
    cosine, sine_rows = rope_tables(position, HEAD_DIM // 2)

    cot_sent = gate(pack_cot([0]), scale_in)
    cot_trade = ctx_trade(cot_sent)
    fence(cot_sent, w_qkv)
    hidden_in = after((x_all * after(scale_in) * by_exp(gain_in)).astype(BF16))
    projected = dot(hidden_in, w_qkv)

    def ctx_sum(total):
        k = 1
        while k < n_ctx:
            total = total + ctx_swap(total, k)
            k *= 2
        return total

    raw_query, raw_key = projected[:, :width], projected[:, width : 2 * width]
    squares = jnp.stack([jnp.sum(raw_query * raw_query, axis=-1), jnp.sum(raw_key * raw_key, axis=-1)])
    cot_flight = [exp_shift(gate(cot_blocks[0], squares), s) for s in range(1, n_exp)]
    scales = lax.rsqrt(ctx_sum(squares) / D + NORM_EPS)
    spread += [
        spread_of(
            part_of(v[..., routes_at : routes_at + route_width], 0, c)
            .reshape(-1)[: rows * TOP]
            .reshape(TOP, rows)
        )
        for v in gate(tuple(w_blocks[1:]), squares)
    ]
    out_ctx = gate(out_ctx, scales)
    out_halves = [out_ctx] + [dp_shift(out_ctx, m) for m in range(1, n_dp)]
    fence(scales, out_ctx)
    scales = after(scales)
    scales = scales.T
    head_gains = jnp.stack([gain_query, gain_key])
    mixed_heads, *kept = attend(projected, scales, head_gains, cosine, sine_rows, hidden_pairs)

    mixed_heads = gate(mixed_heads, cot_trade)
    mixed = ctx_trade(mixed_heads.reshape(n_ctx, rows, width))
    cot_own_rows = cot_trade
    spreads = [spread_pair(pair) for pair in pairs]
    fence(mixed_heads, *spreads)
    mixed = after(mixed)
    cot_blocks += gate(tuple(cot_flight), mixed)
    mixed = all_owners(mixed)
    cot_sent = gate(pack_cot(list(range(1, n_exp))), mixed)
    cot_trade = ctx_trade(cot_sent)
    fence(mixed, cot_sent)
    mixed = after(mixed)
    half = D // n_dp
    mixed_halves = jnp.stack([mixed[:, i * half : (i + 1) * half] for i in range(n_dp)])
    inputs = x_own.astype(F32)
    mid_rows = inputs
    for m in range(n_dp):
        mid_rows = mid_rows + dot(
            part_of(mixed_halves, 0, (d - m) % n_dp), out_halves[m].reshape(half, D)
        )
    scale_ffn = row_scale(mid_rows)
    normed_ffn = mid_rows * scale_ffn
    hidden_ffn = (normed_ffn * gain_ffn).astype(BF16)

    def softmax(logits):
        shifted = jnp.exp(logits - jnp.max(logits, axis=-1, keepdims=True))
        return shifted / jnp.sum(shifted, axis=-1, keepdims=True)

    cot_rows, made = [], []

    def towards(blocks, back, spread_rows):
        return dot_at(spread_rows, back.reshape(spread_rows.shape[0], -1))

    def home(s, summed):
        return exp_shift(summed, n_exp - s)

    near = exp_shift(hidden_ffn, 1)
    fence(hidden_ffn)

    near = after(near)
    far = [exp_shift(gate(hidden_ffn, near), s) for s in range(2, n_exp)]
    cot_trade = after(cot_trade)
    sent = gate(pack_of(spreads[0], [hidden_ffn, near]), cot_trade)
    plane = ctx_trade(sent)
    fence(near, sent)

    cot_back = [cot_own_rows[:, 0]] + [after(cot_trade)[:, s] for s in range(n_exp - 1)]
    for pair in pairs:
        cot_rows.append(jnp.stack([cot_back[s] for s in pair], axis=1).reshape(-1, D))
    plane = after(plane)
    far = gate(tuple(after(*far)), plane)
    sent = pack_of(spreads[1], far)
    plane_next = ctx_trade(sent)
    fence(sent, plane)

    expert_at = own_expert.reshape(1).astype(jnp.int32)

    def compute(i, in_rows):
        in_rows = in_rows.reshape(-1, D)
        out = expert_rows(
            in_rows, cot_rows[i], w_gate_up, w_down, w_router, expert_at, n_ctx, 2
        )
        made.append([in_rows] + list(out))

    compute(0, plane)
    sent = gate(made[0][2], plane_next)
    back = ctx_trade(sent)
    fence(sent)

    compute(1, after(plane_next))
    back = gate(after(back), made[1][1])
    leaving = towards([1], back, spread[1]).astype(BF16)
    homes = [home(1, leaving)]
    sent = gate(made[1][1], back)
    back = ctx_trade(sent)
    fence(sent, leaving)

    mix_sent, route_grads = [], []

    def weigh(i):
        acts, gates = after(made[i][3], made[i][6])
        mix, route = expert_outs(acts, gates, cot_rows[i], w_down)
        mix_sent.append(mix.reshape(n_ctx, 2, capacity, D))
        route_grads.append(route)

    def grads_sent(lefts, rights, rows_out):
        sent = [weight_grad(lefts, rights, half_rows[m], rows_out) for m in range(1, n_dp)]
        return sent, [dp_shift(v, m + 1) for m, v in enumerate(sent)]

    half_rows = [(d + m) % n_dp for m in range(n_dp)]
    weigh(0)
    back = gate(after(back), mix_sent[0])
    leaving = towards([2], back, spread[2]).astype(BF16)
    homes.append(home(2, leaving))
    sent = gate(made[1][2], back)
    back = ctx_trade(sent)
    fence(sent, leaving)

    weigh(1)
    back = gate(after(back), mix_sent[1])
    leaving = towards([3], back, spread[3]).astype(BF16)
    homes.append(home(3, leaving))
    sent = gate(made[0][1], back)
    back = ctx_trade(sent)
    fence(sent, leaving)

    back = after(back)
    returned = towards([0], back, spread[0])
    fence(returned)
    homes = after(*homes)
    for v in after(*homes):
        returned = returned + v.astype(F32)

    router = softmax(dot(hidden_ffn, w_router))
    prob_grad = returned[:, D : D + experts] + returned[:, D + experts : D + 2 * experts]
    logit_grad = router * (prob_grad - jnp.sum(router * prob_grad, axis=-1, keepdims=True))
    ffn_grad = returned[:, :D] + jnp.dot(logit_grad, w_router.astype(F32).T, precision=HIGHEST_PREC)
    router_grad_t = jnp.einsum(
        "re,rd->ed", logit_grad, hidden_ffn.astype(F32), precision=HIGHEST_PREC
    )
    mid_norm_grad, ffn_gain_grad = norm_back(ffn_grad, normed_ffn, scale_ffn, gain_ffn)
    mid_grad = cot_own.astype(F32) + mid_norm_grad

    attn_grad = mid_grad.astype(BF16)
    grad_halves = jnp.zeros((n_dp, rows, half), BF16)
    for m in range(n_dp):
        grad_halves = place(
            grad_halves,
            dot_bt(attn_grad, out_halves[m].reshape(half, D)).astype(BF16),
            (d - m) % n_dp,
        )
    pieces = by_owner(jnp.concatenate([grad_halves[i] for i in range(n_dp)], axis=1))
    mixed_grad = in_order(trade_pieces([part_of(pieces, 0, c ^ k) for k in range(n_ctx)]))
    sent = gate(mix_sent[1], mixed_grad)
    mix_trade = ctx_trade(sent)
    fence(mixed_grad, sent)
    mixed_grad = after(mixed_grad)
    query_turn, key_turn, value_grad, head_gain_grads, sums = attend_back(
        mixed_grad.reshape(total_rows, width),
        kept,
        projected,
        scales,
        head_gains,
        cosine,
        sine_rows,
        hidden_pairs,
    )
    sums = jnp.stack([sums[:, 0], sums[:, HEAD_DIM]])
    means = ctx_sum(sums) / D
    back = gate(mix_trade, means)
    leaving = towards(pairs[1], back, spreads[1]).astype(BF16)
    mix_homes = [home(2, leaving[:rows]), home(3, leaving[rows:])]
    attn_sent = gate(attn_grad, back)
    attn_grad_all = ctx_gather(attn_sent)
    fence(means, attn_sent, leaving)
    means = after(means)
    proj_grad = norms_back(
        query_turn, key_turn, value_grad, projected, scales, means.T, head_gains
    )

    sent = [
        weight_grad([hidden_in], [[proj_grad]], half_rows[m], half) for m in range(1, n_dp)
    ]
    arrived = [dp_shift(v, m + 1) for m, v in enumerate(sent)]
    fence(*sent)
    hidden_part = dot_bt(gate(proj_grad, *sent), w_qkv).astype(BF16)
    arrived = gate(tuple([after(v) for v in arrived]), hidden_part)
    qkv_dp = weight_grad([hidden_in], [[proj_grad]], half_rows[0], half, arrived)
    qkv_dp = qkv_dp.reshape(n_exp, n_ctx * shard, 3 * width)
    sent = [part_of(qkv_dp, 0, (z + s) % n_exp).astype(BF16) for s in range(1, n_exp)]
    qkv_arrived = [exp_shift(v, s + 1) for s, v in enumerate(sent)]
    attn_grad_all = gate(attn_grad_all, *sent)
    hidden_part = gate(hidden_part, attn_grad_all)
    hidden_trade = ctx_trade(hidden_part.reshape(n_ctx, rows, D))
    attn_grad_all = attn_grad_all.reshape(total_rows, D)
    fence(hidden_part, *sent)

    mix_homes = after(*mix_homes)
    in_rows, acts, gate_grads, up_grads = [after(*[v[i] for v in made]) for i in (0, 3, 4, 5)]
    acts = gate(tuple(acts), *mix_homes)
    gate_up_grads = [[gate_grads[i], up_grads[i]] for i in range(len(pairs))]
    out_rows = width // n_dp
    if head_groups == n_dp:
        out_left = [gate(after(mixed_heads), *mix_homes)]
        out_sent, out_arrived = grads_sent(out_left, [[attn_grad_all]], out_rows)
        acts = gate(tuple(acts), *out_sent)
    down_sent, down_arrived = grads_sent(acts, [[v] for v in route_grads], FF // n_dp)
    in_rows = gate(tuple(in_rows), *down_sent)
    if head_groups == n_dp:
        out_left = gate(tuple(out_left), *down_sent)
        out_dp = weight_grad(out_left, [[attn_grad_all]], half_rows[0], out_rows, out_arrived)
        out_dp = out_dp.reshape(n_exp, shard, D)
        in_rows = gate(tuple(in_rows), out_dp)
    gate_up_sent, gate_up_arrived = grads_sent(in_rows, gate_up_grads, D // n_dp)
    hidden_trade = gate(hidden_trade, *gate_up_sent)
    mix_back = ctx_trade(gate(mix_sent[0], hidden_trade))
    acts = gate(tuple(acts), *gate_up_sent)
    grad_down = weight_grad(acts, [[v] for v in route_grads], d, FF // n_dp, down_arrived)
    mix_back = gate(mix_back, grad_down)
    leaving = towards(pairs[0], mix_back, spreads[0])
    mix_homes = list(mix_homes) + [leaving[:rows], home(1, leaving[rows:].astype(BF16))]
    in_rows = gate(tuple(in_rows), leaving)
    grad_gate_up = weight_grad(in_rows, gate_up_grads, d, D // n_dp, gate_up_arrived)

    hidden_grad = from_exp(jnp.sum(hidden_trade.astype(F32), axis=0))
    scale_own = lax.dynamic_slice_in_dim(scale_in, c * rows, rows, axis=0)
    in_norm_grad, in_gain_grad = norm_back(hidden_grad, inputs * scale_own, scale_own, gain_in)
    input_grad = mid_grad + in_norm_grad

    def spread_features(v):
        shaped = jnp.zeros((head_groups, n_ctx, head_run), F32)
        return place(shaped, v.reshape(head_groups, 1, head_run), None, c).reshape(1, D)

    small_grad = jnp.concatenate(
        [
            router_grad_t,
            in_gain_grad[None],
            spread_features(head_gain_grads[0]),
            spread_features(head_gain_grads[1]),
            ffn_gain_grad[None],
        ],
        axis=0,
    )
    count = small_grad.shape[0]
    part = small_grad.reshape(count, n_dp, n_ctx, n_exp, shard).transpose(1, 2, 3, 0, 4)
    late_d = mark[0, 0].astype(jnp.int32)
    total = lax.dynamic_index_in_dim(part, late_d, 0, keepdims=False)
    for m in range(1, n_dp):
        total = total + dp_shift(
            lax.dynamic_index_in_dim(part, (late_d + m) % n_dp, 0, keepdims=False), m
        )
    part = total
    part = jnp.sum(ctx_trade(gate(part, mix_back)), axis=0)
    if head_groups == n_dp:
        flat = part.reshape(n_exp, count * shard)
        high = flat.astype(BF16)
        flat = jnp.concatenate([high, (flat - high.astype(F32)).astype(BF16)], axis=1)
        lines = -(-2 * count * shard // (8 * D)) * 8
        flat = jnp.pad(flat, ((0, 0), (0, lines * D - 2 * count * shard)))
        out_sent = jnp.concatenate([out_dp.astype(BF16), flat.reshape(n_exp, lines, D)], axis=1)
        out_trade = lax.all_to_all(out_sent, "exp", 0, 0, tiled=True)
        out_trade = gate(out_trade, grad_gate_up)
        grad_out = jnp.sum(out_trade[:, :shard].astype(F32), axis=0)
        flat = jnp.sum(out_trade[:, shard:].astype(F32), axis=0).reshape(-1)
        total = (flat[: count * shard] + flat[count * shard : 2 * count * shard]).reshape(
            count, shard
        )
    else:
        grad_out = lax.psum_scatter(
            dot_at(mixed, attn_grad), ("dp", "ctx", "exp"), scatter_dimension=0, tiled=True
        )
        total = jnp.sum(lax.all_to_all(part, "exp", 0, 0, tiled=True), axis=0)
    small_sum = total.T
    mix_homes = gate(tuple(mix_homes), grad_out)
    mixture = mix_homes[2] + sum(v.astype(F32) for v in mix_homes[:2] + mix_homes[3:])
    final_rows = (mid_rows + mixture).astype(BF16)

    qkv_arrived = gate(tuple(qkv_arrived), final_rows, small_sum)
    qkv_exp = part_of(qkv_dp, 0, z)
    for v in qkv_arrived:
        qkv_exp = qkv_exp + v.astype(F32)
    qkv_exp = qkv_exp.reshape(n_ctx, shard, 3 * width)
    grad_qkv = all_owners(ctx_trade(qkv_exp.astype(BF16)).astype(F32))

    return (
        final_rows[:prompt_len][None],
        final_rows[prompt_len:][None],
        input_grad[:prompt_len][None],
        input_grad[prompt_len:][None],
        grad_qkv,
        grad_out,
        small_sum[:, :experts],
        small_sum[:, experts:],
        grad_gate_up[None],
        grad_down[None],
    )


def solution(mesh):
    return jax.shard_map(
        body,
        mesh=mesh,
        in_specs=(
            P(("dp", "exp"), "ctx", None),
            P(("dp", "exp"), "ctx", None),
            P(("dp", "exp"), "ctx", None),
            P(("dp", "exp"), "ctx", None, None),
            P(("dp", "ctx", "exp"), None),
            P(("dp", "ctx", "exp"), None),
            P(("dp", "ctx", "exp"), None),
            P(("dp", "ctx", "exp"), None),
            P(("ctx", "exp"), None, None),
            P(("ctx", "exp"), None, None),
            P(("dp", "exp"), "ctx", None),
            P(("dp", "exp"), "ctx", None),
        ),
        out_specs=(
            P(("dp", "exp"), "ctx", None),
            P(("dp", "exp"), "ctx", None),
            P(("dp", "exp"), "ctx", None),
            P(("dp", "exp"), "ctx", None),
            P(("dp", "ctx", "exp"), None),
            P(("dp", "ctx", "exp"), None),
            P(("dp", "ctx", "exp"), None),
            P(("dp", "ctx", "exp"), None),
            P(("ctx", "exp"), "dp", None),
            P(("ctx", "exp"), "dp", None),
        ),
        check_vma=False,
    )
```

```python
import jax
import jax.numpy as jnp
from jax import lax
from jax.experimental import pallas as pl
from jax.experimental.pallas import tpu as pltpu
from jax.sharding import PartitionSpec as P

D = 2048
HEADS = 16
HEAD_DIM = 128
FF = 1024
TOP = 8

NORM_EPS = 1e-05
ROPE_BASE = 10000.0
NEGATIVE = -1e30
HIGHEST_PREC = lax.Precision.HIGHEST
F32 = jnp.float32
BF16 = jnp.bfloat16


def row_scale(values):
    return lax.rsqrt(jnp.mean(values * values, axis=-1, keepdims=True) + NORM_EPS)


def rope_tables(position, half_dim):
    inverse = ROPE_BASE ** (-jnp.arange(half_dim, dtype=F32) / half_dim)
    angles = position[:, None] * inverse[None, :]
    cosine, sine_rows = jnp.cos(angles), jnp.sin(angles)
    return (
        jnp.concatenate([cosine, cosine], axis=1),
        jnp.concatenate([-sine_rows, sine_rows], axis=1),
    )


def norm_back(grad_rows, normed, scale_rows, gain_col):
    grad_normed = grad_rows * gain_col
    grad_input = scale_rows * (
        grad_normed - normed * jnp.mean(grad_normed * normed, axis=-1, keepdims=True)
    )
    return (grad_input, jnp.sum(grad_rows * normed, axis=0))


def dot(a, b):
    return jnp.dot(a, b, preferred_element_type=F32)


def dot_bt(a, b):
    return lax.dot_general(a, b, (((1,), (1,)), ((), ())), preferred_element_type=F32)


def dot_at(a, b):
    return lax.dot_general(a, b, (((0,), (0,)), ((), ())), preferred_element_type=F32)


def attend(projected, scales, gains, cosine, sine_rows, hidden_pairs):
    rows = projected.shape[0]
    width = projected.shape[1] // 3
    heads = width // HEAD_DIM

    def kernel(pq, pk, pv, scale_ref, gain_ref, cos_ref, sin_ref, pair_ref, mixed, q, k, v, total):
        def turned(values):
            return values * cos_ref[...] + pltpu.roll(values, HEAD_DIM // 2, 1) * sin_ref[...]

        query = turned(pq[...] * scale_ref[:, :1] * gain_ref[:1, :]).astype(BF16)
        key = turned(pk[...] * scale_ref[:, 1:2] * gain_ref[1:2, :]).astype(BF16)
        value = pv[...].astype(BF16)
        scores = dot_bt(query, key) * HEAD_DIM ** (-0.5)
        scores = jnp.where(pair_ref[...] < 0.0, NEGATIVE, scores)
        row_max = jnp.max(scores, axis=-1, keepdims=True)
        log_total = row_max + jnp.log(
            jnp.sum(jnp.exp(scores - row_max), axis=-1, keepdims=True)
        )
        mixed[...] = dot(jnp.exp(scores - log_total).astype(BF16), value).astype(BF16)
        q[...], k[...], v[...] = query, key, value
        total[...] = jnp.broadcast_to(log_total, total.shape)

    def head(part):
        return pl.BlockSpec((rows, HEAD_DIM), lambda h: (0, part * heads + h))

    def whole(shape):
        return pl.BlockSpec(shape, lambda h: (0, 0))

    return pl.pallas_call(
        kernel,
        grid=(heads,),
        in_specs=[
            head(0),
            head(1),
            head(2),
            whole((rows, 2)),
            pl.BlockSpec((2, HEAD_DIM), lambda h: (0, h)),
            whole((rows, HEAD_DIM)),
            whole((rows, HEAD_DIM)),
            whole((rows, rows)),
        ],
        out_specs=[head(0)] * 5,
        out_shape=[jax.ShapeDtypeStruct((rows, width), BF16)] * 4
        + [jax.ShapeDtypeStruct((rows, width), F32)],
        compiler_params=pltpu.CompilerParams(vmem_limit_bytes=48 << 20),
        cost_estimate=pl.CostEstimate(flops=0, bytes_accessed=0, transcendentals=0),
        name="attend",
    )(projected, projected, projected, scales, gains, cosine, sine_rows, hidden_pairs)


def attend_back(grads, kept, projected, scales, gains, cosine, sine_rows, hidden_pairs):
    query_b, key_b, value_b, log_total = kept
    rows = projected.shape[0]
    width = projected.shape[1] // 3
    heads = width // HEAD_DIM
    scale = HEAD_DIM ** (-0.5)

    def kernel(
        g, q, k, v, total, pq, pk, scale_ref, gain_ref, cos_ref, sin_ref, pair_ref,
        query_out, key_out, value_out, gain_out, sum_out,
    ):
        def turned_back(values):
            return values * cos_ref[...] - pltpu.roll(values, HEAD_DIM // 2, 1) * sin_ref[...]

        scores = dot_bt(q[...], k[...]) * scale
        scores = jnp.where(pair_ref[...] < 0.0, NEGATIVE, scores)
        attention = jnp.exp(scores - total[:, :1])
        prob_att = dot_bt(g[...], v[...])
        delta = jnp.sum(attention * prob_att, axis=-1, keepdims=True)
        score_grad = (attention * (prob_att - delta)).astype(BF16)
        query = turned_back(dot(score_grad, k[...]) * scale)
        key = turned_back(dot_at(score_grad, q[...]) * scale)
        value_out[...] = dot_at(attention.astype(BF16), g[...]).astype(BF16)
        query_out[...], key_out[...] = query, key
        query_n = query * (pq[...] * scale_ref[:, :1])
        key_n = key * (pk[...] * scale_ref[:, 1:2])
        gain_out[:1, :] = jnp.sum(query_n, axis=0, keepdims=True)
        gain_out[1:2, :] = jnp.sum(key_n, axis=0, keepdims=True)
        query_sum = jnp.sum(query_n * gain_ref[:1, :], axis=-1, keepdims=True)
        key_sum = jnp.sum(key_n * gain_ref[1:2, :], axis=-1, keepdims=True)
        sums = jnp.concatenate(
            [
                jnp.broadcast_to(query_sum, (rows, HEAD_DIM)),
                jnp.broadcast_to(key_sum, (rows, HEAD_DIM)),
            ],
            axis=1,
        )

        @pl.when(pl.program_id(0) == 0)
        def _():
            sum_out[...] = sums

        @pl.when(pl.program_id(0) > 0)
        def _():
            sum_out[...] += sums

    def head(part):
        return pl.BlockSpec((rows, HEAD_DIM), lambda h: (0, part * heads + h))

    def whole(shape):
        return pl.BlockSpec(shape, lambda h: (0, 0))

    pair = pl.BlockSpec((2, HEAD_DIM), lambda h: (0, h))
    return pl.pallas_call(
        kernel,
        grid=(heads,),
        in_specs=[head(0)] * 5
        + [
            head(0),
            head(1),
            whole((rows, 2)),
            pair,
            whole((rows, HEAD_DIM)),
            whole((rows, HEAD_DIM)),
            whole((rows, rows)),
        ],
        out_specs=[head(0)] * 3 + [pair, whole((rows, 2 * HEAD_DIM))],
        out_shape=[
            jax.ShapeDtypeStruct((rows, width), F32),
            jax.ShapeDtypeStruct((rows, width), F32),
            jax.ShapeDtypeStruct((rows, width), BF16),
            jax.ShapeDtypeStruct((2, width), F32),
            jax.ShapeDtypeStruct((rows, 2 * HEAD_DIM), F32),
        ],
        compiler_params=pltpu.CompilerParams(vmem_limit_bytes=48 << 20),
        cost_estimate=pl.CostEstimate(flops=0, bytes_accessed=0, transcendentals=0),
        name="attend_back",
    )(
        grads, query_b, key_b, value_b, log_total, projected, projected, scales, gains,
        cosine, sine_rows, hidden_pairs,
    )


def norms_back(query_turn, key_turn, value_grad, projected, scales, means, gains):
    rows, width = query_turn.shape

    def kernel(query, key, value, projected_ref, scale_ref, mean_ref, gain_ref, out):
        for i, turn in enumerate((query, key)):
            at = slice(i * width, (i + 1) * width)
            scale = scale_ref[:, i : i + 1]
            normed = projected_ref[:, at] * scale
            out[:, at] = (
                scale * (turn[...] * gain_ref[i : i + 1, :] - normed * mean_ref[:, i : i + 1])
            ).astype(BF16)
        out[:, 2 * width :] = value[...]

    return pl.pallas_call(
        kernel,
        out_shape=jax.ShapeDtypeStruct((rows, 3 * width), BF16),
        compiler_params=pltpu.CompilerParams(vmem_limit_bytes=48 << 20),
        cost_estimate=pl.CostEstimate(flops=0, bytes_accessed=0, transcendentals=0),
        name="norms_back",
    )(query_turn, key_turn, value_grad, projected, scales, means, gains)


def expert_rows(rows, cot, w_gate_up, w_down, w_router, expert, senders, blocks):
    count, experts = rows.shape[0], w_router.shape[1]
    tile = FF // 2
    steps = FF // tile
    extra = -(-2 * experts // 128) * 128
    piece = count // (senders * blocks)

    def kernel(expert_ref, rows_ref, cot_ref, wg_ref, wu_ref, wd_ref, wr_ref, *refs):
        row_refs = refs[:blocks]
        act_ref, gg_ref, ug_ref, gate_ref, row_sum, gate_grad = refs[blocks:]
        step = pl.program_id(0)
        row_block = rows_ref[...]

        @pl.when(step == 0)
        def _():
            logits = dot(row_block, wr_ref[...])
            shifted = jnp.exp(logits - jnp.max(logits, axis=-1, keepdims=True))
            router = shifted / jnp.sum(shifted, axis=-1, keepdims=True)
            lane = lax.broadcasted_iota(jnp.int32, router.shape, 1)
            own = jnp.sum(jnp.where(lane == expert_ref[0], router, 0.0), axis=-1, keepdims=True)
            gate_ref[...] = jnp.broadcast_to(own, gate_ref.shape)

        gate = gate_ref[:, :1]
        gate_part = dot(row_block, wg_ref[...])
        up_part = dot(row_block, wu_ref[...])
        cot_act = dot_bt(cot_ref[...], wd_ref[...])
        sigmoid_gate = jax.nn.sigmoid(gate_part)
        swish = gate_part * sigmoid_gate
        activated = (swish * up_part).astype(BF16)
        act_grad = gate * cot_act
        gate_part_grad = (
            act_grad * up_part * sigmoid_gate * (1.0 + gate_part * (1.0 - sigmoid_gate))
        ).astype(BF16)
        up_part_grad = (act_grad * swish).astype(BF16)
        act_ref[...] = activated
        gg_ref[...] = gate_part_grad
        ug_ref[...] = up_part_grad
        row_part = dot_bt(gate_part_grad, wg_ref[...]) + dot_bt(up_part_grad, wu_ref[...])
        part = jnp.sum(cot_act * activated.astype(F32), axis=-1, keepdims=True)
        part = jnp.broadcast_to(part, gate_grad.shape)

        @pl.when(step == 0)
        def _():
            row_sum[...] = row_part
            gate_grad[...] = part

        @pl.when(step > 0)
        def _():
            row_sum[...] += row_part
            gate_grad[...] += part

        @pl.when(step == steps - 1)
        def _():
            lane = lax.broadcasted_iota(jnp.int32, (piece, extra), 1)
            for j in range(senders):
                for i in range(blocks):
                    at = pl.ds((j * blocks + i) * piece, piece)
                    row_refs[i][j, :, :D] = row_sum[at, :].astype(BF16)
                    both = jnp.broadcast_to(gate_grad[at, :1], (piece, extra))
                    high = both.astype(BF16).astype(F32)
                    row_refs[i][j, :, D:] = jnp.where(
                        lane == expert_ref[0],
                        high,
                        jnp.where(lane == experts + expert_ref[0], both - high, 0.0),
                    ).astype(BF16)

    def whole(shape):
        return pl.BlockSpec(shape, lambda j, at: (0, 0))

    columns = pl.BlockSpec((count, tile), lambda j, at: (0, j))
    return pl.pallas_call(
        kernel,
        grid_spec=pltpu.PrefetchScalarGridSpec(
            num_scalar_prefetch=1,
            grid=(steps,),
            in_specs=[
                whole((count, D)),
                whole((count, D)),
                pl.BlockSpec((D, tile), lambda j, at: (0, j)),
                pl.BlockSpec((D, tile), lambda j, at: (0, steps + j)),
                pl.BlockSpec((tile, D), lambda j, at: (j, 0)),
                whole((D, experts)),
            ],
            out_specs=[pl.BlockSpec((senders, piece, D + extra), lambda j, at: (0, 0, 0))] * blocks
            + [columns, columns, columns, whole((count, 128))],
            scratch_shapes=[pltpu.VMEM((count, D), F32), pltpu.VMEM((count, 128), F32)],
        ),
        out_shape=[jax.ShapeDtypeStruct((senders, piece, D + extra), BF16)] * blocks
        + [
            jax.ShapeDtypeStruct((count, FF), BF16),
            jax.ShapeDtypeStruct((count, FF), BF16),
            jax.ShapeDtypeStruct((count, FF), BF16),
            jax.ShapeDtypeStruct((count, 128), F32),
        ],
        compiler_params=pltpu.CompilerParams(vmem_limit_bytes=56 << 20),
        cost_estimate=pl.CostEstimate(flops=0, bytes_accessed=0, transcendentals=0),
        name="expert",
    )(expert, rows, cot, w_gate_up, w_gate_up, w_down, w_router)


def expert_outs(acts, gates, cot, w_down):
    count = acts.shape[0]
    tile = count // 2

    def kernel(act_ref, gate_ref, cot_ref, wd_ref, mix_ref, route_ref):
        gate = gate_ref[:, :1]
        out = dot(act_ref[...], wd_ref[...]).astype(BF16)
        mix_ref[...] = (gate * out.astype(F32)).astype(BF16)
        route_ref[...] = (gate * cot_ref[...].astype(F32)).astype(BF16)

    def rows_of(columns):
        return pl.BlockSpec((tile, columns), lambda i: (i, 0))

    return pl.pallas_call(
        kernel,
        grid=(count // tile,),
        in_specs=[rows_of(FF), rows_of(128), rows_of(D), pl.BlockSpec((FF, D), lambda i: (0, 0))],
        out_specs=[rows_of(D), rows_of(D)],
        out_shape=[jax.ShapeDtypeStruct((count, D), BF16)] * 2,
        compiler_params=pltpu.CompilerParams(vmem_limit_bytes=56 << 20),
        cost_estimate=pl.CostEstimate(
            flops=2 * count * FF * D, bytes_accessed=6 * count * D + 2 * FF * D, transcendentals=0
        ),
        name="expert_outs",
    )(acts, gates, cot, w_down)


def weight_grad(lefts, rights, part, rows_out, arrived=()):
    blocks, parts = len(lefts), len(rights[0])
    depth = lefts[0].shape[0]
    tile = min(256, rows_out)
    tiles = rows_out // tile
    widths = [v.shape[1] for v in rights[0]]

    def kernel(part_ref, *refs):
        left, right, out = refs[:blocks], refs[blocks : blocks * (1 + parts)], refs[-1]
        at = 0
        for p in range(parts):
            total = dot_at(left[0][...], right[p][...])
            for b in range(1, blocks):
                total = total + dot_at(left[b][...], right[b * parts + p][...])
            for more in refs[blocks * (1 + parts) : -1]:
                total = total + more[:, at : at + widths[p]].astype(F32)
            out[:, at : at + widths[p]] = total.astype(out.dtype)
            at += widths[p]

    row_block = pl.BlockSpec((tile, sum(widths)), lambda i, at: (i, 0))
    return pl.pallas_call(
        kernel,
        grid_spec=pltpu.PrefetchScalarGridSpec(
            num_scalar_prefetch=1,
            grid=(tiles,),
            in_specs=[pl.BlockSpec((depth, tile), lambda i, at: (0, at[0] * tiles + i))] * blocks
            + [
                pl.BlockSpec((depth, w), lambda i, at: (0, 0))
                for _ in range(blocks)
                for w in widths
            ]
            + [row_block] * len(arrived),
            out_specs=row_block,
        ),
        out_shape=jax.ShapeDtypeStruct((rows_out, sum(widths)), F32 if arrived else BF16),
        compiler_params=pltpu.CompilerParams(vmem_limit_bytes=56 << 20),
        cost_estimate=pl.CostEstimate(
            flops=4 * blocks * depth * rows_out * sum(widths),
            bytes_accessed=2 * blocks * depth * (rows_out + sum(widths)) + 4 * rows_out * sum(widths),
            transcendentals=0,
        ),
        name="weight_grad",
    )(part.reshape(1).astype(jnp.int32), *lefts, *[v for r in rights for v in r], *arrived)


def body(
    prompt_x,
    cont_x,
    cont_ids,
    routes,
    qkv_weight,
    out_weight,
    router_weight,
    norm_gains,
    gate_up_weight,
    down_weight,
    prompt_cot,
    cont_cot,
):
    n_dp, n_ctx, n_exp = lax.axis_size("dp"), lax.axis_size("ctx"), lax.axis_size("exp")
    d, c, z = lax.axis_index("dp"), lax.axis_index("ctx"), lax.axis_index("exp")
    prompt_len = prompt_x.shape[1]
    cont_len = cont_x.shape[1]
    rows = prompt_len + cont_len
    prompt_total = prompt_len * n_ctx
    experts = router_weight.shape[1]
    capacity = rows * TOP * 17 // (16 * experts)
    score_scale = HEAD_DIM ** (-0.5)
    shard = qkv_weight.shape[0]
    heads_own = HEADS // n_ctx
    width = heads_own * HEAD_DIM
    head_groups = n_dp if (D // (n_dp * n_ctx)) % HEAD_DIM == 0 else 1
    head_run = D // (head_groups * n_ctx)
    own_expert = c * n_exp + z

    def ctx_swap(x, k):
        return lax.ppermute(x, "ctx", [(i, i ^ k) for i in range(n_ctx)])

    def ctx_trade(x):
        return lax.all_to_all(x, "ctx", 0, 0, tiled=True)

    def ctx_gather(x):
        return ctx_trade(jnp.broadcast_to(x[None], (n_ctx,) + x.shape))

    def exp_shift(x, s):
        return lax.ppermute(x, "exp", [(i, (i + s) % n_exp) for i in range(n_exp)])

    def dp_shift(x, m):
        return lax.ppermute(x, "dp", [(i, (i + m) % n_dp) for i in range(n_dp)])

    def part_of(x, axis, at):
        return lax.dynamic_index_in_dim(x, at, axis, keepdims=False)

    def place(buffer, x, *index):
        start, shape = [], []
        for at, size in zip(index, buffer.shape):
            start.append(0 if at is None else at)
            shape.append(size if at is None else 1)
        shape += buffer.shape[len(index) :]
        start += [0] * (buffer.ndim - len(index))
        return lax.dynamic_update_slice(buffer, x.reshape(shape), start)

    def gate(x, *others):
        out = lax.optimization_barrier((x,) + others)[0]
        return list(out) if isinstance(out, tuple) else out

    mark = jnp.full((8, 128), d, jnp.int32).astype(F32)

    def hand_on(in_ref, out_ref):
        out_ref[...] = in_ref[...]

    def fence(*values):
        nonlocal mark
        mark = pl.pallas_call(
            hand_on,
            out_shape=jax.ShapeDtypeStruct(mark.shape, mark.dtype),
            cost_estimate=pl.CostEstimate(
                flops=2 * 10**11, bytes_accessed=0, transcendentals=0
            ),
            name="fence",
        )(gate(mark, *values))

    def after(*values):
        out = lax.optimization_barrier(values + (mark,))
        return out[0] if len(values) == 1 else out[:-1]

    def by_owner(v):
        runs = v.shape[1] // (n_ctx * head_run)
        return jnp.stack(
            [
                jnp.concatenate(
                    [
                        v[:, (i * n_ctx + j) * head_run : (i * n_ctx + j + 1) * head_run]
                        for i in range(runs)
                    ],
                    axis=1,
                )
                for j in range(n_ctx)
            ]
        )

    def all_owners(v):
        runs = v.shape[2] // head_run
        return jnp.concatenate(
            [
                v[j][:, i * head_run : (i + 1) * head_run]
                for i in range(runs)
                for j in range(n_ctx)
            ],
            axis=1,
        )

    x_own = jnp.concatenate([prompt_x[0], cont_x[0]], axis=0)
    cot_own = jnp.concatenate([prompt_cot[0], cont_cot[0]], axis=0)

    small_width = experts + norm_gains.shape[1]
    route_width = -(-rows * TOP // shard)
    route_cols = routes[0, 0].T.astype(BF16).reshape(-1)
    route_cols = jnp.pad(route_cols, (0, route_width * shard - rows * TOP)).reshape(shard, -1)
    extra = jnp.concatenate(
        [
            router_weight,
            norm_gains,
            jnp.broadcast_to(cont_ids[0].astype(BF16), (shard, cont_len)),
            route_cols,
        ],
        axis=1,
    )
    extra_width = -(-extra.shape[1] // 128) * 128
    extra = jnp.pad(extra, ((0, 0), (0, extra_width - extra.shape[1])))
    all_width = 3 * width + extra_width
    runs = 3 * width // head_run


    def pack(w_ref, extra_ref, out_ref):
        for j in range(n_ctx):
            for i in range(runs):
                out_ref[j, :, i * head_run : (i + 1) * head_run] = w_ref[
                    :, (i * n_ctx + j) * head_run : (i * n_ctx + j + 1) * head_run
                ]
            out_ref[j, :, 3 * width :] = extra_ref[...]

    packed_w = pl.pallas_call(
        pack, out_shape=jax.ShapeDtypeStruct((n_ctx, shard, all_width), BF16), name="pack"
    )(qkv_weight, extra)
    slab = ctx_trade(packed_w)
    out_blocks = [out_weight] + [exp_shift(out_weight, s) for s in range(1, n_exp)]
    fence(packed_w)

    def by_exp(v):
        shaped = v.reshape(v.shape[:-1] + (n_dp, n_ctx, n_exp, shard))
        return jnp.swapaxes(shaped, -3, -2).reshape(v.shape)

    def from_exp(v):
        shaped = v.reshape(v.shape[:-1] + (n_dp, n_exp, n_ctx, shard))
        return jnp.swapaxes(shaped, -3, -2).reshape(v.shape)

    x_turned = by_exp(x_own)
    out_blocks = after(*out_blocks)
    out_exp = jnp.zeros((n_exp, shard, D), BF16)
    for j in range(n_exp):
        out_exp = place(out_exp, out_blocks[j], (z - j) % n_exp)

    slab = after(slab)
    ids_at = 3 * width + small_width
    ids = slab[:, 0, ids_at : ids_at + cont_len].astype(F32).astype(jnp.int32)
    w_blocks = [slab] + [exp_shift(slab, s) for s in range(1, n_exp)]
    w_sets = [[dp_shift(slab, m)] for m in range(1, n_dp)]
    out_ctx = ctx_gather(gate(out_exp, slab))
    fence(slab, out_exp)
    out_ctx = after(out_ctx)
    x_sent = gate(x_turned, out_ctx)
    x_all = ctx_gather(x_sent)
    fence(x_sent)

    x_all = after(x_all).reshape(n_ctx * rows, D).astype(F32)
    scale_in = row_scale(x_all)
    w_blocks = gate(tuple(w_blocks), scale_in)
    for m in range(1, n_dp):
        w_sets[m - 1] += [dp_shift(v, m) for v in w_blocks[1:]]
    cot_blocks = [cot_own]
    routes_at = ids_at + cont_len
    places = jnp.stack(
        [(d - m) % n_dp for m in range(n_dp)] + [(z - s) % n_exp for s in range(n_exp)]
    ).astype(jnp.int32)

    def assemble(at_ref, *refs):
        blocks, (w_ref, small_ref) = refs[: n_dp * n_exp], refs[n_dp * n_exp :]
        for m in range(n_dp):
            for s in range(n_exp):
                block = blocks[m * n_exp + s]
                w_ref[at_ref[m], at_ref[n_dp + s]] = block[:, :, : 3 * width]
                small_ref[at_ref[m], at_ref[n_dp + s]] = block[:, :, 3 * width :]

    in_vmem = pl.BlockSpec(memory_space=pltpu.VMEM)
    w_qkv, w_small = pl.pallas_call(
        assemble,
        in_specs=[pl.BlockSpec(memory_space=pltpu.SMEM)] + [in_vmem] * (n_dp * n_exp),
        out_specs=[in_vmem] * 2,
        out_shape=[
            jax.ShapeDtypeStruct((n_dp, n_exp, n_ctx, shard, 3 * width), BF16),
            jax.ShapeDtypeStruct((n_dp, n_exp, n_ctx, shard, extra_width), BF16),
        ],
        compiler_params=pltpu.CompilerParams(vmem_limit_bytes=56 << 20),
        cost_estimate=pl.CostEstimate(flops=0, bytes_accessed=0, transcendentals=0),
        name="assemble",
    )(places, *w_blocks, *[v for w_set in w_sets for v in w_set])
    w_qkv = w_qkv.reshape(D, 3 * width)
    w_small = jnp.swapaxes(w_small, 1, 2).reshape(D, extra_width)
    w_router = w_small[:, :experts]
    gains_t = w_small[:, experts:small_width].astype(F32).T
    gain_in, gain_ffn = gains_t[0], gains_t[3]

    def own_features(v):
        shaped = v.reshape(v.shape[:-1] + (head_groups, n_ctx, head_run))
        return part_of(shaped, v.ndim, c).reshape(v.shape[:-1] + (width,))

    gain_query, gain_key = own_features(gains_t[1]), own_features(gains_t[2])

    upper = (
        jnp.arange(rows, dtype=jnp.int32)[:, None] < jnp.arange(rows, dtype=jnp.int32)[None, :]
    ).astype(BF16)
    send_experts = (jnp.arange(n_ctx) * n_exp + z).astype(F32)

    def spread_of(route_cols):
        named = jnp.any(
            route_cols.astype(F32)[None] == send_experts[:, None, None], axis=1
        )
        rank = dot(named.astype(BF16), upper)
        slots = jnp.where(named, rank, -1.0)
        return (
            (slots[:, None, :] == jnp.arange(capacity, dtype=F32)[None, :, None])
            .astype(BF16)
            .reshape(n_ctx * capacity, rows)
        )

    spread = [spread_of(routes[0, 0].T)]

    def spread_pair(blocks):
        n = len(blocks)
        parts = []
        for i, s in enumerate(blocks):
            part = spread[s].reshape(n_ctx, 1, capacity, rows)
            parts.append(jnp.pad(part, ((0, 0), (0, 0), (0, 0), (i * rows, (n - 1 - i) * rows))))
        return jnp.concatenate(parts, axis=1).reshape(n_ctx * n * capacity, n * rows)

    def pack_of(spread_rows, blocks):
        n = len(blocks)
        sent = dot(spread_rows, blocks[0] if n == 1 else jnp.concatenate(blocks, axis=0))
        return sent.astype(BF16).reshape(n_ctx, n, capacity, -1)

    def pack_cot(blocks):
        return pack_of(
            spread_pair(blocks) if len(blocks) > 1 else spread[blocks[0]],
            [cot_blocks[s] for s in blocks],
        )

    def trade_pieces(pieces):
        return [ctx_swap(pieces[k], k) if k else pieces[k] for k in range(n_ctx)]

    def in_order(pieces):
        whole = jnp.zeros((n_ctx,) + pieces[0].shape, pieces[0].dtype)
        for k in range(n_ctx):
            whole = place(whole, pieces[k], c ^ k)
        return whole

    w_gate_up = gate_up_weight[0]
    w_down = down_weight[0]
    pairs = [list(range(i, i + 2)) for i in range(0, n_exp, 2)]

    total_rows = rows * n_ctx
    index = jnp.arange(rows, dtype=jnp.int32)
    in_prompt = index < prompt_len
    position, seg_rows, order = [], [], []
    for j in range(n_ctx):
        seg = ids[j]
        starts = jnp.sum((seg[None, :] < seg[:, None]).astype(jnp.int32), axis=1)
        within = jnp.arange(cont_len, dtype=jnp.int32) - starts
        at = j * prompt_len
        position.append(jnp.concatenate([at + index[:prompt_len], prompt_total + within]))
        order.append(jnp.where(in_prompt, at + index, index))
        seg_rows.append(
            jnp.concatenate([jnp.full((prompt_len,), -1, jnp.int32), j * 64 + seg])
        )
    position = jnp.concatenate(position).astype(F32)
    order = jnp.concatenate(order)
    seg_of = jnp.concatenate(seg_rows)
    is_prompt = jnp.concatenate([in_prompt] * n_ctx)
    before = order[None, :] <= order[:, None]
    allowed = jnp.where(
        is_prompt[:, None],
        is_prompt[None, :] & before,
        is_prompt[None, :] | ((seg_of[None, :] == seg_of[:, None]) & before),
    )
    hidden_pairs = jnp.where(allowed, 0.0, -1.0)
    cosine, sine_rows = rope_tables(position, HEAD_DIM // 2)

    cot_sent = gate(pack_cot([0]), scale_in)
    cot_trade = ctx_trade(cot_sent)
    fence(cot_sent, w_qkv)
    hidden_in = after((x_all * after(scale_in) * by_exp(gain_in)).astype(BF16))
    projected = dot(hidden_in, w_qkv)

    def ctx_sum(total):
        k = 1
        while k < n_ctx:
            total = total + ctx_swap(total, k)
            k *= 2
        return total

    raw_query, raw_key = projected[:, :width], projected[:, width : 2 * width]
    squares = jnp.stack([jnp.sum(raw_query * raw_query, axis=-1), jnp.sum(raw_key * raw_key, axis=-1)])
    cot_flight = [exp_shift(gate(cot_blocks[0], squares), s) for s in range(1, n_exp)]
    scales = lax.rsqrt(ctx_sum(squares) / D + NORM_EPS)
    spread += [
        spread_of(
            part_of(v[..., routes_at : routes_at + route_width], 0, c)
            .reshape(-1)[: rows * TOP]
            .reshape(TOP, rows)
        )
        for v in gate(tuple(w_blocks[1:]), squares)
    ]
    out_ctx = gate(out_ctx, scales)
    out_halves = [out_ctx] + [dp_shift(out_ctx, m) for m in range(1, n_dp)]
    fence(scales, out_ctx)
    scales = after(scales)
    scales = scales.T
    head_gains = jnp.stack([gain_query, gain_key])
    mixed_heads, *kept = attend(projected, scales, head_gains, cosine, sine_rows, hidden_pairs)

    mixed_heads = gate(mixed_heads, cot_trade)
    mixed = ctx_trade(mixed_heads.reshape(n_ctx, rows, width))
    cot_own_rows = cot_trade
    spreads = [spread_pair(pair) for pair in pairs]
    fence(mixed_heads, *spreads)
    mixed = after(mixed)
    cot_blocks += gate(tuple(cot_flight), mixed)
    mixed = all_owners(mixed)
    cot_sent = gate(pack_cot(list(range(1, n_exp))), mixed)
    cot_trade = ctx_trade(cot_sent)
    fence(mixed, cot_sent)
    mixed = after(mixed)
    half = D // n_dp
    mixed_halves = jnp.stack([mixed[:, i * half : (i + 1) * half] for i in range(n_dp)])
    inputs = x_own.astype(F32)
    mid_rows = inputs
    for m in range(n_dp):
        mid_rows = mid_rows + dot(
            part_of(mixed_halves, 0, (d - m) % n_dp), out_halves[m].reshape(half, D)
        )
    scale_ffn = row_scale(mid_rows)
    normed_ffn = mid_rows * scale_ffn
    hidden_ffn = (normed_ffn * gain_ffn).astype(BF16)

    def softmax(logits):
        shifted = jnp.exp(logits - jnp.max(logits, axis=-1, keepdims=True))
        return shifted / jnp.sum(shifted, axis=-1, keepdims=True)

    cot_rows, made = [], []

    def towards(blocks, back, spread_rows):
        return dot_at(spread_rows, back.reshape(spread_rows.shape[0], -1))

    def home(s, summed):
        return exp_shift(summed, n_exp - s)

    near = exp_shift(hidden_ffn, 1)
    fence(hidden_ffn)

    near = after(near)
    far = [exp_shift(gate(hidden_ffn, near), s) for s in range(2, n_exp)]
    cot_trade = after(cot_trade)
    sent = gate(pack_of(spreads[0], [hidden_ffn, near]), cot_trade)
    plane = ctx_trade(sent)
    fence(near, sent)

    cot_back = [cot_own_rows[:, 0]] + [after(cot_trade)[:, s] for s in range(n_exp - 1)]
    for pair in pairs:
        cot_rows.append(jnp.stack([cot_back[s] for s in pair], axis=1).reshape(-1, D))
    plane = after(plane)
    far = gate(tuple(after(*far)), plane)
    sent = pack_of(spreads[1], far)
    plane_next = ctx_trade(sent)
    fence(sent, plane)

    expert_at = own_expert.reshape(1).astype(jnp.int32)

    def compute(i, in_rows):
        in_rows = in_rows.reshape(-1, D)
        out = expert_rows(
            in_rows, cot_rows[i], w_gate_up, w_down, w_router, expert_at, n_ctx, 2
        )
        made.append([in_rows] + list(out))

    compute(0, plane)
    sent = gate(made[0][2], plane_next)
    back = ctx_trade(sent)
    fence(sent)

    compute(1, after(plane_next))
    back = gate(after(back), made[1][1])
    leaving = towards([1], back, spread[1]).astype(BF16)
    homes = [home(1, leaving)]
    sent = gate(made[1][1], back)
    back = ctx_trade(sent)
    fence(sent, leaving)

    mix_sent, route_grads = [], []

    def weigh(i):
        acts, gates = after(made[i][3], made[i][6])
        mix, route = expert_outs(acts, gates, cot_rows[i], w_down)
        mix_sent.append(mix.reshape(n_ctx, 2, capacity, D))
        route_grads.append(route)

    def grads_sent(lefts, rights, rows_out):
        sent = [weight_grad(lefts, rights, half_rows[m], rows_out) for m in range(1, n_dp)]
        return sent, [dp_shift(v, m + 1) for m, v in enumerate(sent)]

    half_rows = [(d + m) % n_dp for m in range(n_dp)]
    weigh(0)
    back = gate(after(back), mix_sent[0])
    leaving = towards([2], back, spread[2]).astype(BF16)
    homes.append(home(2, leaving))
    sent = gate(made[1][2], back)
    back = ctx_trade(sent)
    fence(sent, leaving)

    weigh(1)
    back = gate(after(back), mix_sent[1])
    leaving = towards([3], back, spread[3]).astype(BF16)
    homes.append(home(3, leaving))
    sent = gate(made[0][1], back)
    back = ctx_trade(sent)
    fence(sent, leaving)

    back = after(back)
    returned = towards([0], back, spread[0])
    fence(returned)
    homes = after(*homes)
    for v in after(*homes):
        returned = returned + v.astype(F32)

    router = softmax(dot(hidden_ffn, w_router))
    prob_grad = returned[:, D : D + experts] + returned[:, D + experts : D + 2 * experts]
    logit_grad = router * (prob_grad - jnp.sum(router * prob_grad, axis=-1, keepdims=True))
    ffn_grad = returned[:, :D] + jnp.dot(logit_grad, w_router.astype(F32).T, precision=HIGHEST_PREC)
    router_grad_t = jnp.einsum(
        "re,rd->ed", logit_grad, hidden_ffn.astype(F32), precision=HIGHEST_PREC
    )
    mid_norm_grad, ffn_gain_grad = norm_back(ffn_grad, normed_ffn, scale_ffn, gain_ffn)
    mid_grad = cot_own.astype(F32) + mid_norm_grad

    attn_grad = mid_grad.astype(BF16)
    grad_halves = jnp.zeros((n_dp, rows, half), BF16)
    for m in range(n_dp):
        grad_halves = place(
            grad_halves,
            dot_bt(attn_grad, out_halves[m].reshape(half, D)).astype(BF16),
            (d - m) % n_dp,
        )
    pieces = by_owner(jnp.concatenate([grad_halves[i] for i in range(n_dp)], axis=1))
    mixed_grad = in_order(trade_pieces([part_of(pieces, 0, c ^ k) for k in range(n_ctx)]))
    sent = gate(mix_sent[1], mixed_grad)
    mix_trade = ctx_trade(sent)
    fence(mixed_grad, sent)
    mixed_grad = after(mixed_grad)
    query_turn, key_turn, value_grad, head_gain_grads, sums = attend_back(
        mixed_grad.reshape(total_rows, width),
        kept,
        projected,
        scales,
        head_gains,
        cosine,
        sine_rows,
        hidden_pairs,
    )
    sums = jnp.stack([sums[:, 0], sums[:, HEAD_DIM]])
    means = ctx_sum(sums) / D
    back = gate(mix_trade, means)
    leaving = towards(pairs[1], back, spreads[1]).astype(BF16)
    mix_homes = [home(2, leaving[:rows]), home(3, leaving[rows:])]
    attn_sent = gate(attn_grad, back)
    attn_grad_all = ctx_gather(attn_sent)
    fence(means, attn_sent, leaving)
    means = after(means)
    proj_grad = norms_back(
        query_turn, key_turn, value_grad, projected, scales, means.T, head_gains
    )

    sent = [
        weight_grad([hidden_in], [[proj_grad]], half_rows[m], half) for m in range(1, n_dp)
    ]
    arrived = [dp_shift(v, m + 1) for m, v in enumerate(sent)]
    fence(*sent)
    hidden_part = dot_bt(gate(proj_grad, *sent), w_qkv).astype(BF16)
    arrived = gate(tuple([after(v) for v in arrived]), hidden_part)
    qkv_dp = weight_grad([hidden_in], [[proj_grad]], half_rows[0], half, arrived)
    qkv_dp = qkv_dp.reshape(n_exp, n_ctx * shard, 3 * width)
    sent = [part_of(qkv_dp, 0, (z - 1) % n_exp).astype(BF16)]

    def ring_step(s, sent):
        arrived = exp_shift(sent, 1)
        return arrived, part_of(qkv_dp, 0, (z - s) % n_exp)

    ring_arrived, ring_part = ring_step(2, sent[0])
    attn_grad_all = gate(attn_grad_all, *sent)
    mix_trade = ctx_trade(gate(mix_sent[0], attn_grad_all))
    attn_grad_all = attn_grad_all.reshape(total_rows, D)
    fence(attn_grad_all, *sent)

    mix_homes = after(*mix_homes)
    in_rows, acts, gate_grads, up_grads = [after(*[v[i] for v in made]) for i in (0, 3, 4, 5)]
    acts = gate(tuple(acts), *mix_homes)
    gate_up_grads = [[gate_grads[i], up_grads[i]] for i in range(len(pairs))]
    out_rows = width // n_dp
    if head_groups == n_dp:
        out_left = [gate(after(mixed_heads), *mix_homes)]
        out_sent, out_arrived = grads_sent(out_left, [[attn_grad_all]], out_rows)
        acts = gate(tuple(acts), *out_sent)
    down_sent, down_arrived = grads_sent(acts, [[v] for v in route_grads], FF // n_dp)
    ring_sent = (gate(ring_arrived, *down_sent).astype(F32) + ring_part).astype(BF16)
    ring_arrived, ring_part = ring_step(3, ring_sent)
    in_rows = gate(tuple(in_rows), ring_sent)
    mix_back = gate(after(mix_trade), *down_sent)
    hidden_part = gate(hidden_part, mix_back)
    hidden_trade = ctx_trade(hidden_part.reshape(n_ctx, rows, D))
    if head_groups == n_dp:
        out_left = gate(tuple(out_left), *down_sent)
        out_dp = weight_grad(out_left, [[attn_grad_all]], half_rows[0], out_rows, out_arrived)
        out_dp = out_dp.reshape(n_exp, shard, D)
        in_rows = gate(tuple(in_rows), out_dp)
    gate_up_sent, gate_up_arrived = grads_sent(in_rows, gate_up_grads, D // n_dp)
    ring_sent = (gate(ring_arrived, *gate_up_sent).astype(F32) + ring_part).astype(BF16)
    ring_arrived, ring_part = ring_step(4, ring_sent)
    acts = gate(tuple(acts), ring_sent)
    grad_down = weight_grad(acts, [[v] for v in route_grads], d, FF // n_dp, down_arrived)
    mix_back = gate(mix_back, grad_down)
    leaving = towards(pairs[0], mix_back, spreads[0])
    mix_homes = list(mix_homes) + [leaving[:rows], home(1, leaving[rows:].astype(BF16))]
    in_rows = gate(tuple(in_rows), leaving)
    grad_gate_up = weight_grad(in_rows, gate_up_grads, d, D // n_dp, gate_up_arrived)

    hidden_grad = from_exp(jnp.sum(hidden_trade.astype(F32), axis=0))
    scale_own = lax.dynamic_slice_in_dim(scale_in, c * rows, rows, axis=0)
    in_norm_grad, in_gain_grad = norm_back(hidden_grad, inputs * scale_own, scale_own, gain_in)
    input_grad = mid_grad + in_norm_grad

    def spread_features(v):
        shaped = jnp.zeros((head_groups, n_ctx, head_run), F32)
        return place(shaped, v.reshape(head_groups, 1, head_run), None, c).reshape(1, D)

    small_grad = jnp.concatenate(
        [
            router_grad_t,
            in_gain_grad[None],
            spread_features(head_gain_grads[0]),
            spread_features(head_gain_grads[1]),
            ffn_gain_grad[None],
        ],
        axis=0,
    )
    count = small_grad.shape[0]
    part = small_grad.reshape(count, n_dp, n_ctx, n_exp, shard).transpose(1, 2, 3, 0, 4)
    late_d = mark[0, 0].astype(jnp.int32)
    total = lax.dynamic_index_in_dim(part, late_d, 0, keepdims=False)
    for m in range(1, n_dp):
        total = total + dp_shift(
            lax.dynamic_index_in_dim(part, (late_d + m) % n_dp, 0, keepdims=False), m
        )
    part = total
    part = jnp.sum(ctx_trade(part), axis=0)
    if head_groups == n_dp:
        flat = part.reshape(n_exp, count * shard)
        high = flat.astype(BF16)
        flat = jnp.concatenate([high, (flat - high.astype(F32)).astype(BF16)], axis=1)
        lines = -(-2 * count * shard // (8 * D)) * 8
        flat = jnp.pad(flat, ((0, 0), (0, lines * D - 2 * count * shard)))
        out_sent = jnp.concatenate([out_dp.astype(BF16), flat.reshape(n_exp, lines, D)], axis=1)
        out_trade = lax.all_to_all(out_sent, "exp", 0, 0, tiled=True)
        out_trade = gate(out_trade, grad_gate_up)
        grad_out = jnp.sum(out_trade[:, :shard].astype(F32), axis=0)
        flat = jnp.sum(out_trade[:, shard:].astype(F32), axis=0).reshape(-1)
        total = (flat[: count * shard] + flat[count * shard : 2 * count * shard]).reshape(
            count, shard
        )
    else:
        grad_out = lax.psum_scatter(
            dot_at(mixed, attn_grad), ("dp", "ctx", "exp"), scatter_dimension=0, tiled=True
        )
        total = jnp.sum(lax.all_to_all(part, "exp", 0, 0, tiled=True), axis=0)
    small_sum = total.T
    mix_homes = gate(tuple(mix_homes), grad_out)
    mixture = mix_homes[2] + sum(v.astype(F32) for v in mix_homes[:2] + mix_homes[3:])
    final_rows = (mid_rows + mixture).astype(BF16)

    qkv_exp = gate(ring_arrived, final_rows, small_sum).astype(F32) + ring_part
    qkv_exp = qkv_exp.reshape(n_ctx, shard, 3 * width)
    grad_qkv = all_owners(ctx_trade(qkv_exp.astype(BF16)).astype(F32))

    return (
        final_rows[:prompt_len][None],
        final_rows[prompt_len:][None],
        input_grad[:prompt_len][None],
        input_grad[prompt_len:][None],
        grad_qkv,
        grad_out,
        small_sum[:, :experts],
        small_sum[:, experts:],
        grad_gate_up[None],
        grad_down[None],
    )


def solution(mesh):
    return jax.shard_map(
        body,
        mesh=mesh,
        in_specs=(
            P(("dp", "exp"), "ctx", None),
            P(("dp", "exp"), "ctx", None),
            P(("dp", "exp"), "ctx", None),
            P(("dp", "exp"), "ctx", None, None),
            P(("dp", "ctx", "exp"), None),
            P(("dp", "ctx", "exp"), None),
            P(("dp", "ctx", "exp"), None),
            P(("dp", "ctx", "exp"), None),
            P(("ctx", "exp"), None, None),
            P(("ctx", "exp"), None, None),
            P(("dp", "exp"), "ctx", None),
            P(("dp", "exp"), "ctx", None),
        ),
        out_specs=(
            P(("dp", "exp"), "ctx", None),
            P(("dp", "exp"), "ctx", None),
            P(("dp", "exp"), "ctx", None),
            P(("dp", "exp"), "ctx", None),
            P(("dp", "ctx", "exp"), None),
            P(("dp", "ctx", "exp"), None),
            P(("dp", "ctx", "exp"), None),
            P(("dp", "ctx", "exp"), None),
            P(("ctx", "exp"), "dp", None),
            P(("ctx", "exp"), "dp", None),
        ),
        check_vma=False,
    )
```

```python
import jax
import jax.numpy as jnp
from jax import lax
from jax.experimental import pallas as pl
from jax.experimental.pallas import tpu as pltpu
from jax.sharding import PartitionSpec as P

D = 2048
HEADS = 16
HEAD_DIM = 128
FF = 1024
TOP = 8

NORM_EPS = 1e-05
ROPE_BASE = 10000.0
NEGATIVE = -1e30
HIGHEST_PREC = lax.Precision.HIGHEST
F32 = jnp.float32
BF16 = jnp.bfloat16


def row_scale(values):
    return lax.rsqrt(jnp.mean(values * values, axis=-1, keepdims=True) + NORM_EPS)


def rope_tables(position, half_dim):
    inverse = ROPE_BASE ** (-jnp.arange(half_dim, dtype=F32) / half_dim)
    angles = position[:, None] * inverse[None, :]
    cosine, sine_rows = jnp.cos(angles), jnp.sin(angles)
    return (
        jnp.concatenate([cosine, cosine], axis=1),
        jnp.concatenate([-sine_rows, sine_rows], axis=1),
    )


def norm_back(grad_rows, normed, scale_rows, gain_col):
    grad_normed = grad_rows * gain_col
    grad_input = scale_rows * (
        grad_normed - normed * jnp.mean(grad_normed * normed, axis=-1, keepdims=True)
    )
    return (grad_input, jnp.sum(grad_rows * normed, axis=0))


def dot(a, b):
    return jnp.dot(a, b, preferred_element_type=F32)


def dot_bt(a, b):
    return lax.dot_general(a, b, (((1,), (1,)), ((), ())), preferred_element_type=F32)


def dot_at(a, b):
    return lax.dot_general(a, b, (((0,), (0,)), ((), ())), preferred_element_type=F32)


def attend(projected, scales, gains, cosine, sine_rows, hidden_pairs):
    rows = projected.shape[0]
    width = projected.shape[1] // 3
    heads = width // HEAD_DIM

    def kernel(pq, pk, pv, scale_ref, gain_ref, cos_ref, sin_ref, pair_ref, mixed, q, k, v, total):
        def turned(values):
            return values * cos_ref[...] + pltpu.roll(values, HEAD_DIM // 2, 1) * sin_ref[...]

        query = turned(pq[...] * scale_ref[:, :1] * gain_ref[:1, :]).astype(BF16)
        key = turned(pk[...] * scale_ref[:, 1:2] * gain_ref[1:2, :]).astype(BF16)
        value = pv[...].astype(BF16)
        scores = dot_bt(query, key) * HEAD_DIM ** (-0.5)
        scores = jnp.where(pair_ref[...] < 0.0, NEGATIVE, scores)
        row_max = jnp.max(scores, axis=-1, keepdims=True)
        log_total = row_max + jnp.log(
            jnp.sum(jnp.exp(scores - row_max), axis=-1, keepdims=True)
        )
        mixed[...] = dot(jnp.exp(scores - log_total).astype(BF16), value).astype(BF16)
        q[...], k[...], v[...] = query, key, value
        total[...] = jnp.broadcast_to(log_total, total.shape)

    def head(part):
        return pl.BlockSpec((rows, HEAD_DIM), lambda h: (0, part * heads + h))

    def whole(shape):
        return pl.BlockSpec(shape, lambda h: (0, 0))

    return pl.pallas_call(
        kernel,
        grid=(heads,),
        in_specs=[
            head(0),
            head(1),
            head(2),
            whole((rows, 2)),
            pl.BlockSpec((2, HEAD_DIM), lambda h: (0, h)),
            whole((rows, HEAD_DIM)),
            whole((rows, HEAD_DIM)),
            whole((rows, rows)),
        ],
        out_specs=[head(0)] * 5,
        out_shape=[jax.ShapeDtypeStruct((rows, width), BF16)] * 4
        + [jax.ShapeDtypeStruct((rows, width), F32)],
        compiler_params=pltpu.CompilerParams(vmem_limit_bytes=48 << 20),
        cost_estimate=pl.CostEstimate(flops=0, bytes_accessed=0, transcendentals=0),
        name="attend",
    )(projected, projected, projected, scales, gains, cosine, sine_rows, hidden_pairs)


def attend_back(grads, kept, projected, scales, gains, cosine, sine_rows, hidden_pairs):
    query_b, key_b, value_b, log_total = kept
    rows = projected.shape[0]
    width = projected.shape[1] // 3
    heads = width // HEAD_DIM
    scale = HEAD_DIM ** (-0.5)

    def kernel(
        g, q, k, v, total, pq, pk, scale_ref, gain_ref, cos_ref, sin_ref, pair_ref,
        query_out, key_out, value_out, gain_out, sum_out,
    ):
        def turned_back(values):
            return values * cos_ref[...] - pltpu.roll(values, HEAD_DIM // 2, 1) * sin_ref[...]

        scores = dot_bt(q[...], k[...]) * scale
        scores = jnp.where(pair_ref[...] < 0.0, NEGATIVE, scores)
        attention = jnp.exp(scores - total[:, :1])
        prob_att = dot_bt(g[...], v[...])
        delta = jnp.sum(attention * prob_att, axis=-1, keepdims=True)
        score_grad = (attention * (prob_att - delta)).astype(BF16)
        query = turned_back(dot(score_grad, k[...]) * scale)
        key = turned_back(dot_at(score_grad, q[...]) * scale)
        value_out[...] = dot_at(attention.astype(BF16), g[...]).astype(BF16)
        query_out[...], key_out[...] = query, key
        query_n = query * (pq[...] * scale_ref[:, :1])
        key_n = key * (pk[...] * scale_ref[:, 1:2])
        gain_out[:1, :] = jnp.sum(query_n, axis=0, keepdims=True)
        gain_out[1:2, :] = jnp.sum(key_n, axis=0, keepdims=True)
        query_sum = jnp.sum(query_n * gain_ref[:1, :], axis=-1, keepdims=True)
        key_sum = jnp.sum(key_n * gain_ref[1:2, :], axis=-1, keepdims=True)
        sums = jnp.concatenate(
            [
                jnp.broadcast_to(query_sum, (rows, HEAD_DIM)),
                jnp.broadcast_to(key_sum, (rows, HEAD_DIM)),
            ],
            axis=1,
        )

        @pl.when(pl.program_id(0) == 0)
        def _():
            sum_out[...] = sums

        @pl.when(pl.program_id(0) > 0)
        def _():
            sum_out[...] += sums

    def head(part):
        return pl.BlockSpec((rows, HEAD_DIM), lambda h: (0, part * heads + h))

    def whole(shape):
        return pl.BlockSpec(shape, lambda h: (0, 0))

    pair = pl.BlockSpec((2, HEAD_DIM), lambda h: (0, h))
    return pl.pallas_call(
        kernel,
        grid=(heads,),
        in_specs=[head(0)] * 5
        + [
            head(0),
            head(1),
            whole((rows, 2)),
            pair,
            whole((rows, HEAD_DIM)),
            whole((rows, HEAD_DIM)),
            whole((rows, rows)),
        ],
        out_specs=[head(0)] * 3 + [pair, whole((rows, 2 * HEAD_DIM))],
        out_shape=[
            jax.ShapeDtypeStruct((rows, width), F32),
            jax.ShapeDtypeStruct((rows, width), F32),
            jax.ShapeDtypeStruct((rows, width), BF16),
            jax.ShapeDtypeStruct((2, width), F32),
            jax.ShapeDtypeStruct((rows, 2 * HEAD_DIM), F32),
        ],
        compiler_params=pltpu.CompilerParams(vmem_limit_bytes=48 << 20),
        cost_estimate=pl.CostEstimate(flops=0, bytes_accessed=0, transcendentals=0),
        name="attend_back",
    )(
        grads, query_b, key_b, value_b, log_total, projected, projected, scales, gains,
        cosine, sine_rows, hidden_pairs,
    )


def norms_back(query_turn, key_turn, value_grad, projected, scales, means, gains):
    rows, width = query_turn.shape

    def kernel(query, key, value, projected_ref, scale_ref, mean_ref, gain_ref, out):
        for i, turn in enumerate((query, key)):
            at = slice(i * width, (i + 1) * width)
            scale = scale_ref[:, i : i + 1]
            normed = projected_ref[:, at] * scale
            out[:, at] = (
                scale * (turn[...] * gain_ref[i : i + 1, :] - normed * mean_ref[:, i : i + 1])
            ).astype(BF16)
        out[:, 2 * width :] = value[...]

    return pl.pallas_call(
        kernel,
        out_shape=jax.ShapeDtypeStruct((rows, 3 * width), BF16),
        compiler_params=pltpu.CompilerParams(vmem_limit_bytes=48 << 20),
        cost_estimate=pl.CostEstimate(flops=0, bytes_accessed=0, transcendentals=0),
        name="norms_back",
    )(query_turn, key_turn, value_grad, projected, scales, means, gains)


def expert_rows(rows, cot, w_gate_up, w_down, w_router, expert, senders, blocks):
    count, experts = rows.shape[0], w_router.shape[1]
    tile = FF // 2
    steps = FF // tile
    extra = -(-2 * experts // 128) * 128
    piece = count // (senders * blocks)

    def kernel(expert_ref, rows_ref, cot_ref, wg_ref, wu_ref, wd_ref, wr_ref, *refs):
        row_refs = refs[:blocks]
        act_ref, gg_ref, ug_ref, gate_ref, row_sum, gate_grad = refs[blocks:]
        step = pl.program_id(0)
        row_block = rows_ref[...]

        @pl.when(step == 0)
        def _():
            logits = dot(row_block, wr_ref[...])
            shifted = jnp.exp(logits - jnp.max(logits, axis=-1, keepdims=True))
            router = shifted / jnp.sum(shifted, axis=-1, keepdims=True)
            lane = lax.broadcasted_iota(jnp.int32, router.shape, 1)
            own = jnp.sum(jnp.where(lane == expert_ref[0], router, 0.0), axis=-1, keepdims=True)
            gate_ref[...] = jnp.broadcast_to(own, gate_ref.shape)

        gate = gate_ref[:, :1]
        gate_part = dot(row_block, wg_ref[...])
        up_part = dot(row_block, wu_ref[...])
        cot_act = dot_bt(cot_ref[...], wd_ref[...])
        sigmoid_gate = jax.nn.sigmoid(gate_part)
        swish = gate_part * sigmoid_gate
        activated = (swish * up_part).astype(BF16)
        act_grad = gate * cot_act
        gate_part_grad = (
            act_grad * up_part * sigmoid_gate * (1.0 + gate_part * (1.0 - sigmoid_gate))
        ).astype(BF16)
        up_part_grad = (act_grad * swish).astype(BF16)
        act_ref[...] = activated
        gg_ref[...] = gate_part_grad
        ug_ref[...] = up_part_grad
        row_part = dot_bt(gate_part_grad, wg_ref[...]) + dot_bt(up_part_grad, wu_ref[...])
        part = jnp.sum(cot_act * activated.astype(F32), axis=-1, keepdims=True)
        part = jnp.broadcast_to(part, gate_grad.shape)

        @pl.when(step == 0)
        def _():
            row_sum[...] = row_part
            gate_grad[...] = part

        @pl.when(step > 0)
        def _():
            row_sum[...] += row_part
            gate_grad[...] += part

        @pl.when(step == steps - 1)
        def _():
            lane = lax.broadcasted_iota(jnp.int32, (piece, extra), 1)
            for j in range(senders):
                for i in range(blocks):
                    at = pl.ds((j * blocks + i) * piece, piece)
                    row_refs[i][j, :, :D] = row_sum[at, :].astype(BF16)
                    both = jnp.broadcast_to(gate_grad[at, :1], (piece, extra))
                    high = both.astype(BF16).astype(F32)
                    row_refs[i][j, :, D:] = jnp.where(
                        lane == expert_ref[0],
                        high,
                        jnp.where(lane == experts + expert_ref[0], both - high, 0.0),
                    ).astype(BF16)

    def whole(shape):
        return pl.BlockSpec(shape, lambda j, at: (0, 0))

    columns = pl.BlockSpec((count, tile), lambda j, at: (0, j))
    return pl.pallas_call(
        kernel,
        grid_spec=pltpu.PrefetchScalarGridSpec(
            num_scalar_prefetch=1,
            grid=(steps,),
            in_specs=[
                whole((count, D)),
                whole((count, D)),
                pl.BlockSpec((D, tile), lambda j, at: (0, j)),
                pl.BlockSpec((D, tile), lambda j, at: (0, steps + j)),
                pl.BlockSpec((tile, D), lambda j, at: (j, 0)),
                whole((D, experts)),
            ],
            out_specs=[pl.BlockSpec((senders, piece, D + extra), lambda j, at: (0, 0, 0))] * blocks
            + [columns, columns, columns, whole((count, 128))],
            scratch_shapes=[pltpu.VMEM((count, D), F32), pltpu.VMEM((count, 128), F32)],
        ),
        out_shape=[jax.ShapeDtypeStruct((senders, piece, D + extra), BF16)] * blocks
        + [
            jax.ShapeDtypeStruct((count, FF), BF16),
            jax.ShapeDtypeStruct((count, FF), BF16),
            jax.ShapeDtypeStruct((count, FF), BF16),
            jax.ShapeDtypeStruct((count, 128), F32),
        ],
        compiler_params=pltpu.CompilerParams(vmem_limit_bytes=56 << 20),
        cost_estimate=pl.CostEstimate(flops=0, bytes_accessed=0, transcendentals=0),
        name="expert",
    )(expert, rows, cot, w_gate_up, w_gate_up, w_down, w_router)


def expert_outs(acts, gates, cot, w_down):
    count = acts.shape[0]
    tile = count // 2

    def kernel(act_ref, gate_ref, cot_ref, wd_ref, mix_ref, route_ref):
        gate = gate_ref[:, :1]
        out = dot(act_ref[...], wd_ref[...]).astype(BF16)
        mix_ref[...] = (gate * out.astype(F32)).astype(BF16)
        route_ref[...] = (gate * cot_ref[...].astype(F32)).astype(BF16)

    def rows_of(columns):
        return pl.BlockSpec((tile, columns), lambda i: (i, 0))

    return pl.pallas_call(
        kernel,
        grid=(count // tile,),
        in_specs=[rows_of(FF), rows_of(128), rows_of(D), pl.BlockSpec((FF, D), lambda i: (0, 0))],
        out_specs=[rows_of(D), rows_of(D)],
        out_shape=[jax.ShapeDtypeStruct((count, D), BF16)] * 2,
        compiler_params=pltpu.CompilerParams(vmem_limit_bytes=56 << 20),
        cost_estimate=pl.CostEstimate(
            flops=2 * count * FF * D, bytes_accessed=6 * count * D + 2 * FF * D, transcendentals=0
        ),
        name="expert_outs",
    )(acts, gates, cot, w_down)


def weight_grad(lefts, rights, part, rows_out, arrived=()):
    blocks, parts = len(lefts), len(rights[0])
    depth = lefts[0].shape[0]
    tile = min(256, rows_out)
    tiles = rows_out // tile
    widths = [v.shape[1] for v in rights[0]]

    def kernel(part_ref, *refs):
        left, right, out = refs[:blocks], refs[blocks : blocks * (1 + parts)], refs[-1]
        at = 0
        for p in range(parts):
            total = dot_at(left[0][...], right[p][...])
            for b in range(1, blocks):
                total = total + dot_at(left[b][...], right[b * parts + p][...])
            for more in refs[blocks * (1 + parts) : -1]:
                total = total + more[:, at : at + widths[p]].astype(F32)
            out[:, at : at + widths[p]] = total.astype(out.dtype)
            at += widths[p]

    row_block = pl.BlockSpec((tile, sum(widths)), lambda i, at: (i, 0))
    return pl.pallas_call(
        kernel,
        grid_spec=pltpu.PrefetchScalarGridSpec(
            num_scalar_prefetch=1,
            grid=(tiles,),
            in_specs=[pl.BlockSpec((depth, tile), lambda i, at: (0, at[0] * tiles + i))] * blocks
            + [
                pl.BlockSpec((depth, w), lambda i, at: (0, 0))
                for _ in range(blocks)
                for w in widths
            ]
            + [row_block] * len(arrived),
            out_specs=row_block,
        ),
        out_shape=jax.ShapeDtypeStruct((rows_out, sum(widths)), F32 if arrived else BF16),
        compiler_params=pltpu.CompilerParams(vmem_limit_bytes=56 << 20),
        cost_estimate=pl.CostEstimate(
            flops=4 * blocks * depth * rows_out * sum(widths),
            bytes_accessed=2 * blocks * depth * (rows_out + sum(widths)) + 4 * rows_out * sum(widths),
            transcendentals=0,
        ),
        name="weight_grad",
    )(part.reshape(1).astype(jnp.int32), *lefts, *[v for r in rights for v in r], *arrived)


def body(
    prompt_x,
    cont_x,
    cont_ids,
    routes,
    qkv_weight,
    out_weight,
    router_weight,
    norm_gains,
    gate_up_weight,
    down_weight,
    prompt_cot,
    cont_cot,
):
    n_dp, n_ctx, n_exp = lax.axis_size("dp"), lax.axis_size("ctx"), lax.axis_size("exp")
    d, c, z = lax.axis_index("dp"), lax.axis_index("ctx"), lax.axis_index("exp")
    prompt_len = prompt_x.shape[1]
    cont_len = cont_x.shape[1]
    rows = prompt_len + cont_len
    prompt_total = prompt_len * n_ctx
    experts = router_weight.shape[1]
    capacity = rows * TOP * 17 // (16 * experts)
    score_scale = HEAD_DIM ** (-0.5)
    shard = qkv_weight.shape[0]
    heads_own = HEADS // n_ctx
    width = heads_own * HEAD_DIM
    head_groups = n_dp if (D // (n_dp * n_ctx)) % HEAD_DIM == 0 else 1
    head_run = D // (head_groups * n_ctx)
    own_expert = c * n_exp + z

    def ctx_swap(x, k):
        return lax.ppermute(x, "ctx", [(i, i ^ k) for i in range(n_ctx)])

    def ctx_trade(x):
        return lax.all_to_all(x, "ctx", 0, 0, tiled=True)

    def ctx_gather(x):
        return ctx_trade(jnp.broadcast_to(x[None], (n_ctx,) + x.shape))

    def exp_shift(x, s):
        return lax.ppermute(x, "exp", [(i, (i + s) % n_exp) for i in range(n_exp)])

    def dp_shift(x, m):
        return lax.ppermute(x, "dp", [(i, (i + m) % n_dp) for i in range(n_dp)])

    def part_of(x, axis, at):
        return lax.dynamic_index_in_dim(x, at, axis, keepdims=False)

    def place(buffer, x, *index):
        start, shape = [], []
        for at, size in zip(index, buffer.shape):
            start.append(0 if at is None else at)
            shape.append(size if at is None else 1)
        shape += buffer.shape[len(index) :]
        start += [0] * (buffer.ndim - len(index))
        return lax.dynamic_update_slice(buffer, x.reshape(shape), start)

    def gate(x, *others):
        out = lax.optimization_barrier((x,) + others)[0]
        return list(out) if isinstance(out, tuple) else out

    mark = jnp.full((8, 128), d, jnp.int32).astype(F32)

    def hand_on(in_ref, out_ref):
        out_ref[...] = in_ref[...]

    def fence(*values):
        nonlocal mark
        mark = pl.pallas_call(
            hand_on,
            out_shape=jax.ShapeDtypeStruct(mark.shape, mark.dtype),
            cost_estimate=pl.CostEstimate(
                flops=2 * 10**11, bytes_accessed=0, transcendentals=0
            ),
            name="fence",
        )(gate(mark, *values))

    def after(*values):
        out = lax.optimization_barrier(values + (mark,))
        return out[0] if len(values) == 1 else out[:-1]

    def by_owner(v):
        runs = v.shape[1] // (n_ctx * head_run)
        return jnp.stack(
            [
                jnp.concatenate(
                    [
                        v[:, (i * n_ctx + j) * head_run : (i * n_ctx + j + 1) * head_run]
                        for i in range(runs)
                    ],
                    axis=1,
                )
                for j in range(n_ctx)
            ]
        )

    def all_owners(v):
        runs = v.shape[2] // head_run
        return jnp.concatenate(
            [
                v[j][:, i * head_run : (i + 1) * head_run]
                for i in range(runs)
                for j in range(n_ctx)
            ],
            axis=1,
        )

    x_own = jnp.concatenate([prompt_x[0], cont_x[0]], axis=0)
    cot_own = jnp.concatenate([prompt_cot[0], cont_cot[0]], axis=0)

    small_width = experts + norm_gains.shape[1]
    route_width = -(-rows * TOP // shard)
    route_cols = routes[0, 0].T.astype(BF16).reshape(-1)
    route_cols = jnp.pad(route_cols, (0, route_width * shard - rows * TOP)).reshape(shard, -1)
    extra = jnp.concatenate(
        [
            router_weight,
            norm_gains,
            jnp.broadcast_to(cont_ids[0].astype(BF16), (shard, cont_len)),
            route_cols,
        ],
        axis=1,
    )
    extra_width = -(-extra.shape[1] // 128) * 128
    extra = jnp.pad(extra, ((0, 0), (0, extra_width - extra.shape[1])))
    all_width = 3 * width + extra_width
    runs = 3 * width // head_run


    def pack(w_ref, extra_ref, out_ref):
        for j in range(n_ctx):
            for i in range(runs):
                out_ref[j, :, i * head_run : (i + 1) * head_run] = w_ref[
                    :, (i * n_ctx + j) * head_run : (i * n_ctx + j + 1) * head_run
                ]
            out_ref[j, :, 3 * width :] = extra_ref[...]

    packed_w = pl.pallas_call(
        pack, out_shape=jax.ShapeDtypeStruct((n_ctx, shard, all_width), BF16), name="pack"
    )(qkv_weight, extra)
    slab = ctx_trade(packed_w)
    out_blocks = [out_weight] + [exp_shift(out_weight, s) for s in range(1, n_exp)]
    fence(packed_w)

    def by_exp(v):
        shaped = v.reshape(v.shape[:-1] + (n_dp, n_ctx, n_exp, shard))
        return jnp.swapaxes(shaped, -3, -2).reshape(v.shape)

    def from_exp(v):
        shaped = v.reshape(v.shape[:-1] + (n_dp, n_exp, n_ctx, shard))
        return jnp.swapaxes(shaped, -3, -2).reshape(v.shape)

    x_turned = by_exp(x_own)
    out_blocks = after(*out_blocks)
    out_exp = jnp.zeros((n_exp, shard, D), BF16)
    for j in range(n_exp):
        out_exp = place(out_exp, out_blocks[j], (z - j) % n_exp)

    slab = after(slab)
    ids_at = 3 * width + small_width
    ids = slab[:, 0, ids_at : ids_at + cont_len].astype(F32).astype(jnp.int32)
    w_blocks = [slab] + [exp_shift(slab, s) for s in range(1, n_exp)]
    w_sets = [[dp_shift(slab, m)] for m in range(1, n_dp)]
    out_ctx = ctx_gather(gate(out_exp, slab))
    fence(slab, out_exp)
    out_ctx = after(out_ctx)
    x_sent = gate(x_turned, out_ctx)
    x_all = ctx_gather(x_sent)
    fence(x_sent)

    x_all = after(x_all).reshape(n_ctx * rows, D).astype(F32)
    scale_in = row_scale(x_all)
    w_blocks = gate(tuple(w_blocks), scale_in)
    for m in range(1, n_dp):
        w_sets[m - 1] += [dp_shift(v, m) for v in w_blocks[1:]]
    cot_blocks = [cot_own]
    routes_at = ids_at + cont_len
    places = jnp.stack(
        [(d - m) % n_dp for m in range(n_dp)] + [(z - s) % n_exp for s in range(n_exp)]
    ).astype(jnp.int32)

    def assemble(at_ref, *refs):
        blocks, (w_ref, small_ref) = refs[: n_dp * n_exp], refs[n_dp * n_exp :]
        for m in range(n_dp):
            for s in range(n_exp):
                block = blocks[m * n_exp + s]
                w_ref[at_ref[m], at_ref[n_dp + s]] = block[:, :, : 3 * width]
                small_ref[at_ref[m], at_ref[n_dp + s]] = block[:, :, 3 * width :]

    in_vmem = pl.BlockSpec(memory_space=pltpu.VMEM)
    w_qkv, w_small = pl.pallas_call(
        assemble,
        in_specs=[pl.BlockSpec(memory_space=pltpu.SMEM)] + [in_vmem] * (n_dp * n_exp),
        out_specs=[in_vmem] * 2,
        out_shape=[
            jax.ShapeDtypeStruct((n_dp, n_exp, n_ctx, shard, 3 * width), BF16),
            jax.ShapeDtypeStruct((n_dp, n_exp, n_ctx, shard, extra_width), BF16),
        ],
        compiler_params=pltpu.CompilerParams(vmem_limit_bytes=56 << 20),
        cost_estimate=pl.CostEstimate(flops=0, bytes_accessed=0, transcendentals=0),
        name="assemble",
    )(places, *w_blocks, *[v for w_set in w_sets for v in w_set])
    w_qkv = w_qkv.reshape(D, 3 * width)
    w_small = jnp.swapaxes(w_small, 1, 2).reshape(D, extra_width)
    w_router = w_small[:, :experts]
    gains_t = w_small[:, experts:small_width].astype(F32).T
    gain_in, gain_ffn = gains_t[0], gains_t[3]

    def own_features(v):
        shaped = v.reshape(v.shape[:-1] + (head_groups, n_ctx, head_run))
        return part_of(shaped, v.ndim, c).reshape(v.shape[:-1] + (width,))

    gain_query, gain_key = own_features(gains_t[1]), own_features(gains_t[2])

    upper = (
        jnp.arange(rows, dtype=jnp.int32)[:, None] < jnp.arange(rows, dtype=jnp.int32)[None, :]
    ).astype(BF16)
    send_experts = (jnp.arange(n_ctx) * n_exp + z).astype(F32)

    def spread_of(route_cols):
        named = jnp.any(
            route_cols.astype(F32)[None] == send_experts[:, None, None], axis=1
        )
        rank = dot(named.astype(BF16), upper)
        slots = jnp.where(named, rank, -1.0)
        return (
            (slots[:, None, :] == jnp.arange(capacity, dtype=F32)[None, :, None])
            .astype(BF16)
            .reshape(n_ctx * capacity, rows)
        )

    spread = [spread_of(routes[0, 0].T)]

    def spread_pair(blocks):
        n = len(blocks)
        parts = []
        for i, s in enumerate(blocks):
            part = spread[s].reshape(n_ctx, 1, capacity, rows)
            parts.append(jnp.pad(part, ((0, 0), (0, 0), (0, 0), (i * rows, (n - 1 - i) * rows))))
        return jnp.concatenate(parts, axis=1).reshape(n_ctx * n * capacity, n * rows)

    def pack_of(spread_rows, blocks):
        n = len(blocks)
        sent = dot(spread_rows, blocks[0] if n == 1 else jnp.concatenate(blocks, axis=0))
        return sent.astype(BF16).reshape(n_ctx, n, capacity, -1)

    def pack_cot(blocks):
        return pack_of(
            spread_pair(blocks) if len(blocks) > 1 else spread[blocks[0]],
            [cot_blocks[s] for s in blocks],
        )

    def trade_pieces(pieces):
        return [ctx_swap(pieces[k], k) if k else pieces[k] for k in range(n_ctx)]

    def in_order(pieces):
        whole = jnp.zeros((n_ctx,) + pieces[0].shape, pieces[0].dtype)
        for k in range(n_ctx):
            whole = place(whole, pieces[k], c ^ k)
        return whole

    w_gate_up = gate_up_weight[0]
    w_down = down_weight[0]
    pairs = [list(range(i, i + 2)) for i in range(0, n_exp, 2)]

    total_rows = rows * n_ctx
    index = jnp.arange(rows, dtype=jnp.int32)
    in_prompt = index < prompt_len
    position, seg_rows, order = [], [], []
    for j in range(n_ctx):
        seg = ids[j]
        starts = jnp.sum((seg[None, :] < seg[:, None]).astype(jnp.int32), axis=1)
        within = jnp.arange(cont_len, dtype=jnp.int32) - starts
        at = j * prompt_len
        position.append(jnp.concatenate([at + index[:prompt_len], prompt_total + within]))
        order.append(jnp.where(in_prompt, at + index, index))
        seg_rows.append(
            jnp.concatenate([jnp.full((prompt_len,), -1, jnp.int32), j * 64 + seg])
        )
    position = jnp.concatenate(position).astype(F32)
    order = jnp.concatenate(order)
    seg_of = jnp.concatenate(seg_rows)
    is_prompt = jnp.concatenate([in_prompt] * n_ctx)
    before = order[None, :] <= order[:, None]
    allowed = jnp.where(
        is_prompt[:, None],
        is_prompt[None, :] & before,
        is_prompt[None, :] | ((seg_of[None, :] == seg_of[:, None]) & before),
    )
    hidden_pairs = jnp.where(allowed, 0.0, -1.0)
    cosine, sine_rows = rope_tables(position, HEAD_DIM // 2)

    cot_sent = gate(pack_cot([0]), scale_in)
    cot_trade = ctx_trade(cot_sent)
    fence(cot_sent, w_qkv)
    hidden_in = after((x_all * after(scale_in) * by_exp(gain_in)).astype(BF16))
    projected = dot(hidden_in, w_qkv)

    def ctx_sum(total):
        k = 1
        while k < n_ctx:
            total = total + ctx_swap(total, k)
            k *= 2
        return total

    raw_query, raw_key = projected[:, :width], projected[:, width : 2 * width]
    squares = jnp.stack([jnp.sum(raw_query * raw_query, axis=-1), jnp.sum(raw_key * raw_key, axis=-1)])
    cot_flight = [exp_shift(gate(cot_blocks[0], squares), s) for s in range(1, n_exp)]
    scales = lax.rsqrt(ctx_sum(squares) / D + NORM_EPS)
    spread += [
        spread_of(
            part_of(v[..., routes_at : routes_at + route_width], 0, c)
            .reshape(-1)[: rows * TOP]
            .reshape(TOP, rows)
        )
        for v in gate(tuple(w_blocks[1:]), squares)
    ]
    out_ctx = gate(out_ctx, scales)
    out_halves = [out_ctx] + [dp_shift(out_ctx, m) for m in range(1, n_dp)]
    fence(scales, out_ctx)
    scales = after(scales)
    scales = scales.T
    head_gains = jnp.stack([gain_query, gain_key])
    mixed_heads, *kept = attend(projected, scales, head_gains, cosine, sine_rows, hidden_pairs)

    mixed_heads = gate(mixed_heads, cot_trade)
    mixed = ctx_trade(mixed_heads.reshape(n_ctx, rows, width))
    cot_own_rows = cot_trade
    spreads = [spread_pair(pair) for pair in pairs]
    fence(mixed_heads, *spreads)
    mixed = after(mixed)
    cot_blocks += gate(tuple(cot_flight), mixed)
    mixed = all_owners(mixed)
    cot_sent = gate(pack_cot(list(range(1, n_exp))), mixed)
    cot_trade = ctx_trade(cot_sent)
    fence(mixed, cot_sent)
    mixed = after(mixed)
    half = D // n_dp
    mixed_halves = jnp.stack([mixed[:, i * half : (i + 1) * half] for i in range(n_dp)])
    inputs = x_own.astype(F32)
    mid_rows = inputs
    for m in range(n_dp):
        mid_rows = mid_rows + dot(
            part_of(mixed_halves, 0, (d - m) % n_dp), out_halves[m].reshape(half, D)
        )
    scale_ffn = row_scale(mid_rows)
    normed_ffn = mid_rows * scale_ffn
    hidden_ffn = (normed_ffn * gain_ffn).astype(BF16)

    def softmax(logits):
        shifted = jnp.exp(logits - jnp.max(logits, axis=-1, keepdims=True))
        return shifted / jnp.sum(shifted, axis=-1, keepdims=True)

    cot_rows, made = [], []

    def towards(blocks, back, spread_rows):
        return dot_at(spread_rows, back.reshape(spread_rows.shape[0], -1))

    def home(s, summed):
        return exp_shift(summed, n_exp - s)

    near = exp_shift(hidden_ffn, 1)
    fence(hidden_ffn)

    near = after(near)
    far = [exp_shift(gate(hidden_ffn, near), s) for s in range(2, n_exp)]
    cot_trade = after(cot_trade)
    sent = gate(pack_of(spreads[0], [hidden_ffn, near]), cot_trade)
    plane = ctx_trade(sent)
    fence(near, sent)

    cot_back = [cot_own_rows[:, 0]] + [after(cot_trade)[:, s] for s in range(n_exp - 1)]
    for pair in pairs:
        cot_rows.append(jnp.stack([cot_back[s] for s in pair], axis=1).reshape(-1, D))
    plane = after(plane)
    far = gate(tuple(after(*far)), plane)
    sent = pack_of(spreads[1], far)
    plane_next = ctx_trade(sent)
    fence(sent, plane)

    expert_at = own_expert.reshape(1).astype(jnp.int32)

    def compute(i, in_rows):
        in_rows = in_rows.reshape(-1, D)
        out = expert_rows(
            in_rows, cot_rows[i], w_gate_up, w_down, w_router, expert_at, n_ctx, 2
        )
        made.append([in_rows] + list(out))

    compute(0, plane)
    sent = gate(made[0][2], plane_next)
    back = ctx_trade(sent)
    fence(sent)

    compute(1, after(plane_next))
    back = gate(after(back), made[1][1])
    leaving = towards([1], back, spread[1]).astype(BF16)
    homes = [home(1, leaving)]
    sent = gate(made[1][1], back)
    back = ctx_trade(sent)
    fence(sent, leaving)

    mix_sent, route_grads = [], []

    def weigh(i):
        acts, gates = after(made[i][3], made[i][6])
        mix, route = expert_outs(acts, gates, cot_rows[i], w_down)
        mix_sent.append(mix.reshape(n_ctx, 2, capacity, D))
        route_grads.append(route)

    def grads_sent(lefts, rights, rows_out):
        sent = [weight_grad(lefts, rights, half_rows[m], rows_out) for m in range(1, n_dp)]
        return sent, [dp_shift(v, m + 1) for m, v in enumerate(sent)]

    half_rows = [(d + m) % n_dp for m in range(n_dp)]
    weigh(0)
    back = gate(after(back), mix_sent[0])
    leaving = towards([2], back, spread[2]).astype(BF16)
    homes.append(home(2, leaving))
    sent = gate(made[1][2], back)
    back = ctx_trade(sent)
    fence(sent, leaving)

    weigh(1)
    back = gate(after(back), mix_sent[1])
    leaving = towards([3], back, spread[3]).astype(BF16)
    homes.append(home(3, leaving))
    sent = gate(made[0][1], back)
    back = ctx_trade(sent)
    fence(sent, leaving)

    back = after(back)
    returned = towards([0], back, spread[0])
    fence(returned)
    homes = after(*homes)
    for v in after(*homes):
        returned = returned + v.astype(F32)

    router = softmax(dot(hidden_ffn, w_router))
    prob_grad = returned[:, D : D + experts] + returned[:, D + experts : D + 2 * experts]
    logit_grad = router * (prob_grad - jnp.sum(router * prob_grad, axis=-1, keepdims=True))
    ffn_grad = returned[:, :D] + jnp.dot(logit_grad, w_router.astype(F32).T, precision=HIGHEST_PREC)
    router_grad_t = jnp.einsum(
        "re,rd->ed", logit_grad, hidden_ffn.astype(F32), precision=HIGHEST_PREC
    )
    mid_norm_grad, ffn_gain_grad = norm_back(ffn_grad, normed_ffn, scale_ffn, gain_ffn)
    mid_grad = cot_own.astype(F32) + mid_norm_grad

    attn_grad = mid_grad.astype(BF16)
    grad_halves = jnp.zeros((n_dp, rows, half), BF16)
    for m in range(n_dp):
        grad_halves = place(
            grad_halves,
            dot_bt(attn_grad, out_halves[m].reshape(half, D)).astype(BF16),
            (d - m) % n_dp,
        )
    pieces = by_owner(jnp.concatenate([grad_halves[i] for i in range(n_dp)], axis=1))
    mixed_grad = in_order(trade_pieces([part_of(pieces, 0, c ^ k) for k in range(n_ctx)]))
    sent = gate(mix_sent[1], mixed_grad)
    mix_trade = ctx_trade(sent)
    fence(mixed_grad, sent)
    mixed_grad = after(mixed_grad)
    query_turn, key_turn, value_grad, head_gain_grads, sums = attend_back(
        mixed_grad.reshape(total_rows, width),
        kept,
        projected,
        scales,
        head_gains,
        cosine,
        sine_rows,
        hidden_pairs,
    )
    sums = jnp.stack([sums[:, 0], sums[:, HEAD_DIM]])
    means = ctx_sum(sums) / D
    back = gate(mix_trade, means)
    leaving = towards(pairs[1], back, spreads[1]).astype(BF16)
    mix_homes = [home(2, leaving[:rows]), home(3, leaving[rows:])]
    attn_sent = gate(attn_grad, back)
    attn_grad_all = ctx_gather(attn_sent)
    fence(means, attn_sent, leaving)
    means = after(means)
    proj_grad = norms_back(
        query_turn, key_turn, value_grad, projected, scales, means.T, head_gains
    )

    sent = [
        weight_grad([hidden_in], [[proj_grad]], half_rows[m], half) for m in range(1, n_dp)
    ]
    arrived = [dp_shift(v, m + 1) for m, v in enumerate(sent)]
    fence(*sent)
    hidden_part = dot_bt(gate(proj_grad, *sent), w_qkv).astype(BF16)
    arrived = gate(tuple([after(v) for v in arrived]), hidden_part)
    qkv_dp = weight_grad([hidden_in], [[proj_grad]], half_rows[0], half, arrived)
    qkv_dp = qkv_dp.reshape(n_exp, n_ctx * shard, 3 * width)
    sent = [part_of(qkv_dp, 0, (z - 1) % n_exp).astype(BF16)]

    def ring_step(s, sent):
        arrived = exp_shift(sent, 1)
        return arrived, part_of(qkv_dp, 0, (z - s) % n_exp)

    ring_arrived, ring_part = ring_step(2, sent[0])
    attn_grad_all = gate(attn_grad_all, *sent)
    mix_trade = ctx_trade(gate(mix_sent[0], attn_grad_all))
    attn_grad_all = attn_grad_all.reshape(total_rows, D)
    fence(attn_grad_all, *sent)

    mix_homes = after(*mix_homes)
    in_rows, acts, gate_grads, up_grads = [after(*[v[i] for v in made]) for i in (0, 3, 4, 5)]
    acts = gate(tuple(acts), *mix_homes)
    gate_up_grads = [[gate_grads[i], up_grads[i]] for i in range(len(pairs))]
    out_rows = width // n_dp
    if head_groups == n_dp:
        out_left = [gate(after(mixed_heads), *mix_homes)]
        out_sent, out_arrived = grads_sent(out_left, [[attn_grad_all]], out_rows)
        acts = gate(tuple(acts), *out_sent)
    down_sent, down_arrived = grads_sent(acts, [[v] for v in route_grads], FF // n_dp)
    ring_sent = (gate(ring_arrived, *down_sent).astype(F32) + ring_part).astype(BF16)
    ring_arrived, ring_part = ring_step(3, ring_sent)
    in_rows = gate(tuple(in_rows), ring_sent)
    mix_back = gate(after(mix_trade), *down_sent)
    hidden_part = gate(hidden_part, mix_back)
    hidden_trade = ctx_trade(hidden_part.reshape(n_ctx, rows, D))
    if head_groups == n_dp:
        out_left = gate(tuple(out_left), *down_sent)
        out_dp = weight_grad(out_left, [[attn_grad_all]], half_rows[0], out_rows, out_arrived)
        out_dp = out_dp.reshape(n_exp, shard, D)
        in_rows = gate(tuple(in_rows), out_dp)
    gate_up_sent, gate_up_arrived = grads_sent(in_rows, gate_up_grads, D // n_dp)
    ring_sent = (gate(ring_arrived, *gate_up_sent).astype(F32) + ring_part).astype(BF16)
    ring_arrived, ring_part = ring_step(4, ring_sent)
    acts = gate(tuple(acts), ring_sent)
    grad_down = weight_grad(acts, [[v] for v in route_grads], d, FF // n_dp, down_arrived)
    mix_back = gate(mix_back, grad_down)
    leaving = towards(pairs[0], mix_back, spreads[0])
    mix_homes = list(mix_homes) + [leaving[:rows], home(1, leaving[rows:].astype(BF16))]
    in_rows = gate(tuple(in_rows), leaving)
    grad_gate_up = weight_grad(in_rows, gate_up_grads, d, D // n_dp, gate_up_arrived)

    hidden_grad = from_exp(jnp.sum(hidden_trade.astype(F32), axis=0))
    scale_own = lax.dynamic_slice_in_dim(scale_in, c * rows, rows, axis=0)
    in_norm_grad, in_gain_grad = norm_back(hidden_grad, inputs * scale_own, scale_own, gain_in)
    input_grad = mid_grad + in_norm_grad

    def spread_features(v):
        shaped = jnp.zeros((head_groups, n_ctx, head_run), F32)
        return place(shaped, v.reshape(head_groups, 1, head_run), None, c).reshape(1, D)

    small_grad = jnp.concatenate(
        [
            router_grad_t,
            in_gain_grad[None],
            spread_features(head_gain_grads[0]),
            spread_features(head_gain_grads[1]),
            ffn_gain_grad[None],
        ],
        axis=0,
    )
    count = small_grad.shape[0]
    part = small_grad.reshape(count, n_dp, n_ctx, n_exp, shard).transpose(1, 2, 3, 0, 4)
    late_d = mark[0, 0].astype(jnp.int32)
    total = lax.dynamic_index_in_dim(part, late_d, 0, keepdims=False)
    for m in range(1, n_dp):
        total = total + dp_shift(
            lax.dynamic_index_in_dim(part, (late_d + m) % n_dp, 0, keepdims=False), m
        )
    part = total
    if head_groups == n_dp:
        out_sent = gate(out_dp.astype(BF16), hidden_trade)
        out_trade = lax.all_to_all(out_sent, "exp", 0, 0, tiled=True)
        out_trade = gate(out_trade, grad_gate_up)
        part = jnp.sum(ctx_trade(gate(part, out_trade)), axis=0)
        grad_out = jnp.sum(out_trade.astype(F32), axis=0)
    else:
        part = jnp.sum(ctx_trade(part), axis=0)
        grad_out = lax.psum_scatter(
            dot_at(mixed, attn_grad), ("dp", "ctx", "exp"), scatter_dimension=0, tiled=True
        )
    total = lax.dynamic_index_in_dim(part, z, 0, keepdims=False)
    for s in range(1, n_exp):
        piece = lax.dynamic_index_in_dim(part, (z + s) % n_exp, 0, keepdims=False)
        total = total + exp_shift(piece, s)
    small_sum = total.T
    mix_homes = gate(tuple(mix_homes), grad_out)
    mixture = mix_homes[2] + sum(v.astype(F32) for v in mix_homes[:2] + mix_homes[3:])
    final_rows = (mid_rows + mixture).astype(BF16)

    qkv_exp = gate(ring_arrived, final_rows, part).astype(F32) + ring_part
    qkv_exp = qkv_exp.reshape(n_ctx, shard, 3 * width)
    grad_qkv = all_owners(ctx_trade(qkv_exp.astype(BF16)).astype(F32))

    return (
        final_rows[:prompt_len][None],
        final_rows[prompt_len:][None],
        input_grad[:prompt_len][None],
        input_grad[prompt_len:][None],
        grad_qkv,
        grad_out,
        small_sum[:, :experts],
        small_sum[:, experts:],
        grad_gate_up[None],
        grad_down[None],
    )


def solution(mesh):
    return jax.shard_map(
        body,
        mesh=mesh,
        in_specs=(
            P(("dp", "exp"), "ctx", None),
            P(("dp", "exp"), "ctx", None),
            P(("dp", "exp"), "ctx", None),
            P(("dp", "exp"), "ctx", None, None),
            P(("dp", "ctx", "exp"), None),
            P(("dp", "ctx", "exp"), None),
            P(("dp", "ctx", "exp"), None),
            P(("dp", "ctx", "exp"), None),
            P(("ctx", "exp"), None, None),
            P(("ctx", "exp"), None, None),
            P(("dp", "exp"), "ctx", None),
            P(("dp", "exp"), "ctx", None),
        ),
        out_specs=(
            P(("dp", "exp"), "ctx", None),
            P(("dp", "exp"), "ctx", None),
            P(("dp", "exp"), "ctx", None),
            P(("dp", "exp"), "ctx", None),
            P(("dp", "ctx", "exp"), None),
            P(("dp", "ctx", "exp"), None),
            P(("dp", "ctx", "exp"), None),
            P(("dp", "ctx", "exp"), None),
            P(("ctx", "exp"), "dp", None),
            P(("ctx", "exp"), "dp", None),
        ),
        check_vma=False,
    )
```

```python
import jax
import jax.numpy as jnp
from jax import lax
from jax.experimental import pallas as pl
from jax.experimental.pallas import tpu as pltpu
from jax.sharding import PartitionSpec as P

D = 2048
HEADS = 16
HEAD_DIM = 128
FF = 1024
TOP = 8

NORM_EPS = 1e-05
ROPE_BASE = 10000.0
NEGATIVE = -1e30
HIGHEST_PREC = lax.Precision.HIGHEST
F32 = jnp.float32
BF16 = jnp.bfloat16


def row_scale(values):
    return lax.rsqrt(jnp.mean(values * values, axis=-1, keepdims=True) + NORM_EPS)


def rope_tables(position, half_dim):
    inverse = ROPE_BASE ** (-jnp.arange(half_dim, dtype=F32) / half_dim)
    angles = position[:, None] * inverse[None, :]
    cosine, sine_rows = jnp.cos(angles), jnp.sin(angles)
    return (
        jnp.concatenate([cosine, cosine], axis=1),
        jnp.concatenate([-sine_rows, sine_rows], axis=1),
    )


def norm_back(grad_rows, normed, scale_rows, gain_col):
    grad_normed = grad_rows * gain_col
    grad_input = scale_rows * (
        grad_normed - normed * jnp.mean(grad_normed * normed, axis=-1, keepdims=True)
    )
    return (grad_input, jnp.sum(grad_rows * normed, axis=0))


def dot(a, b):
    return jnp.dot(a, b, preferred_element_type=F32)


def dot_bt(a, b):
    return lax.dot_general(a, b, (((1,), (1,)), ((), ())), preferred_element_type=F32)


def dot_at(a, b):
    return lax.dot_general(a, b, (((0,), (0,)), ((), ())), preferred_element_type=F32)


def attend(projected, scales, gains, cosine, sine_rows, hidden_pairs):
    rows = projected.shape[0]
    width = projected.shape[1] // 3
    heads = width // HEAD_DIM

    def kernel(pq, pk, pv, scale_ref, gain_ref, cos_ref, sin_ref, pair_ref, mixed, q, k, v, total):
        def turned(values):
            return values * cos_ref[...] + pltpu.roll(values, HEAD_DIM // 2, 1) * sin_ref[...]

        query = turned(pq[...] * scale_ref[:, :1] * gain_ref[:1, :]).astype(BF16)
        key = turned(pk[...] * scale_ref[:, 1:2] * gain_ref[1:2, :]).astype(BF16)
        value = pv[...].astype(BF16)
        scores = dot_bt(query, key) * HEAD_DIM ** (-0.5)
        scores = jnp.where(pair_ref[...] < 0.0, NEGATIVE, scores)
        row_max = jnp.max(scores, axis=-1, keepdims=True)
        log_total = row_max + jnp.log(
            jnp.sum(jnp.exp(scores - row_max), axis=-1, keepdims=True)
        )
        mixed[...] = dot(jnp.exp(scores - log_total).astype(BF16), value).astype(BF16)
        q[...], k[...], v[...] = query, key, value
        total[...] = jnp.broadcast_to(log_total, total.shape)

    def head(part):
        return pl.BlockSpec((rows, HEAD_DIM), lambda h: (0, part * heads + h))

    def whole(shape):
        return pl.BlockSpec(shape, lambda h: (0, 0))

    return pl.pallas_call(
        kernel,
        grid=(heads,),
        in_specs=[
            head(0),
            head(1),
            head(2),
            whole((rows, 2)),
            pl.BlockSpec((2, HEAD_DIM), lambda h: (0, h)),
            whole((rows, HEAD_DIM)),
            whole((rows, HEAD_DIM)),
            whole((rows, rows)),
        ],
        out_specs=[head(0)] * 5,
        out_shape=[jax.ShapeDtypeStruct((rows, width), BF16)] * 4
        + [jax.ShapeDtypeStruct((rows, width), F32)],
        compiler_params=pltpu.CompilerParams(vmem_limit_bytes=48 << 20),
        cost_estimate=pl.CostEstimate(flops=0, bytes_accessed=0, transcendentals=0),
        name="attend",
    )(projected, projected, projected, scales, gains, cosine, sine_rows, hidden_pairs)


def attend_back(grads, kept, projected, scales, gains, cosine, sine_rows, hidden_pairs):
    query_b, key_b, value_b, log_total = kept
    rows = projected.shape[0]
    width = projected.shape[1] // 3
    heads = width // HEAD_DIM
    scale = HEAD_DIM ** (-0.5)

    def kernel(
        g, q, k, v, total, pq, pk, scale_ref, gain_ref, cos_ref, sin_ref, pair_ref,
        query_out, key_out, value_out, gain_out, sum_out,
    ):
        def turned_back(values):
            return values * cos_ref[...] - pltpu.roll(values, HEAD_DIM // 2, 1) * sin_ref[...]

        scores = dot_bt(q[...], k[...]) * scale
        scores = jnp.where(pair_ref[...] < 0.0, NEGATIVE, scores)
        attention = jnp.exp(scores - total[:, :1])
        prob_att = dot_bt(g[...], v[...])
        delta = jnp.sum(attention * prob_att, axis=-1, keepdims=True)
        score_grad = (attention * (prob_att - delta)).astype(BF16)
        query = turned_back(dot(score_grad, k[...]) * scale)
        key = turned_back(dot_at(score_grad, q[...]) * scale)
        value_out[...] = dot_at(attention.astype(BF16), g[...]).astype(BF16)
        query_out[...], key_out[...] = query, key
        query_n = query * (pq[...] * scale_ref[:, :1])
        key_n = key * (pk[...] * scale_ref[:, 1:2])
        gain_out[:1, :] = jnp.sum(query_n, axis=0, keepdims=True)
        gain_out[1:2, :] = jnp.sum(key_n, axis=0, keepdims=True)
        query_sum = jnp.sum(query_n * gain_ref[:1, :], axis=-1, keepdims=True)
        key_sum = jnp.sum(key_n * gain_ref[1:2, :], axis=-1, keepdims=True)
        sums = jnp.concatenate(
            [
                jnp.broadcast_to(query_sum, (rows, HEAD_DIM)),
                jnp.broadcast_to(key_sum, (rows, HEAD_DIM)),
            ],
            axis=1,
        )

        @pl.when(pl.program_id(0) == 0)
        def _():
            sum_out[...] = sums

        @pl.when(pl.program_id(0) > 0)
        def _():
            sum_out[...] += sums

    def head(part):
        return pl.BlockSpec((rows, HEAD_DIM), lambda h: (0, part * heads + h))

    def whole(shape):
        return pl.BlockSpec(shape, lambda h: (0, 0))

    pair = pl.BlockSpec((2, HEAD_DIM), lambda h: (0, h))
    return pl.pallas_call(
        kernel,
        grid=(heads,),
        in_specs=[head(0)] * 5
        + [
            head(0),
            head(1),
            whole((rows, 2)),
            pair,
            whole((rows, HEAD_DIM)),
            whole((rows, HEAD_DIM)),
            whole((rows, rows)),
        ],
        out_specs=[head(0)] * 3 + [pair, whole((rows, 2 * HEAD_DIM))],
        out_shape=[
            jax.ShapeDtypeStruct((rows, width), F32),
            jax.ShapeDtypeStruct((rows, width), F32),
            jax.ShapeDtypeStruct((rows, width), BF16),
            jax.ShapeDtypeStruct((2, width), F32),
            jax.ShapeDtypeStruct((rows, 2 * HEAD_DIM), F32),
        ],
        compiler_params=pltpu.CompilerParams(vmem_limit_bytes=48 << 20),
        cost_estimate=pl.CostEstimate(flops=0, bytes_accessed=0, transcendentals=0),
        name="attend_back",
    )(
        grads, query_b, key_b, value_b, log_total, projected, projected, scales, gains,
        cosine, sine_rows, hidden_pairs,
    )


def norms_back(query_turn, key_turn, value_grad, projected, scales, means, gains):
    rows, width = query_turn.shape

    def kernel(query, key, value, projected_ref, scale_ref, mean_ref, gain_ref, out):
        for i, turn in enumerate((query, key)):
            at = slice(i * width, (i + 1) * width)
            scale = scale_ref[:, i : i + 1]
            normed = projected_ref[:, at] * scale
            out[:, at] = (
                scale * (turn[...] * gain_ref[i : i + 1, :] - normed * mean_ref[:, i : i + 1])
            ).astype(BF16)
        out[:, 2 * width :] = value[...]

    return pl.pallas_call(
        kernel,
        out_shape=jax.ShapeDtypeStruct((rows, 3 * width), BF16),
        compiler_params=pltpu.CompilerParams(vmem_limit_bytes=48 << 20),
        cost_estimate=pl.CostEstimate(flops=0, bytes_accessed=0, transcendentals=0),
        name="norms_back",
    )(query_turn, key_turn, value_grad, projected, scales, means, gains)


def expert_rows(rows, cot, w_gate_up, w_down, w_router, expert, senders, blocks):
    count, experts = rows.shape[0], w_router.shape[1]
    tile = FF // 2
    steps = FF // tile
    extra = -(-2 * experts // 128) * 128
    piece = count // (senders * blocks)

    def kernel(expert_ref, rows_ref, cot_ref, wg_ref, wu_ref, wd_ref, wr_ref, *refs):
        row_refs = refs[:blocks]
        act_ref, gg_ref, ug_ref, gate_ref, row_sum, gate_grad = refs[blocks:]
        step = pl.program_id(0)
        row_block = rows_ref[...]

        @pl.when(step == 0)
        def _():
            logits = dot(row_block, wr_ref[...])
            shifted = jnp.exp(logits - jnp.max(logits, axis=-1, keepdims=True))
            router = shifted / jnp.sum(shifted, axis=-1, keepdims=True)
            lane = lax.broadcasted_iota(jnp.int32, router.shape, 1)
            own = jnp.sum(jnp.where(lane == expert_ref[0], router, 0.0), axis=-1, keepdims=True)
            gate_ref[...] = jnp.broadcast_to(own, gate_ref.shape)

        gate = gate_ref[:, :1]
        gate_part = dot(row_block, wg_ref[...])
        up_part = dot(row_block, wu_ref[...])
        cot_act = dot_bt(cot_ref[...], wd_ref[...])
        sigmoid_gate = jax.nn.sigmoid(gate_part)
        swish = gate_part * sigmoid_gate
        activated = (swish * up_part).astype(BF16)
        act_grad = gate * cot_act
        gate_part_grad = (
            act_grad * up_part * sigmoid_gate * (1.0 + gate_part * (1.0 - sigmoid_gate))
        ).astype(BF16)
        up_part_grad = (act_grad * swish).astype(BF16)
        act_ref[...] = activated
        gg_ref[...] = gate_part_grad
        ug_ref[...] = up_part_grad
        row_part = dot_bt(gate_part_grad, wg_ref[...]) + dot_bt(up_part_grad, wu_ref[...])
        part = jnp.sum(cot_act * activated.astype(F32), axis=-1, keepdims=True)
        part = jnp.broadcast_to(part, gate_grad.shape)

        @pl.when(step == 0)
        def _():
            row_sum[...] = row_part
            gate_grad[...] = part

        @pl.when(step > 0)
        def _():
            row_sum[...] += row_part
            gate_grad[...] += part

        @pl.when(step == steps - 1)
        def _():
            lane = lax.broadcasted_iota(jnp.int32, (piece, extra), 1)
            for j in range(senders):
                for i in range(blocks):
                    at = pl.ds((j * blocks + i) * piece, piece)
                    row_refs[i][j, :, :D] = row_sum[at, :].astype(BF16)
                    both = jnp.broadcast_to(gate_grad[at, :1], (piece, extra))
                    high = both.astype(BF16).astype(F32)
                    row_refs[i][j, :, D:] = jnp.where(
                        lane == expert_ref[0],
                        high,
                        jnp.where(lane == experts + expert_ref[0], both - high, 0.0),
                    ).astype(BF16)

    def whole(shape):
        return pl.BlockSpec(shape, lambda j, at: (0, 0))

    columns = pl.BlockSpec((count, tile), lambda j, at: (0, j))
    return pl.pallas_call(
        kernel,
        grid_spec=pltpu.PrefetchScalarGridSpec(
            num_scalar_prefetch=1,
            grid=(steps,),
            in_specs=[
                whole((count, D)),
                whole((count, D)),
                pl.BlockSpec((D, tile), lambda j, at: (0, j)),
                pl.BlockSpec((D, tile), lambda j, at: (0, steps + j)),
                pl.BlockSpec((tile, D), lambda j, at: (j, 0)),
                whole((D, experts)),
            ],
            out_specs=[pl.BlockSpec((senders, piece, D + extra), lambda j, at: (0, 0, 0))] * blocks
            + [columns, columns, columns, whole((count, 128))],
            scratch_shapes=[pltpu.VMEM((count, D), F32), pltpu.VMEM((count, 128), F32)],
        ),
        out_shape=[jax.ShapeDtypeStruct((senders, piece, D + extra), BF16)] * blocks
        + [
            jax.ShapeDtypeStruct((count, FF), BF16),
            jax.ShapeDtypeStruct((count, FF), BF16),
            jax.ShapeDtypeStruct((count, FF), BF16),
            jax.ShapeDtypeStruct((count, 128), F32),
        ],
        compiler_params=pltpu.CompilerParams(vmem_limit_bytes=56 << 20),
        cost_estimate=pl.CostEstimate(flops=0, bytes_accessed=0, transcendentals=0),
        name="expert",
    )(expert, rows, cot, w_gate_up, w_gate_up, w_down, w_router)


def expert_outs(acts, gates, cot, w_down):
    count = acts.shape[0]
    tile = count // 2

    def kernel(act_ref, gate_ref, cot_ref, wd_ref, mix_ref, route_ref):
        gate = gate_ref[:, :1]
        out = dot(act_ref[...], wd_ref[...]).astype(BF16)
        mix_ref[...] = (gate * out.astype(F32)).astype(BF16)
        route_ref[...] = (gate * cot_ref[...].astype(F32)).astype(BF16)

    def rows_of(columns):
        return pl.BlockSpec((tile, columns), lambda i: (i, 0))

    return pl.pallas_call(
        kernel,
        grid=(count // tile,),
        in_specs=[rows_of(FF), rows_of(128), rows_of(D), pl.BlockSpec((FF, D), lambda i: (0, 0))],
        out_specs=[rows_of(D), rows_of(D)],
        out_shape=[jax.ShapeDtypeStruct((count, D), BF16)] * 2,
        compiler_params=pltpu.CompilerParams(vmem_limit_bytes=56 << 20),
        cost_estimate=pl.CostEstimate(
            flops=2 * count * FF * D, bytes_accessed=6 * count * D + 2 * FF * D, transcendentals=0
        ),
        name="expert_outs",
    )(acts, gates, cot, w_down)


def weight_grad(lefts, rights, part, rows_out, arrived=()):
    blocks, parts = len(lefts), len(rights[0])
    depth = lefts[0].shape[0]
    tile = min(256, rows_out)
    tiles = rows_out // tile
    widths = [v.shape[1] for v in rights[0]]

    def kernel(part_ref, *refs):
        left, right, out = refs[:blocks], refs[blocks : blocks * (1 + parts)], refs[-1]
        at = 0
        for p in range(parts):
            total = dot_at(left[0][...], right[p][...])
            for b in range(1, blocks):
                total = total + dot_at(left[b][...], right[b * parts + p][...])
            for more in refs[blocks * (1 + parts) : -1]:
                total = total + more[:, at : at + widths[p]].astype(F32)
            out[:, at : at + widths[p]] = total.astype(out.dtype)
            at += widths[p]

    row_block = pl.BlockSpec((tile, sum(widths)), lambda i, at: (i, 0))
    return pl.pallas_call(
        kernel,
        grid_spec=pltpu.PrefetchScalarGridSpec(
            num_scalar_prefetch=1,
            grid=(tiles,),
            in_specs=[pl.BlockSpec((depth, tile), lambda i, at: (0, at[0] * tiles + i))] * blocks
            + [
                pl.BlockSpec((depth, w), lambda i, at: (0, 0))
                for _ in range(blocks)
                for w in widths
            ]
            + [row_block] * len(arrived),
            out_specs=row_block,
        ),
        out_shape=jax.ShapeDtypeStruct((rows_out, sum(widths)), F32 if arrived else BF16),
        compiler_params=pltpu.CompilerParams(vmem_limit_bytes=56 << 20),
        cost_estimate=pl.CostEstimate(
            flops=4 * blocks * depth * rows_out * sum(widths),
            bytes_accessed=2 * blocks * depth * (rows_out + sum(widths)) + 4 * rows_out * sum(widths),
            transcendentals=0,
        ),
        name="weight_grad",
    )(part.reshape(1).astype(jnp.int32), *lefts, *[v for r in rights for v in r], *arrived)


def body(
    prompt_x,
    cont_x,
    cont_ids,
    routes,
    qkv_weight,
    out_weight,
    router_weight,
    norm_gains,
    gate_up_weight,
    down_weight,
    prompt_cot,
    cont_cot,
):
    n_dp, n_ctx, n_exp = lax.axis_size("dp"), lax.axis_size("ctx"), lax.axis_size("exp")
    d, c, z = lax.axis_index("dp"), lax.axis_index("ctx"), lax.axis_index("exp")
    prompt_len = prompt_x.shape[1]
    cont_len = cont_x.shape[1]
    rows = prompt_len + cont_len
    prompt_total = prompt_len * n_ctx
    experts = router_weight.shape[1]
    capacity = rows * TOP * 17 // (16 * experts)
    score_scale = HEAD_DIM ** (-0.5)
    shard = qkv_weight.shape[0]
    heads_own = HEADS // n_ctx
    width = heads_own * HEAD_DIM
    head_groups = n_dp if (D // (n_dp * n_ctx)) % HEAD_DIM == 0 else 1
    head_run = D // (head_groups * n_ctx)
    own_expert = c * n_exp + z

    def ctx_swap(x, k):
        return lax.ppermute(x, "ctx", [(i, i ^ k) for i in range(n_ctx)])

    def ctx_trade(x):
        return lax.all_to_all(x, "ctx", 0, 0, tiled=True)

    def ctx_gather(x):
        return ctx_trade(jnp.broadcast_to(x[None], (n_ctx,) + x.shape))

    def exp_shift(x, s):
        return lax.ppermute(x, "exp", [(i, (i + s) % n_exp) for i in range(n_exp)])

    def dp_shift(x, m):
        return lax.ppermute(x, "dp", [(i, (i + m) % n_dp) for i in range(n_dp)])

    def part_of(x, axis, at):
        return lax.dynamic_index_in_dim(x, at, axis, keepdims=False)

    def place(buffer, x, *index):
        start, shape = [], []
        for at, size in zip(index, buffer.shape):
            start.append(0 if at is None else at)
            shape.append(size if at is None else 1)
        shape += buffer.shape[len(index) :]
        start += [0] * (buffer.ndim - len(index))
        return lax.dynamic_update_slice(buffer, x.reshape(shape), start)

    def gate(x, *others):
        out = lax.optimization_barrier((x,) + others)[0]
        return list(out) if isinstance(out, tuple) else out

    mark = jnp.full((8, 128), d, jnp.int32).astype(F32)

    def hand_on(in_ref, out_ref):
        out_ref[...] = in_ref[...]

    def fence(*values):
        nonlocal mark
        mark = pl.pallas_call(
            hand_on,
            out_shape=jax.ShapeDtypeStruct(mark.shape, mark.dtype),
            cost_estimate=pl.CostEstimate(
                flops=2 * 10**11, bytes_accessed=0, transcendentals=0
            ),
            name="fence",
        )(gate(mark, *values))

    def after(*values):
        out = lax.optimization_barrier(values + (mark,))
        return out[0] if len(values) == 1 else out[:-1]

    def by_owner(v):
        runs = v.shape[1] // (n_ctx * head_run)
        return jnp.stack(
            [
                jnp.concatenate(
                    [
                        v[:, (i * n_ctx + j) * head_run : (i * n_ctx + j + 1) * head_run]
                        for i in range(runs)
                    ],
                    axis=1,
                )
                for j in range(n_ctx)
            ]
        )

    def all_owners(v):
        runs = v.shape[2] // head_run
        return jnp.concatenate(
            [
                v[j][:, i * head_run : (i + 1) * head_run]
                for i in range(runs)
                for j in range(n_ctx)
            ],
            axis=1,
        )

    x_own = jnp.concatenate([prompt_x[0], cont_x[0]], axis=0)
    cot_own = jnp.concatenate([prompt_cot[0], cont_cot[0]], axis=0)

    small_width = experts + norm_gains.shape[1]
    route_width = -(-rows * TOP // shard)
    route_cols = routes[0, 0].T.astype(BF16).reshape(-1)
    route_cols = jnp.pad(route_cols, (0, route_width * shard - rows * TOP)).reshape(shard, -1)
    extra = jnp.concatenate(
        [
            router_weight,
            norm_gains,
            jnp.broadcast_to(cont_ids[0].astype(BF16), (shard, cont_len)),
            route_cols,
        ],
        axis=1,
    )
    extra_width = -(-extra.shape[1] // 128) * 128
    extra = jnp.pad(extra, ((0, 0), (0, extra_width - extra.shape[1])))
    all_width = 3 * width + extra_width
    runs = 3 * width // head_run


    def pack(w_ref, extra_ref, out_ref):
        for j in range(n_ctx):
            for i in range(runs):
                out_ref[j, :, i * head_run : (i + 1) * head_run] = w_ref[
                    :, (i * n_ctx + j) * head_run : (i * n_ctx + j + 1) * head_run
                ]
            out_ref[j, :, 3 * width :] = extra_ref[...]

    packed_w = pl.pallas_call(
        pack, out_shape=jax.ShapeDtypeStruct((n_ctx, shard, all_width), BF16), name="pack"
    )(qkv_weight, extra)
    slab = ctx_trade(packed_w)
    out_blocks = [out_weight] + [exp_shift(out_weight, s) for s in range(1, n_exp)]
    fence(packed_w)

    def by_exp(v):
        shaped = v.reshape(v.shape[:-1] + (n_dp, n_ctx, n_exp, shard))
        return jnp.swapaxes(shaped, -3, -2).reshape(v.shape)

    def from_exp(v):
        shaped = v.reshape(v.shape[:-1] + (n_dp, n_exp, n_ctx, shard))
        return jnp.swapaxes(shaped, -3, -2).reshape(v.shape)

    x_turned = by_exp(x_own)
    out_blocks = after(*out_blocks)
    out_exp = jnp.zeros((n_exp, shard, D), BF16)
    for j in range(n_exp):
        out_exp = place(out_exp, out_blocks[j], (z - j) % n_exp)

    slab = after(slab)
    ids_at = 3 * width + small_width
    ids = slab[:, 0, ids_at : ids_at + cont_len].astype(F32).astype(jnp.int32)
    w_blocks = [slab] + [exp_shift(slab, s) for s in range(1, n_exp)]
    w_sets = [[dp_shift(slab, m)] for m in range(1, n_dp)]
    out_ctx = ctx_gather(gate(out_exp, slab))
    fence(slab, out_exp)
    out_ctx = after(out_ctx)
    x_sent = gate(x_turned, out_ctx)
    x_all = ctx_gather(x_sent)
    fence(x_sent)

    x_all = after(x_all).reshape(n_ctx * rows, D).astype(F32)
    scale_in = row_scale(x_all)
    w_blocks = gate(tuple(w_blocks), scale_in)
    for m in range(1, n_dp):
        w_sets[m - 1] += [dp_shift(v, m) for v in w_blocks[1:]]
    cot_blocks = [cot_own]
    routes_at = ids_at + cont_len
    places = jnp.stack(
        [(d - m) % n_dp for m in range(n_dp)] + [(z - s) % n_exp for s in range(n_exp)]
    ).astype(jnp.int32)

    def assemble(at_ref, *refs):
        blocks, (w_ref, small_ref) = refs[: n_dp * n_exp], refs[n_dp * n_exp :]
        for m in range(n_dp):
            for s in range(n_exp):
                block = blocks[m * n_exp + s]
                w_ref[at_ref[m], at_ref[n_dp + s]] = block[:, :, : 3 * width]
                small_ref[at_ref[m], at_ref[n_dp + s]] = block[:, :, 3 * width :]

    in_vmem = pl.BlockSpec(memory_space=pltpu.VMEM)
    w_qkv, w_small = pl.pallas_call(
        assemble,
        in_specs=[pl.BlockSpec(memory_space=pltpu.SMEM)] + [in_vmem] * (n_dp * n_exp),
        out_specs=[in_vmem] * 2,
        out_shape=[
            jax.ShapeDtypeStruct((n_dp, n_exp, n_ctx, shard, 3 * width), BF16),
            jax.ShapeDtypeStruct((n_dp, n_exp, n_ctx, shard, extra_width), BF16),
        ],
        compiler_params=pltpu.CompilerParams(vmem_limit_bytes=56 << 20),
        cost_estimate=pl.CostEstimate(flops=0, bytes_accessed=0, transcendentals=0),
        name="assemble",
    )(places, *w_blocks, *[v for w_set in w_sets for v in w_set])
    w_qkv = w_qkv.reshape(D, 3 * width)
    w_small = jnp.swapaxes(w_small, 1, 2).reshape(D, extra_width)
    w_router = w_small[:, :experts]
    gains_t = w_small[:, experts:small_width].astype(F32).T
    gain_in, gain_ffn = gains_t[0], gains_t[3]

    def own_features(v):
        shaped = v.reshape(v.shape[:-1] + (head_groups, n_ctx, head_run))
        return part_of(shaped, v.ndim, c).reshape(v.shape[:-1] + (width,))

    gain_query, gain_key = own_features(gains_t[1]), own_features(gains_t[2])

    upper = (
        jnp.arange(rows, dtype=jnp.int32)[:, None] < jnp.arange(rows, dtype=jnp.int32)[None, :]
    ).astype(BF16)
    send_experts = (jnp.arange(n_ctx) * n_exp + z).astype(F32)

    def spread_of(route_cols):
        named = jnp.any(
            route_cols.astype(F32)[None] == send_experts[:, None, None], axis=1
        )
        rank = dot(named.astype(BF16), upper)
        slots = jnp.where(named, rank, -1.0)
        return (
            (slots[:, None, :] == jnp.arange(capacity, dtype=F32)[None, :, None])
            .astype(BF16)
            .reshape(n_ctx * capacity, rows)
        )

    spread = [spread_of(routes[0, 0].T)]

    def spread_pair(blocks):
        n = len(blocks)
        parts = []
        for i, s in enumerate(blocks):
            part = spread[s].reshape(n_ctx, 1, capacity, rows)
            parts.append(jnp.pad(part, ((0, 0), (0, 0), (0, 0), (i * rows, (n - 1 - i) * rows))))
        return jnp.concatenate(parts, axis=1).reshape(n_ctx * n * capacity, n * rows)

    def pack_of(spread_rows, blocks):
        n = len(blocks)
        sent = dot(spread_rows, blocks[0] if n == 1 else jnp.concatenate(blocks, axis=0))
        return sent.astype(BF16).reshape(n_ctx, n, capacity, -1)

    def pack_cot(blocks):
        return pack_of(
            spread_pair(blocks) if len(blocks) > 1 else spread[blocks[0]],
            [cot_blocks[s] for s in blocks],
        )

    def trade_pieces(pieces):
        return [ctx_swap(pieces[k], k) if k else pieces[k] for k in range(n_ctx)]

    def in_order(pieces):
        whole = jnp.zeros((n_ctx,) + pieces[0].shape, pieces[0].dtype)
        for k in range(n_ctx):
            whole = place(whole, pieces[k], c ^ k)
        return whole

    w_gate_up = gate_up_weight[0]
    w_down = down_weight[0]
    pairs = [list(range(i, i + 2)) for i in range(0, n_exp, 2)]

    total_rows = rows * n_ctx
    index = jnp.arange(rows, dtype=jnp.int32)
    in_prompt = index < prompt_len
    position, seg_rows, order = [], [], []
    for j in range(n_ctx):
        seg = ids[j]
        starts = jnp.sum((seg[None, :] < seg[:, None]).astype(jnp.int32), axis=1)
        within = jnp.arange(cont_len, dtype=jnp.int32) - starts
        at = j * prompt_len
        position.append(jnp.concatenate([at + index[:prompt_len], prompt_total + within]))
        order.append(jnp.where(in_prompt, at + index, index))
        seg_rows.append(
            jnp.concatenate([jnp.full((prompt_len,), -1, jnp.int32), j * 64 + seg])
        )
    position = jnp.concatenate(position).astype(F32)
    order = jnp.concatenate(order)
    seg_of = jnp.concatenate(seg_rows)
    is_prompt = jnp.concatenate([in_prompt] * n_ctx)
    before = order[None, :] <= order[:, None]
    allowed = jnp.where(
        is_prompt[:, None],
        is_prompt[None, :] & before,
        is_prompt[None, :] | ((seg_of[None, :] == seg_of[:, None]) & before),
    )
    hidden_pairs = jnp.where(allowed, 0.0, -1.0)
    cosine, sine_rows = rope_tables(position, HEAD_DIM // 2)

    cot_sent = gate(pack_cot([0]), scale_in)
    cot_trade = ctx_trade(cot_sent)
    fence(cot_sent, w_qkv)
    hidden_in = after((x_all * after(scale_in) * by_exp(gain_in)).astype(BF16))
    projected = dot(hidden_in, w_qkv)

    def ctx_sum(total):
        k = 1
        while k < n_ctx:
            total = total + ctx_swap(total, k)
            k *= 2
        return total

    raw_query, raw_key = projected[:, :width], projected[:, width : 2 * width]
    squares = jnp.stack([jnp.sum(raw_query * raw_query, axis=-1), jnp.sum(raw_key * raw_key, axis=-1)])
    cot_flight = [exp_shift(gate(cot_blocks[0], squares), s) for s in range(1, n_exp)]
    scales = lax.rsqrt(ctx_sum(squares) / D + NORM_EPS)
    spread += [
        spread_of(
            part_of(v[..., routes_at : routes_at + route_width], 0, c)
            .reshape(-1)[: rows * TOP]
            .reshape(TOP, rows)
        )
        for v in gate(tuple(w_blocks[1:]), squares)
    ]
    out_ctx = gate(out_ctx, scales)
    out_halves = [out_ctx] + [dp_shift(out_ctx, m) for m in range(1, n_dp)]
    fence(scales, out_ctx)
    scales = after(scales)
    scales = scales.T
    head_gains = jnp.stack([gain_query, gain_key])
    mixed_heads, *kept = attend(projected, scales, head_gains, cosine, sine_rows, hidden_pairs)

    mixed_heads = gate(mixed_heads, cot_trade)
    mixed = ctx_trade(mixed_heads.reshape(n_ctx, rows, width))
    cot_own_rows = cot_trade
    spreads = [spread_pair(pair) for pair in pairs]
    fence(mixed_heads, *spreads)
    mixed = after(mixed)
    cot_blocks += gate(tuple(cot_flight), mixed)
    mixed = all_owners(mixed)
    cot_sent = gate(pack_cot(list(range(1, n_exp))), mixed)
    cot_trade = ctx_trade(cot_sent)
    fence(mixed, cot_sent)
    mixed = after(mixed)
    half = D // n_dp
    mixed_halves = jnp.stack([mixed[:, i * half : (i + 1) * half] for i in range(n_dp)])
    inputs = x_own.astype(F32)
    mid_rows = inputs
    for m in range(n_dp):
        mid_rows = mid_rows + dot(
            part_of(mixed_halves, 0, (d - m) % n_dp), out_halves[m].reshape(half, D)
        )
    scale_ffn = row_scale(mid_rows)
    normed_ffn = mid_rows * scale_ffn
    hidden_ffn = (normed_ffn * gain_ffn).astype(BF16)

    def softmax(logits):
        shifted = jnp.exp(logits - jnp.max(logits, axis=-1, keepdims=True))
        return shifted / jnp.sum(shifted, axis=-1, keepdims=True)

    cot_rows, made = [], []

    def towards(blocks, back, spread_rows):
        return dot_at(spread_rows, back.reshape(spread_rows.shape[0], -1))

    def home(s, summed):
        return exp_shift(summed, n_exp - s)

    near = exp_shift(hidden_ffn, 1)
    fence(hidden_ffn)

    near = after(near)
    far = [exp_shift(gate(hidden_ffn, near), s) for s in range(2, n_exp)]
    cot_trade = after(cot_trade)
    sent = gate(pack_of(spreads[0], [hidden_ffn, near]), cot_trade)
    plane = ctx_trade(sent)
    fence(near, sent)

    cot_back = [cot_own_rows[:, 0]] + [after(cot_trade)[:, s] for s in range(n_exp - 1)]
    for pair in pairs:
        cot_rows.append(jnp.stack([cot_back[s] for s in pair], axis=1).reshape(-1, D))
    plane = after(plane)
    far = gate(tuple(after(*far)), plane)
    sent = pack_of(spreads[1], far)
    plane_next = ctx_trade(sent)
    fence(sent, plane)

    expert_at = own_expert.reshape(1).astype(jnp.int32)

    def compute(i, in_rows):
        in_rows = in_rows.reshape(-1, D)
        out = expert_rows(
            in_rows, cot_rows[i], w_gate_up, w_down, w_router, expert_at, n_ctx, 2
        )
        made.append([in_rows] + list(out))

    compute(0, plane)
    sent = gate(made[0][2], plane_next)
    back = ctx_trade(sent)
    fence(sent)

    compute(1, after(plane_next))
    back = gate(after(back), made[1][1])
    leaving = towards([1], back, spread[1]).astype(BF16)
    homes = [home(1, leaving)]
    sent = gate(made[1][1], back)
    back = ctx_trade(sent)
    fence(sent, leaving)

    mix_sent, route_grads = [], []

    def weigh(i):
        acts, gates = after(made[i][3], made[i][6])
        mix, route = expert_outs(acts, gates, cot_rows[i], w_down)
        mix_sent.append(mix.reshape(n_ctx, 2, capacity, D))
        route_grads.append(route)

    def grads_sent(lefts, rights, rows_out):
        sent = [weight_grad(lefts, rights, half_rows[m], rows_out) for m in range(1, n_dp)]
        return sent, [dp_shift(v, m + 1) for m, v in enumerate(sent)]

    half_rows = [(d + m) % n_dp for m in range(n_dp)]
    weigh(0)
    back = gate(after(back), mix_sent[0])
    leaving = towards([2], back, spread[2]).astype(BF16)
    homes.append(home(2, leaving))
    sent = gate(made[1][2], back)
    back = ctx_trade(sent)
    fence(sent, leaving)

    weigh(1)
    back = gate(after(back), mix_sent[1])
    leaving = towards([3], back, spread[3]).astype(BF16)
    homes.append(home(3, leaving))
    sent = gate(made[0][1], back)
    back = ctx_trade(sent)
    fence(sent, leaving)

    back = after(back)
    returned = towards([0], back, spread[0])
    fence(returned)
    homes = after(*homes)
    for v in after(*homes):
        returned = returned + v.astype(F32)

    router = softmax(dot(hidden_ffn, w_router))
    prob_grad = returned[:, D : D + experts] + returned[:, D + experts : D + 2 * experts]
    logit_grad = router * (prob_grad - jnp.sum(router * prob_grad, axis=-1, keepdims=True))
    ffn_grad = returned[:, :D] + jnp.dot(logit_grad, w_router.astype(F32).T, precision=HIGHEST_PREC)
    router_grad_t = jnp.einsum(
        "re,rd->ed", logit_grad, hidden_ffn.astype(F32), precision=HIGHEST_PREC
    )
    mid_norm_grad, ffn_gain_grad = norm_back(ffn_grad, normed_ffn, scale_ffn, gain_ffn)
    mid_grad = cot_own.astype(F32) + mid_norm_grad

    attn_grad = mid_grad.astype(BF16)
    grad_halves = jnp.zeros((n_dp, rows, half), BF16)
    for m in range(n_dp):
        grad_halves = place(
            grad_halves,
            dot_bt(attn_grad, out_halves[m].reshape(half, D)).astype(BF16),
            (d - m) % n_dp,
        )
    pieces = by_owner(jnp.concatenate([grad_halves[i] for i in range(n_dp)], axis=1))
    mixed_grad = in_order(trade_pieces([part_of(pieces, 0, c ^ k) for k in range(n_ctx)]))
    sent = gate(mix_sent[1], mixed_grad)
    mix_trade = ctx_trade(sent)
    fence(mixed_grad, sent)
    mixed_grad = after(mixed_grad)
    query_turn, key_turn, value_grad, head_gain_grads, sums = attend_back(
        mixed_grad.reshape(total_rows, width),
        kept,
        projected,
        scales,
        head_gains,
        cosine,
        sine_rows,
        hidden_pairs,
    )
    sums = jnp.stack([sums[:, 0], sums[:, HEAD_DIM]])
    means = ctx_sum(sums) / D
    back = gate(mix_trade, means)
    leaving = towards(pairs[1], back, spreads[1]).astype(BF16)
    mix_homes = [home(2, leaving[:rows]), home(3, leaving[rows:])]
    attn_sent = gate(attn_grad, back)
    attn_grad_all = ctx_gather(attn_sent)
    fence(means, attn_sent, leaving)
    means = after(means)
    proj_grad = norms_back(
        query_turn, key_turn, value_grad, projected, scales, means.T, head_gains
    )

    sent = [
        weight_grad([hidden_in], [[proj_grad]], half_rows[m], half) for m in range(1, n_dp)
    ]
    arrived = [dp_shift(v, m + 1) for m, v in enumerate(sent)]
    fence(*sent)
    hidden_part = dot_bt(gate(proj_grad, *sent), w_qkv).astype(BF16)
    arrived = gate(tuple([after(v) for v in arrived]), hidden_part)
    qkv_dp = weight_grad([hidden_in], [[proj_grad]], half_rows[0], half, arrived)
    qkv_dp = qkv_dp.reshape(n_exp, n_ctx * shard, 3 * width)
    sent = [part_of(qkv_dp, 0, (z - 1) % n_exp).astype(BF16)]

    def ring_step(s, sent):
        arrived = exp_shift(sent, 1)
        return arrived, part_of(qkv_dp, 0, (z - s) % n_exp)

    ring_arrived, ring_part = ring_step(2, sent[0])
    attn_grad_all = gate(attn_grad_all, *sent)
    mix_trade = ctx_trade(gate(mix_sent[0], attn_grad_all))
    attn_grad_all = attn_grad_all.reshape(total_rows, D)
    fence(attn_grad_all, *sent)

    mix_homes = after(*mix_homes)
    in_rows, acts, gate_grads, up_grads = [after(*[v[i] for v in made]) for i in (0, 3, 4, 5)]
    acts = gate(tuple(acts), *mix_homes)
    gate_up_grads = [[gate_grads[i], up_grads[i]] for i in range(len(pairs))]
    out_rows = width // n_dp
    if head_groups == n_dp:
        out_left = [gate(after(mixed_heads), *mix_homes)]
        out_sent, out_arrived = grads_sent(out_left, [[attn_grad_all]], out_rows)
        acts = gate(tuple(acts), *out_sent)
    down_sent, down_arrived = grads_sent(acts, [[v] for v in route_grads], FF // n_dp)
    ring_sent = (gate(ring_arrived, *down_sent).astype(F32) + ring_part).astype(BF16)
    ring_arrived, ring_part = ring_step(3, ring_sent)
    in_rows = gate(tuple(in_rows), ring_sent)
    mix_back = gate(after(mix_trade), *down_sent)
    hidden_part = gate(hidden_part, mix_back)
    hidden_trade = ctx_trade(hidden_part.reshape(n_ctx, rows, D))
    if head_groups == n_dp:
        out_left = gate(tuple(out_left), *down_sent)
        out_dp = weight_grad(out_left, [[attn_grad_all]], half_rows[0], out_rows, out_arrived)
        out_dp = out_dp.reshape(n_exp, shard, D)
        in_rows = gate(tuple(in_rows), out_dp)
    gate_up_sent, gate_up_arrived = grads_sent(in_rows, gate_up_grads, D // n_dp)
    ring_sent = (gate(ring_arrived, *gate_up_sent).astype(F32) + ring_part).astype(BF16)
    ring_arrived, ring_part = ring_step(4, ring_sent)
    acts = gate(tuple(acts), ring_sent)
    grad_down = weight_grad(acts, [[v] for v in route_grads], d, FF // n_dp, down_arrived)
    mix_back = gate(mix_back, grad_down)
    leaving = towards(pairs[0], mix_back, spreads[0])
    mix_homes = list(mix_homes) + [leaving[:rows], home(1, leaving[rows:].astype(BF16))]
    in_rows = gate(tuple(in_rows), leaving)
    grad_gate_up = weight_grad(in_rows, gate_up_grads, d, D // n_dp, gate_up_arrived)

    hidden_grad = from_exp(jnp.sum(hidden_trade.astype(F32), axis=0))
    scale_own = lax.dynamic_slice_in_dim(scale_in, c * rows, rows, axis=0)
    in_norm_grad, in_gain_grad = norm_back(hidden_grad, inputs * scale_own, scale_own, gain_in)
    input_grad = mid_grad + in_norm_grad

    def spread_features(v):
        shaped = jnp.zeros((head_groups, n_ctx, head_run), F32)
        return place(shaped, v.reshape(head_groups, 1, head_run), None, c).reshape(1, D)

    small_grad = jnp.concatenate(
        [
            router_grad_t,
            in_gain_grad[None],
            spread_features(head_gain_grads[0]),
            spread_features(head_gain_grads[1]),
            ffn_gain_grad[None],
        ],
        axis=0,
    )
    count = small_grad.shape[0]
    part = small_grad.reshape(count, n_dp, n_ctx, n_exp, shard).transpose(1, 2, 3, 0, 4)
    late_d = mark[0, 0].astype(jnp.int32)
    total = lax.dynamic_index_in_dim(part, late_d, 0, keepdims=False)
    for m in range(1, n_dp):
        total = total + dp_shift(
            lax.dynamic_index_in_dim(part, (late_d + m) % n_dp, 0, keepdims=False), m
        )
    part = total
    if head_groups == n_dp:
        out_sent = gate(out_dp.astype(BF16), hidden_trade)
        out_trade = lax.all_to_all(out_sent, "exp", 0, 0, tiled=True)
        out_trade = gate(out_trade, grad_gate_up)
        whole_part = part
        part = part_of(whole_part, 0, c)
        for k in range(1, n_ctx):
            part = part + ctx_swap(part_of(whole_part, 0, c ^ k), k)
        grad_out = jnp.sum(out_trade.astype(F32), axis=0)
    else:
        part = jnp.sum(ctx_trade(part), axis=0)
        grad_out = lax.psum_scatter(
            dot_at(mixed, attn_grad), ("dp", "ctx", "exp"), scatter_dimension=0, tiled=True
        )
    total = lax.dynamic_index_in_dim(part, z, 0, keepdims=False)
    for s in range(1, n_exp):
        piece = lax.dynamic_index_in_dim(part, (z + s) % n_exp, 0, keepdims=False)
        total = total + exp_shift(piece, s)
    small_sum = total.T
    mix_homes = gate(tuple(mix_homes), grad_out)
    mixture = mix_homes[2] + sum(v.astype(F32) for v in mix_homes[:2] + mix_homes[3:])
    final_rows = (mid_rows + mixture).astype(BF16)

    qkv_exp = gate(ring_arrived, final_rows, part).astype(F32) + ring_part
    qkv_exp = qkv_exp.reshape(n_ctx, shard, 3 * width)
    grad_qkv = all_owners(ctx_trade(qkv_exp.astype(BF16)).astype(F32))

    return (
        final_rows[:prompt_len][None],
        final_rows[prompt_len:][None],
        input_grad[:prompt_len][None],
        input_grad[prompt_len:][None],
        grad_qkv,
        grad_out,
        small_sum[:, :experts],
        small_sum[:, experts:],
        grad_gate_up[None],
        grad_down[None],
    )


def solution(mesh):
    return jax.shard_map(
        body,
        mesh=mesh,
        in_specs=(
            P(("dp", "exp"), "ctx", None),
            P(("dp", "exp"), "ctx", None),
            P(("dp", "exp"), "ctx", None),
            P(("dp", "exp"), "ctx", None, None),
            P(("dp", "ctx", "exp"), None),
            P(("dp", "ctx", "exp"), None),
            P(("dp", "ctx", "exp"), None),
            P(("dp", "ctx", "exp"), None),
            P(("ctx", "exp"), None, None),
            P(("ctx", "exp"), None, None),
            P(("dp", "exp"), "ctx", None),
            P(("dp", "exp"), "ctx", None),
        ),
        out_specs=(
            P(("dp", "exp"), "ctx", None),
            P(("dp", "exp"), "ctx", None),
            P(("dp", "exp"), "ctx", None),
            P(("dp", "exp"), "ctx", None),
            P(("dp", "ctx", "exp"), None),
            P(("dp", "ctx", "exp"), None),
            P(("dp", "ctx", "exp"), None),
            P(("dp", "ctx", "exp"), None),
            P(("ctx", "exp"), "dp", None),
            P(("ctx", "exp"), "dp", None),
        ),
        check_vma=False,
    )
```
